128 devices in a mesh: rep: 16 (over y_hi, x, core), shard: 8 (over y_lo, z).
Axes of the slice: x: 4, y: 4 (y_hi: 2, y_lo: 2; y = y_hi * 2 + y_lo), z: 4, core: 2. Of those that a mesh axis runs over, the one named last changes fastest.
Arguments:
- tokens: bfloat16 [16384, 1600], P(('rep', 'shard')), may hold values from -6 to 6
- lengths: int32 [16, 4], P('rep'), may hold values from 1 to 1021, as said below
- ln1_gain: bfloat16 [1600], P('shard'), may hold values from 0.25 to 1.75
- ln1_bias: bfloat16 [1600], P('shard'), may hold values from -3 to 3
- qkv_weight: bfloat16 [1600, 4800], P('shard'), may hold values from -0.15625 to 0.15625
- q_bias: bfloat16 [1600], P('shard'), may hold values from -3 to 3
- v_bias: bfloat16 [1600], P('shard'), may hold values from -3 to 3
- out_weight: bfloat16 [1600, 1600], P('shard'), may hold values from -0.625 to 0.625
- out_bias: bfloat16 [1600], P('shard'), may hold values from -2 to 2
- ln2_gain: bfloat16 [1600], P('shard'), may hold values from 0.25 to 1.75
- ln2_bias: bfloat16 [1600], P('shard'), may hold values from -3 to 3
- fc_weight: bfloat16 [1600, 6400], P('shard'), may hold values from -0.15625 to 0.15625
- fc_bias: bfloat16 [6400], P('shard'), may hold values from -3 to 3
- proj_weight: bfloat16 [6400, 1600], P('shard'), may hold values from -0.078125 to 0.078125
- proj_bias: bfloat16 [1600], P('shard'), may hold values from -2 to 2
- cotangent: bfloat16 [16384, 1600], P(('rep', 'shard')), may hold values from -6 to 6
Outputs:
- output: bfloat16 [16384, 1600], P(('rep', 'shard'))
- input_grad: float32 [16384, 1600], P(('rep', 'shard'))
- grad_ln1_gain: float32 [1600], P('shard')
- grad_ln1_bias: float32 [1600], P('shard')
- grad_qkv_weight: float32 [1600, 4800], P('shard')
- grad_q_bias: float32 [1600], P('shard')
- grad_v_bias: float32 [1600], P('shard')
- grad_out_weight: float32 [1600, 1600], P('shard')
- grad_out_bias: float32 [1600], P('shard')
- grad_ln2_gain: float32 [1600], P('shard')
- grad_ln2_bias: float32 [1600], P('shard')
- grad_fc_weight: float32 [1600, 6400], P('shard')
- grad_fc_bias: float32 [6400], P('shard')
- grad_proj_weight: float32 [6400, 1600], P('shard')
- grad_proj_bias: float32 [1600], P('shard')
The draws below stay inside these ranges and needn't reach their ends.
Inputs may be any that keep to these rules, and one draw needn't show every extreme that they name: Each row's 4 lengths are positive and sum to 1024.
All inputs are finite; a program needn't handle non-finite values.
Results may differ from the reference program's by a relative error of at most 0.024.
Values may be sent and summed in bfloat16 or wider, within the bound.
No kernel may reach another device: no remote copies, remote signals or barrier semaphores. Data moves between devices by JAX's collectives and lax.ppermute only.
A program may use at most 256 MiB of HBM per device.

```python
import jax
import jax.numpy as jnp
from jax import lax

D = 1600
HEADS = 25
HEAD_DIM = 64
FF = 6400
SEQS = 4
GROUPS = 16
GROUP_TOK = 1024
TOK_LOCAL = 128
TOKENS = 16384
QBLOCK = 512


def draw_lengths(key, part):
    key = jax.random.fold_in(key, 7)
    short_key, place_key = jax.random.split(key)
    shorts = jax.random.randint(short_key, (GROUPS, SEQS - 1), 1, TOK_LOCAL // (SEQS - 1) + 1, dtype=jnp.int32)
    before = jax.random.randint(place_key, (GROUPS, 1), 0, SEQS, dtype=jnp.int32)
    longest = GROUP_TOK - jnp.sum(shorts, axis=1, keepdims=True)
    positions = jnp.arange(SEQS, dtype=jnp.int32)[None, :]
    early_part = jnp.concatenate([shorts, jnp.zeros((GROUPS, 1), jnp.int32)], axis=1)
    late_part = jnp.concatenate([jnp.zeros((GROUPS, 1), jnp.int32), shorts], axis=1)
    return jnp.where(positions < before, early_part, jnp.where(positions == before, longest, late_part)).astype(jnp.int32)


def levels(stream_key, shape, pieces, low, high):
    factor_of = 1.0
    for axis_at, shards_of in pieces:
        heights = jax.random.uniform(jax.random.fold_in(jax.random.fold_in(stream_key, 6), axis_at), (shards_of,), jnp.float32, low / len(pieces), high / len(pieces))
        factor_of = factor_of * jnp.repeat(jnp.exp(heights), shape[axis_at] // shards_of).reshape((-1,) + (1,) * (len(shape) - 1 - axis_at))
    return factor_of


def normal_values(own_key, extent, scale, reach, shards=(), held_as=jnp.bfloat16):
    factor_of = levels(own_key, extent, shards, -0.22, 0.18) if shards else 1.0
    drawn = jax.random.normal(own_key, extent, jnp.float32) * scale * factor_of
    return jnp.minimum(jnp.maximum(drawn, -reach), reach).astype(held_as)


def setup_inputs(seed: int = 0) -> dict:
    key_list = jax.random.split(jax.random.key(seed), 17)
    return {
        "tokens": normal_values(key_list[0], (TOKENS, D), 1.0, 6.0, ((0, 128),)),
        "lengths": draw_lengths(jax.random.fold_in(key_list[16], 71), 0),
        "ln1_gain": jnp.clip(1.0 + 0.15 * jax.random.normal(key_list[2], (D,), jnp.float32), 0.25, 1.75).astype(jnp.bfloat16),
        "ln1_bias": normal_values(key_list[3], (D,), 0.5, 3.0, ((0, 8),)),
        "qkv_weight": normal_values(key_list[4], (D, 3 * D), D ** -0.5, 0.15625, ((0, 8),)),
        "q_bias": normal_values(key_list[5], (D,), 0.5, 3.0, ((0, 8),)),
        "v_bias": normal_values(key_list[6], (D,), 0.5, 3.0, ((0, 8),)),
        "out_weight": normal_values(key_list[7], (D, D), (D // 16) ** -0.5, 0.625, ((0, 8),)),
        "out_bias": normal_values(key_list[8], (D,), 0.3, 2.0, ((0, 8),)),
        "ln2_gain": jnp.clip(1.0 + 0.15 * jax.random.normal(key_list[9], (D,), jnp.float32), 0.25, 1.75).astype(jnp.bfloat16),
        "ln2_bias": normal_values(key_list[10], (D,), 0.5, 3.0, ((0, 8),)),
        "fc_weight": normal_values(key_list[11], (D, FF), D ** -0.5, 0.15625, ((0, 8),)),
        "fc_bias": normal_values(key_list[12], (FF,), 0.5, 3.0, ((0, 8),)),
        "proj_weight": normal_values(key_list[13], (FF, D), FF ** -0.5, 0.078125, ((0, 8),)),
        "proj_bias": normal_values(key_list[14], (D,), 0.3, 2.0, ((0, 8),)),
        "cotangent": normal_values(key_list[15], (TOKENS, D), 1.0, 6.0, ((0, 128),)),
    }


PRECISE = lax.Precision.HIGHEST
EPSILON = 1e-05

@jax.custom_vjp
def low(v):
    return lax.optimization_barrier(v.astype(jnp.bfloat16)).astype(jnp.float32)

@jax.custom_vjp
def low_back(v):
    return v

def low_keep(v):
    return (low(v), None)

def low_pass(kept, grad):
    return (grad,)

def back_keep(v):
    return (v, None)

def back_low(kept, grad):
    return (low(grad),)
low.defvjp(low_keep, low_pass)
low_back.defvjp(back_keep, back_low)

def norm_rows(inputs, scales, offset):
    average = lax.optimization_barrier(jnp.mean(inputs, axis=-1, keepdims=True))
    centred = inputs - average
    spread = lax.optimization_barrier(jnp.mean(centred * centred, axis=-1, keepdims=True))
    return centred * lax.rsqrt(spread + EPSILON) * scales + offset

def segment_numbers(length_row, count):
    boundaries = jnp.cumsum(length_row)
    positions = jnp.arange(count, dtype=jnp.int32)
    return lax.optimization_barrier(jnp.sum((positions[:, None] >= boundaries[None, :]).astype(jnp.int32), axis=1))

def group_forward(params, source, length_row):
    gain_one, bias_one, weight_qkv, bias_query, bias_value, weight_out, bias_out, gain_two, bias_two, weight_fc, bias_fc, weight_proj, bias_proj = params
    group_rows = source.shape[0]
    segment = segment_numbers(length_row, group_rows)
    positions = jnp.arange(group_rows, dtype=jnp.int32)
    normed_first = low(norm_rows(source, gain_one, bias_one))
    qkv_bias = jnp.concatenate([bias_query, jnp.zeros_like(bias_query), bias_value])
    qkv = jnp.dot(normed_first, weight_qkv, precision=PRECISE) + qkv_bias
    qkv = low(low_back(qkv))
    query_heads = qkv[:, :D].reshape(group_rows, HEADS, HEAD_DIM)
    key_heads = qkv[:, D:2 * D].reshape(group_rows, HEADS, HEAD_DIM)
    value_heads = qkv[:, 2 * D:].reshape(group_rows, HEADS, HEAD_DIM)
    attn_scale = HEAD_DIM ** (-0.5)

    def attend(start):
        query_part = lax.dynamic_slice_in_dim(query_heads, start, QBLOCK, 0)
        query_seg = lax.dynamic_slice_in_dim(segment, start, QBLOCK, 0)
        query_pos = start + jnp.arange(QBLOCK, dtype=jnp.int32)
        allowed = (query_seg[:, None] == segment[None, :]) & (positions[None, :] <= query_pos[:, None])
        scores = low_back(attn_scale * jnp.einsum('qhd,khd->hqk', query_part, key_heads, precision=PRECISE))
        scores = jnp.where(allowed[None], scores, -1e+30)
        top = lax.optimization_barrier(jnp.max(scores, axis=-1, keepdims=True))
        powers = jnp.exp(scores - top)
        probs = powers / lax.optimization_barrier(jnp.sum(powers, axis=-1, keepdims=True))
        return jnp.einsum('hqk,khd->qhd', low(probs), value_heads, precision=PRECISE)
    starts = (jnp.arange(group_rows // QBLOCK, dtype=jnp.int32) * QBLOCK).astype(jnp.int32)
    attended = lax.map(jax.checkpoint(attend), starts).reshape(group_rows, D)
    mixed = low(low_back(attended))
    branch = low_back(jnp.dot(mixed, weight_out, precision=PRECISE) + bias_out)
    middle = source + branch
    normed_second = low(norm_rows(middle, gain_two, bias_two))
    hidden_in = low_back(jnp.dot(normed_second, weight_fc, precision=PRECISE) + bias_fc)
    hidden = low(jax.nn.gelu(hidden_in, approximate=True))
    final = low_back(jnp.dot(hidden, weight_proj, precision=PRECISE) + bias_proj)
    return middle + final

def reference(tokens, lengths, ln1_gain, ln1_bias, qkv_weight, q_bias, v_bias, out_weight, out_bias, ln2_gain, ln2_bias, fc_weight, fc_bias, proj_weight, proj_bias, cotangent):
    params = tuple((item.astype(jnp.float32) for item in (ln1_gain, ln1_bias, qkv_weight, q_bias, v_bias, out_weight, out_bias, ln2_gain, ln2_bias, fc_weight, fc_bias, proj_weight, proj_bias)))
    source = tokens.astype(jnp.float32).reshape(GROUPS, GROUP_TOK, D)

    def whole(source_all, params_all):
        return lax.map(lambda items: group_forward(params_all, items[0], items[1]), (source_all, lengths))
    result, pullback = jax.vjp(whole, source, params)
    grad_source, grad_params = pullback(cotangent.astype(jnp.float32).reshape(GROUPS, GROUP_TOK, D))
    return (result.reshape(TOKENS, D).astype(jnp.bfloat16), grad_source.reshape(TOKENS, D), grad_params[0], grad_params[1], grad_params[2], grad_params[3], grad_params[4], grad_params[5], grad_params[6], grad_params[7], grad_params[8], grad_params[9], grad_params[10], grad_params[11], grad_params[12])
```

```python
import jax
import jax.numpy as jnp
from jax import lax
from jax.experimental import pallas as pl
from jax.experimental.pallas import tpu as pltpu
from jax.sharding import Mesh
from jax.sharding import PartitionSpec as P

HEADS = 25
HEAD_DIM = 64
EPSILON = 1e-05
LOW = jnp.bfloat16
WIDE = jnp.float32

TEAM_HEADS = 4
SPAN = TEAM_HEADS * HEAD_DIM


def z_swap(value, step):
    return lax.ppermute(value, "z", [(i, i ^ step) for i in range(4)])


def x_swap(value, step):
    return lax.ppermute(value, "x", [(i, i ^ step) for i in range(4)])


def y_swap(value, step):
    return lax.ppermute(value, ("yh", "yl"), [(i, i ^ step) for i in range(4)])


def c_swap(value):
    return lax.ppermute(value, "c", [(0, 1), (1, 0)])


def turn(value):
    return lax.ppermute(value, ("c", "yl"), [(0, 0), (1, 2), (2, 1), (3, 3)])


def y_swap_some(value, step, sender_diagonal):
    pairs = []
    for yh in range(2):
        for c in range(2):
            for yl in range(2):
                if (c == yl) == sender_diagonal:
                    y = (yh * 2 + yl) ^ step
                    pairs.append((yh * 4 + c * 2 + yl, (y // 2) * 4 + c * 2 + y % 2))
    return lax.ppermute(value, ("yh", "c", "yl"), pairs)


def x_swap_diagonal(value, step):
    pairs = []
    for x in range(4):
        for c in range(2):
            pairs.append((x * 4 + c * 3, (x ^ step) * 4 + c * 3))
    return lax.ppermute(value, ("x", "c", "yl"), pairs)


def pick(blocks, index):
    return lax.dynamic_index_in_dim(blocks, index, 0, keepdims=False)


def unmix(blocks, me):
    return jnp.stack([pick(blocks, me ^ k) for k in range(blocks.shape[0])])


def gather_rows(block):
    near = jnp.stack([block] + [z_swap(block, d) for d in (1, 2, 3)])
    far = c_swap(near)
    return jnp.concatenate([near, far]).reshape(-1, block.shape[-1])


def scatter_rows(part):
    rows = part.shape[0] // 8
    part = part.reshape(2, 4, rows, part.shape[-1])
    pair = part[0].astype(WIDE) + c_swap(part[1].astype(LOW)).astype(WIDE)
    pair_low = pair.astype(LOW)
    total = pair[0]
    for d in (1, 2, 3):
        total = total + z_swap(pair_low[d], d).astype(WIDE)
    return total


def gather_weight(blocks, c, yl, z):
    near = jnp.stack(
        [pick(blocks, c * 4 + z)] + [z_swap(pick(blocks, c * 4 + (z ^ d)), d) for d in (1, 2, 3)]
    )
    far = jnp.concatenate([y_swap(near[:2], 1), y_swap(near[2:], 3)])
    return unmix(jnp.concatenate([near, far]), yl * 4 + z)


def reduce_columns(pieces, c, x, yl, z):
    total = pick(pieces, x).astype(WIDE)
    for d in (1, 2, 3):
        total = total + x_swap(pick(pieces, x ^ d), d).astype(WIDE)
    total = total.astype(LOW)
    keep, give = pick(total, yl), pick(total, 1 - yl)
    total = keep.astype(WIDE)
    total = total + y_swap(give, 1).astype(WIDE) + y_swap(give, 3).astype(WIDE)
    total = (total + y_swap(keep, 2).astype(WIDE)).astype(LOW)
    cols = jnp.stack([pick(total, z)] + [z_swap(pick(total, z ^ d), d) for d in (1, 2, 3)])
    cols = unmix(cols, z)
    rows = jnp.stack([cols] + [x_swap(cols, d) for d in (1, 2, 3)])
    rows = unmix(rows, x)
    other = c_swap(rows)
    both = jnp.stack([jnp.where(c == 0, rows, other), jnp.where(c == 0, other, rows)])
    both = both.transpose(1, 3, 0, 2, 4)
    return both.reshape(both.shape[0], both.shape[1], 8, both.shape[-1])


def reduce_rows(pieces, c, x, yl):
    total = pick(pieces, x).astype(WIDE)
    for d in (1, 2, 3):
        total = total + x_swap(pick(pieces, x ^ d), d).astype(WIDE)
    low = total.astype(LOW)
    total = low.astype(WIDE) + y_swap_some(low, 1, False).astype(WIDE)
    total = total + y_swap_some(low, 3, False).astype(WIDE)
    total = (total + y_swap_some(low, 2, True).astype(WIDE)).astype(LOW)
    rows = jnp.stack([total] + [x_swap_diagonal(total, d) for d in (1, 2, 3)])
    rows = jnp.where(c == yl, rows, c_swap(rows))
    return unmix(rows, x)


def attend_kernel(pos_ref, start_ref, key_pos_ref, q_ref, k_ref, v_ref, mixed_ref, logsum_ref):
    q, k, v = q_ref[...], k_ref[...], v_ref[...]
    key_pos = key_pos_ref[...]
    allowed = (key_pos <= pos_ref[...]) & (key_pos >= start_ref[...])
    lane = lax.broadcasted_iota(jnp.int32, q.shape, 1) // HEAD_DIM
    slim = lax.broadcasted_iota(jnp.int32, logsum_ref.shape, 1)
    mixed = jnp.zeros(q.shape, WIDE)
    logsums = jnp.zeros(logsum_ref.shape, WIDE)
    for head in range(TEAM_HEADS):
        own = lane == head
        scores = lax.dot_general(
            jnp.where(own, q, jnp.zeros_like(q)),
            k,
            (((1,), (1,)), ((), ())),
            preferred_element_type=WIDE,
        )
        scores = jnp.where(allowed, scores * (HEAD_DIM**-0.5), -1e30)
        top = jnp.max(scores, axis=-1, keepdims=True)
        powers = jnp.exp(scores - top)
        total = jnp.sum(powers, axis=-1, keepdims=True)
        probs = (powers * (1.0 / total)).astype(LOW)
        mixed = jnp.where(own, jnp.dot(probs, v, preferred_element_type=WIDE), mixed)
        logsums = jnp.where(slim == head, top + jnp.log(total), logsums)
    mixed_ref[...] = mixed.astype(LOW)
    logsum_ref[...] = logsums


def attend_back_kernel(
    pos_ref,
    start_ref,
    key_pos_ref,
    q_ref,
    k_ref,
    v_ref,
    logsum_ref,
    dmix_ref,
    dq_ref,
    dk_ref,
    dv_ref,
    dk_total,
    dv_total,
):
    step = pl.program_id(0)

    @pl.when(step == 0)
    def _():
        dk_total[...] = jnp.zeros_like(dk_total)
        dv_total[...] = jnp.zeros_like(dv_total)

    q, k, v, dmix = q_ref[...], k_ref[...], v_ref[...], dmix_ref[...]
    key_pos = key_pos_ref[...]
    allowed = (key_pos <= pos_ref[...]) & (key_pos >= start_ref[...])
    lane = lax.broadcasted_iota(jnp.int32, q.shape, 1) // HEAD_DIM
    scale = HEAD_DIM**-0.5
    dq = jnp.zeros(q.shape, WIDE)
    for head in range(TEAM_HEADS):
        own = lane == head
        q_own = jnp.where(own, q, jnp.zeros_like(q))
        dmix_own = jnp.where(own, dmix, jnp.zeros_like(dmix))
        across = (((1,), (1,)), ((), ()))
        down = (((0,), (0,)), ((), ()))
        scores = lax.dot_general(q_own, k, across, preferred_element_type=WIDE) * scale
        scores = jnp.where(allowed, scores, -1e30)
        probs = jnp.exp(scores - logsum_ref[:, head : head + 1])
        d_probs = lax.dot_general(dmix_own, v, across, preferred_element_type=WIDE)
        term = jnp.sum(probs * d_probs, axis=-1, keepdims=True)
        d_scores = (probs * (d_probs - term)).astype(LOW)
        dq = jnp.where(own, jnp.dot(d_scores, k, preferred_element_type=WIDE), dq)
        dk_total[...] += lax.dot_general(d_scores, q_own, down, preferred_element_type=WIDE)
        dv_total[...] += lax.dot_general(
            probs.astype(LOW), dmix_own, down, preferred_element_type=WIDE
        )
    dq_ref[...] = (dq * scale).astype(LOW)

    @pl.when(step == pl.num_programs(0) - 1)
    def _():
        dk_ref[...] = (dk_total[...] * scale).astype(LOW)
        dv_ref[...] = dv_total[...].astype(LOW)


Q_ROWS = 256
VMEM_LIMIT = 48 * 1024 * 1024


def attend_specs(rows):
    column = pl.BlockSpec((Q_ROWS, 1), lambda i: (i, 0))
    return [
        column,
        column,
        pl.BlockSpec((1, rows), lambda i: (0, 0)),
        pl.BlockSpec((Q_ROWS, SPAN), lambda i: (i, 0)),
        pl.BlockSpec((rows, SPAN), lambda i: (0, 1)),
        pl.BlockSpec((rows, SPAN), lambda i: (0, 2)),
    ]


def attend(pos, start, qkv):
    rows = qkv.shape[0]
    return pl.pallas_call(
        attend_kernel,
        grid=(rows // Q_ROWS,),
        in_specs=attend_specs(rows),
        out_specs=[
            pl.BlockSpec((Q_ROWS, SPAN), lambda i: (i, 0)),
            pl.BlockSpec((Q_ROWS, 128), lambda i: (i, 0)),
        ],
        out_shape=[
            jax.ShapeDtypeStruct((rows, SPAN), LOW),
            jax.ShapeDtypeStruct((rows, 128), WIDE),
        ],
        compiler_params=pltpu.CompilerParams(vmem_limit_bytes=VMEM_LIMIT),
        cost_estimate=pl.CostEstimate(
            flops=16 * rows * rows * SPAN,
            bytes_accessed=rows * SPAN * 10,
            transcendentals=4 * rows * rows,
        ),
        name="attend",
    )(pos[:, None], start[:, None], pos[None, :], qkv, qkv, qkv)


def attend_back(pos, start, qkv, logsum, dmix):
    rows = qkv.shape[0]
    whole = pl.BlockSpec((rows, SPAN), lambda i: (0, 0))
    part = pl.BlockSpec((Q_ROWS, SPAN), lambda i: (i, 0))
    return pl.pallas_call(
        attend_back_kernel,
        grid=(rows // Q_ROWS,),
        in_specs=attend_specs(rows) + [pl.BlockSpec((Q_ROWS, 128), lambda i: (i, 0)), part],
        out_specs=[part, whole, whole],
        out_shape=[jax.ShapeDtypeStruct((rows, SPAN), LOW)] * 3,
        scratch_shapes=[pltpu.VMEM((rows, SPAN), WIDE)] * 2,
        compiler_params=pltpu.CompilerParams(vmem_limit_bytes=VMEM_LIMIT),
        cost_estimate=pl.CostEstimate(
            flops=40 * rows * rows * SPAN,
            bytes_accessed=rows * SPAN * 14,
            transcendentals=4 * rows * rows,
        ),
        name="attend_back",
    )(pos[:, None], start[:, None], pos[None, :], qkv, qkv, qkv, logsum, dmix)


def norm_parts(inputs):
    average = jnp.mean(inputs, axis=-1, keepdims=True)
    centred = inputs - average
    spread = jnp.mean(centred * centred, axis=-1, keepdims=True)
    inverse = lax.rsqrt(spread + EPSILON)
    return centred * inverse, inverse


def norm_back(d_normed, hat, inverse, gain):
    e = d_normed * gain
    return inverse * (
        e
        - jnp.mean(e, axis=-1, keepdims=True)
        - hat * jnp.mean(e * hat, axis=-1, keepdims=True)
    )


def gelu_tanh(values):
    return jax.nn.gelu(values, approximate=True)


def wide_dot(a, b):
    return jnp.dot(a, b, preferred_element_type=WIDE)


def local(
    tokens,
    lengths,
    ln1_gain,
    ln1_bias,
    qkv_weight,
    q_bias,
    v_bias,
    out_weight,
    out_bias,
    ln2_gain,
    ln2_bias,
    fc_weight,
    fc_bias,
    proj_weight,
    proj_bias,
    cotangent,
):
    rows, width = tokens.shape
    shard = qkv_weight.shape[0]
    hidden_width = fc_weight.shape[1] // 8
    c, x, yl, z = (lax.axis_index(a) for a in ("c", "x", "yl", "z"))
    member = c * 4 + z

    own_tokens = turn(tokens)
    own_cotangent = turn(cotangent)
    all_tokens = gather_rows(own_tokens)
    all_cotangent = gather_rows(own_cotangent)
    other_lengths = c_swap(lengths)
    boundaries = jnp.cumsum(jnp.where(c == yl, lengths, other_lengths)[0])
    slots = jnp.arange(8, dtype=jnp.int32) ^ member
    pos = (slots[:, None] * rows + jnp.arange(rows, dtype=jnp.int32)[None, :]).reshape(-1)
    before = jnp.where(boundaries[None, :] <= pos[:, None], boundaries[None, :], 0)
    start = jnp.max(before, axis=1)

    vectors = jnp.concatenate(
        [ln1_gain, ln1_bias, q_bias, v_bias, out_bias, ln2_gain, ln2_bias, proj_bias, fc_bias]
    )
    vectors = jnp.pad(vectors, (0, 8 * 3 * SPAN - vectors.shape[0])).reshape(8, 3 * SPAN)
    spare = 8 * TEAM_HEADS - HEADS
    qkv_blocks = jnp.pad(
        qkv_weight.reshape(shard, 3, HEADS, HEAD_DIM), ((0, 0), (0, 0), (0, spare), (0, 0))
    )
    qkv_blocks = qkv_blocks.reshape(shard, 3, 8, SPAN).transpose(2, 0, 1, 3)
    qkv_blocks = qkv_blocks.reshape(8, shard, 3 * SPAN)
    qkv_blocks = jnp.concatenate(
        [qkv_blocks, jnp.broadcast_to(vectors[None], (8, 8, 3 * SPAN))], axis=1
    )
    qkv_all = gather_weight(qkv_blocks, c, yl, z)
    weight_qkv = qkv_all[:, :shard].reshape(width, 3 * SPAN)
    small = qkv_all[:, shard:].reshape(8, -1).astype(WIDE)
    (
        gain_one,
        bias_one,
        bias_query,
        bias_value,
        bias_out,
        gain_two,
        bias_two,
        bias_proj,
    ) = [small[:, i * shard : (i + 1) * shard].reshape(-1) for i in range(8)]
    bias_fc = pick(small[:, 8 * shard : 8 * shard + hidden_width], member)

    out_half = width // 2
    out_blocks = out_weight.reshape(shard, 2, out_half).transpose(1, 0, 2)
    out_mine = pick(out_blocks, c)
    out_near = jnp.stack([out_mine] + [z_swap(out_mine, d) for d in (1, 2, 3)])
    out_far = jnp.concatenate([y_swap(out_near[:2], 1), y_swap(out_near[2:], 3)])
    out_mine = unmix(jnp.concatenate([out_near, out_far]), yl * 4 + z).reshape(width, out_half)
    out_other = c_swap(out_mine)
    weight_out = jnp.concatenate(
        [jnp.where(c == 0, out_mine, out_other), jnp.where(c == 0, out_other, out_mine)], axis=1
    )

    fc_blocks = fc_weight.reshape(shard, 8, hidden_width).transpose(1, 0, 2)
    weight_fc = gather_weight(fc_blocks, c, yl, z).reshape(width, hidden_width)

    half = proj_weight.shape[0] // 2
    proj_got = jnp.concatenate(
        [
            y_swap_some(proj_weight[:half], 1, True),
            y_swap_some(proj_weight[half:], 3, True),
        ]
    )
    weight_proj = jnp.where(c == yl, proj_weight, proj_got)

    hat, _ = norm_parts(all_tokens.astype(WIDE))
    normed_first = (hat * gain_one + bias_one).astype(LOW)
    query_pad = jnp.pad(bias_query, (0, 8 * SPAN - width)).reshape(8, SPAN)
    value_pad = jnp.pad(bias_value, (0, 8 * SPAN - width)).reshape(8, SPAN)
    qkv_bias = jnp.concatenate(
        [pick(query_pad, member), jnp.zeros((SPAN,), WIDE), pick(value_pad, member)]
    )
    qkv = (wide_dot(normed_first, weight_qkv) + qkv_bias).astype(LOW)
    mixed_heads, logsum = attend(pos, start, qkv)

    mixed_slots = mixed_heads.reshape(2, 4, rows, SPAN)
    mixed_pair = jnp.stack([mixed_slots[0], c_swap(mixed_slots[1])], axis=1)
    mixed_got = jnp.stack([mixed_pair[0]] + [z_swap(mixed_pair[d], d) for d in (1, 2, 3)])
    mixed_got = unmix(mixed_got, z)
    mixed_got = jnp.where(c == 0, mixed_got, mixed_got[:, ::-1])
    mixed = mixed_got.transpose(2, 1, 0, 3).reshape(rows, 8 * SPAN)[:, :width]
    source = own_tokens.astype(WIDE)
    middle = source + wide_dot(mixed, weight_out) + bias_out
    hat_two, inverse_two = norm_parts(middle)
    normed_second = (hat_two * gain_two + bias_two).astype(LOW)

    all_second = gather_rows(normed_second)
    d_hidden = lax.dot_general(
        all_cotangent, weight_proj, (((1,), (1,)), ((), ())), preferred_element_type=WIDE
    )
    hidden_in = wide_dot(all_second, weight_fc) + bias_fc
    hidden_wide, gelu_back = jax.vjp(gelu_tanh, hidden_in)
    hidden = hidden_wide.astype(LOW)
    d_hidden_in = gelu_back(d_hidden)[0].astype(LOW)
    d_second = scatter_rows(
        lax.dot_general(
            d_hidden_in, weight_fc, (((1,), (1,)), ((), ())), preferred_element_type=WIDE
        )
    )
    final = scatter_rows(wide_dot(hidden, weight_proj))
    output = turn((middle + final + bias_proj).astype(LOW))

    d_middle = own_cotangent.astype(WIDE) + norm_back(d_second, hat_two, inverse_two, gain_two)
    d_branch = d_middle.astype(LOW)
    d_mixed = lax.dot_general(
        d_branch, weight_out, (((1,), (1,)), ((), ())), preferred_element_type=WIDE
    ).astype(LOW)
    d_mixed = jnp.pad(d_mixed, ((0, 0), (0, 8 * SPAN - width)))
    d_mixed = d_mixed.reshape(rows, 2, 4, SPAN).transpose(2, 1, 0, 3)
    d_got = jnp.stack([pick(d_mixed, z)] + [z_swap(pick(d_mixed, z ^ d), d) for d in (1, 2, 3)])
    d_keep = jnp.where(c == 0, d_got[:, 0], d_got[:, 1])
    d_give = jnp.where(c == 0, d_got[:, 1], d_got[:, 0])
    d_mixed_heads = jnp.concatenate([d_keep, c_swap(d_give)]).reshape(8 * rows, SPAN)

    dq, dk, dv = attend_back(pos, start, qkv, logsum, d_mixed_heads)
    d_qkv = jnp.concatenate([dq, dk, dv], axis=1)
    d_first = scatter_rows(
        lax.dot_general(d_qkv, weight_qkv, (((1,), (1,)), ((), ())), preferred_element_type=WIDE)
    )
    hat_one, inverse_one = norm_parts(source)
    d_source = norm_back(d_first, hat_one, inverse_one, gain_one)
    input_grad = turn((d_middle + d_source).astype(LOW)).astype(WIDE)

    down = (((0,), (0,)), ((), ()))
    grad_proj = lax.dot_general(hidden, all_cotangent, down, preferred_element_type=WIDE)
    grad_proj = reduce_rows(grad_proj.astype(LOW).reshape(4, -1, width), c, x, yl)
    grad_proj = grad_proj.reshape(-1, width).astype(WIDE)

    def column_pieces(grad):
        grad = grad.astype(LOW).reshape(2, 4, 4, shard // 4, grad.shape[-1])
        return grad.transpose(2, 0, 1, 3, 4)

    grad_fc = lax.dot_general(all_second, d_hidden_in, down, preferred_element_type=WIDE)
    grad_fc = reduce_columns(column_pieces(grad_fc), c, x, yl, z)
    grad_fc = grad_fc.reshape(shard, 8 * hidden_width).astype(WIDE)

    grad_out = lax.dot_general(mixed, d_branch, down, preferred_element_type=WIDE)
    grad_out = grad_out.astype(LOW).reshape(2, 4, shard, width)
    grad_out = pick(grad_out, c).astype(WIDE) + c_swap(pick(grad_out, 1 - c)).astype(WIDE)
    out_low = grad_out.astype(LOW)
    grad_out = pick(out_low, z).astype(WIDE)
    for d in (1, 2, 3):
        grad_out = grad_out + z_swap(pick(out_low, z ^ d), d).astype(WIDE)
    grad_out = reduce_rows(grad_out.astype(LOW).reshape(4, shard // 4, width), c, x, yl)
    grad_out = grad_out.reshape(shard, width).astype(WIDE)

    grad_qkv = lax.dot_general(normed_first, d_qkv, down, preferred_element_type=WIDE)
    grad_qkv = reduce_columns(column_pieces(grad_qkv), c, x, yl, z)
    grad_qkv = grad_qkv.reshape(shard, 8, 3, SPAN).transpose(0, 2, 1, 3)
    grad_qkv = grad_qkv.reshape(shard, 3, 8 * SPAN)[:, :, :width].reshape(shard, 3 * width)
    grad_qkv = grad_qkv.astype(WIDE)

    def total(value):
        return jnp.sum(value.astype(WIDE), axis=0)

    def spread(value, size):
        return lax.dynamic_update_slice_in_dim(
            jnp.zeros((8 * size,), WIDE), value, member * size, 0
        )

    d_qkv_sum = total(d_qkv)
    sums = jnp.concatenate(
        [
            total(d_first * hat_one),
            total(d_first),
            total(d_branch),
            total(d_second * hat_two),
            total(d_second),
            total(own_cotangent),
            spread(total(d_hidden_in), hidden_width),
            spread(d_qkv_sum[:SPAN], SPAN),
            spread(d_qkv_sum[2 * SPAN :], SPAN),
        ]
    )
    count = sums.shape[0]
    sums = jnp.pad(sums, (0, -count % 1024)).reshape(-1, 128)
    for swap in (z_swap, x_swap, y_swap):
        sums = sums + swap(sums, 1) + swap(sums, 2) + swap(sums, 3)
    sums = (sums + c_swap(sums)).reshape(-1)

    def own_part(at, size):
        return lax.dynamic_slice_in_dim(sums, at + (yl * 4 + z) * size, size, 0)

    vector_grads = [own_part(i * width, shard) for i in range(6)]
    g_gain_one, g_bias_one, g_out_b, g_gain_two, g_bias_two, g_proj_b = vector_grads
    at = 6 * width
    g_fc_b = own_part(at, hidden_width)
    at += 8 * hidden_width
    g_query_b = own_part(at, shard)
    at += 8 * SPAN
    g_value_b = own_part(at, shard)

    return (
        output,
        input_grad,
        g_gain_one,
        g_bias_one,
        grad_qkv,
        g_query_b,
        g_value_b,
        grad_out,
        g_out_b,
        g_gain_two,
        g_bias_two,
        grad_fc,
        g_fc_b,
        grad_proj,
        g_proj_b,
    )


def solution(mesh):
    fine = Mesh(mesh.devices.reshape(2, 4, 2, 2, 4), ("yh", "x", "c", "yl", "z"))
    group, owner = ("yh", "x", "c"), ("yl", "z")
    everyone = group + owner
    vector, matrix = P(owner), P(owner, None)
    rows = P(everyone, None)
    return jax.shard_map(
        local,
        mesh=fine,
        in_specs=(
            rows,
            P(group, None),
            vector,
            vector,
            matrix,
            vector,
            vector,
            matrix,
            vector,
            vector,
            vector,
            matrix,
            vector,
            matrix,
            vector,
            rows,
        ),
        out_specs=(
            rows,
            rows,
            vector,
            vector,
            matrix,
            vector,
            vector,
            matrix,
            vector,
            vector,
            vector,
            matrix,
            vector,
            matrix,
            vector,
        ),
        check_vma=False,
    )
```

```python
import functools

import jax
import jax.numpy as jnp
from jax import lax
from jax.experimental import pallas as pl
from jax.experimental.pallas import tpu as pltpu
from jax.sharding import Mesh
from jax.sharding import PartitionSpec as P

HEADS = 25
HEAD_DIM = 64
EPSILON = 1e-05
LOW = jnp.bfloat16
WIDE = jnp.float32

TEAM_HEADS = 4
SPAN = TEAM_HEADS * HEAD_DIM
SHARD = 200
BLOCK = 256
CARRY = 208
WIDTH = 1600
LANES = 1664
ROWS = 128
FF_PART = 800
PIECE = 56
PIECE_STEP = 48
VMEM_LIMIT = 60 * 1024 * 1024


def after(value, *others):
    if not jax.tree.leaves(others):
        return value
    return lax.optimization_barrier((value, others))[0]


def z_swap(value, step):
    return lax.ppermute(value, "z", [(i, i ^ step) for i in range(4)])


def x_swap(value, step):
    return lax.ppermute(value, "x", [(i, i ^ step) for i in range(4)])


def y_swap(value, step):
    return lax.ppermute(value, ("yh", "yl"), [(i, i ^ step) for i in range(4)])


def c_swap(value):
    return lax.ppermute(value, "c", [(0, 1), (1, 0)])


def team_swap(value, slot):
    return lax.ppermute(value, ("c", "z"), [(i, i ^ slot) for i in range(8)])


def turn(value):
    return lax.ppermute(value, ("c", "yl"), [(0, 0), (1, 2), (2, 1), (3, 3)])


def y_swap_some(value, step, sender_diagonal):
    pairs = []
    for yh in range(2):
        for c in range(2):
            for yl in range(2):
                if (c == yl) == sender_diagonal:
                    y = (yh * 2 + yl) ^ step
                    pairs.append((yh * 4 + c * 2 + yl, (y // 2) * 4 + c * 2 + y % 2))
    return lax.ppermute(value, ("yh", "c", "yl"), pairs)


def x_swap_diagonal(value, step):
    pairs = []
    for x in range(4):
        for c in range(2):
            pairs.append((x * 4 + c * 3, (x ^ step) * 4 + c * 3))
    return lax.ppermute(value, ("x", "c", "yl"), pairs)


def pick(blocks, index):
    return lax.dynamic_index_in_dim(blocks, index, 0, keepdims=False)


DOWN = (((0,), (0,)), ((), ()))


ME, MEMBER, CORE, X, YL, Z = range(6)

def cost(microseconds):
    return pl.CostEstimate(flops=microseconds * 10**9, bytes_accessed=0, transcendentals=0)


SMEM = pl.BlockSpec(memory_space=pltpu.SMEM)
VMEM = pl.BlockSpec(memory_space=pltpu.VMEM)
ANY = pl.BlockSpec(memory_space=pltpu.HBM)


def like(shape, dtype=LOW):
    return jax.ShapeDtypeStruct(shape, dtype)


def whole_call(body, name, outs, *args, scratch=()):
    return pl.pallas_call(
        body,
        in_specs=[SMEM] + [VMEM] * (len(args) - 1),
        out_specs=[VMEM] * len(outs),
        out_shape=list(outs),
        scratch_shapes=list(scratch),
        compiler_params=pltpu.CompilerParams(vmem_limit_bytes=VMEM_LIMIT),
        cost_estimate=cost(0),
        name=name,
    )(*args)


def whole_call_any(body, name, outs, args, others, scratch=()):
    return pl.pallas_call(
        body,
        in_specs=[SMEM] + [VMEM] * (len(args) - 1) + [ANY] * len(others),
        out_specs=[VMEM] * len(outs),
        out_shape=list(outs),
        scratch_shapes=list(scratch),
        compiler_params=pltpu.CompilerParams(vmem_limit_bytes=VMEM_LIMIT),
        cost_estimate=cost(0),
        name=name,
    )(*args, *others)


def block_at(index):
    return pl.ds(pl.multiple_of(index * BLOCK, BLOCK), BLOCK)


def to_blocks(source, mine, write):
    lane = lax.broadcasted_iota(jnp.int32, (source.shape[0], BLOCK), 1)
    for s in range(8):
        block = source[:, SHARD * s : SHARD * s + BLOCK]
        write(s ^ mine, jnp.where(lane < SHARD, block, jnp.zeros_like(block)))


def from_blocks(source, mine, target):
    for s in range(8):
        block = source[:, block_at(s ^ mine)]
        target[:, SHARD * s : SHARD * s + SHARD] = block[:, :SHARD].astype(target.dtype)


def prepare_qkv_kernel(at, weight, *refs):
    held, outs, vectors, sems = refs[:9], refs[9:13], refs[13:22], refs[22]
    copies = load(list(zip(held, vectors)), sems)
    for copy in copies:
        copy.wait()
    lane = lax.broadcasted_iota(jnp.int32, (SHARD, SPAN), 1)
    for d, out in enumerate(outs):
        j = at[CORE] * 4 + (at[Z] ^ d)
        valid = lane < WIDTH - SPAN * j
        none = jnp.zeros((SHARD, SPAN), LOW)
        query = weight[:, pl.ds(pl.multiple_of(SPAN * j, SPAN), SPAN)]
        out[:SHARD, :SPAN] = jnp.where(valid, query, none)
        key = weight[:, pl.ds(pl.multiple_of(WIDTH - 64 + SPAN * j, SPAN), SPAN + 128)]
        out[:SHARD, SPAN : 2 * SPAN] = jnp.where(valid, key[:, 64 : 64 + SPAN], none)

        @pl.when(j < 6)
        def _():
            start = pl.multiple_of(2 * WIDTH + SPAN * j, 128)
            out[:SHARD, 2 * SPAN :] = weight[:, pl.ds(start, SPAN)]

        @pl.when(j >= 6)
        def _():
            out[:SHARD, 2 * SPAN :] = none

        @pl.when(j == 6)
        def _():
            out[:SHARD, 2 * SPAN : 2 * SPAN + 64] = weight[:, 3 * WIDTH - 64 :]

        out[SHARD:, :] = jnp.zeros((CARRY - SHARD, 3 * SPAN), LOW)
        for i, vector in enumerate(vectors[:8]):
            out[SHARD + i : SHARD + i + 1, :SHARD] = vector[...].reshape(1, SHARD)
        for i in range(4):
            part = vectors[8][SHARD * i : SHARD * (i + 1)]
            out[SHARD + i : SHARD + i + 1, BLOCK : BLOCK + SHARD] = part.reshape(1, SHARD)


def prepare_rest_kernel(at, fc, outer, out_half, *outs):
    pad = jnp.zeros((CARRY - SHARD, FF_PART), LOW)
    for half in range(2):

        @pl.when(at[CORE] == half)
        def _():
            out_half[:SHARD, :] = outer[:, FF_PART * half : FF_PART * (half + 1)]

    out_half[SHARD:, :] = pad
    for r in range(4):
        start, shift = FF_PART * r // 128 * 128, FF_PART * r % 128
        start = pl.multiple_of(at[CORE] * (4 * FF_PART) + start, 128)
        part = fc[:, pl.ds(start, 896)][:, shift : shift + FF_PART]
        for d, out in enumerate(outs):

            @pl.when((at[Z] ^ d) == r)
            def _():
                out[:SHARD, :] = part
                out[SHARD:, :] = pad


def normalize(inputs):
    average = jnp.mean(inputs, axis=-1, keepdims=True)
    centred = inputs - average
    spread = jnp.mean(centred * centred, axis=-1, keepdims=True)
    inverse = lax.rsqrt(spread + EPSILON)
    return centred * inverse, inverse


def norm_back(d_normed, hat, inverse, gain):
    e = d_normed * gain
    return inverse * (
        e
        - jnp.mean(e, axis=-1, keepdims=True)
        - hat * jnp.mean(e * hat, axis=-1, keepdims=True)
    )


def load(pairs, sems):
    copies = [pltpu.make_async_copy(f, t, sems.at[i]) for i, (f, t) in enumerate(pairs)]
    for copy in copies:
        copy.start()
    return copies


def weight_pairs(pieces, target):
    pairs, k = [], 0
    for piece in pieces:
        for one in [piece] if len(piece.shape) == 2 else [piece.at[0], piece.at[1]]:
            pairs.append((one, target.at[k, pl.ds(0, CARRY)]))
            k += 1
    return pairs


def clear_pad(target):
    target[:, CARRY:, :] = jnp.zeros((8, BLOCK - CARRY, target.shape[2]), LOW)


def first_kernel(at, *refs):
    token_refs, weight_refs, refs = refs[:8], refs[8:12], refs[12:]
    normed, qkv, vectors, fc_bias, tokens, weight, wide, blocks, spread, *sems = refs
    step = pl.program_id(0)

    def token_copy(k):
        target = tokens.at[k ^ at[MEMBER]]
        return pltpu.make_async_copy(token_refs[k], target, sems[1].at[k])

    @pl.when(step == 0)
    def _():
        for k in range(8):
            token_copy(k).start()
        copies = load(weight_pairs(weight_refs, weight), sems[0])
        clear_pad(weight)
        spread[...] = jnp.zeros_like(spread)
        wide[:, WIDTH:] = jnp.zeros((wide.shape[0], wide.shape[1] - WIDTH), LOW)
        for copy in copies:
            copy.wait()
        for k in range(8):
            block = weight[k ^ at[ME], SHARD:CARRY, :BLOCK].astype(WIDE)
            spread[:, SHARD * k : SHARD * (k + 1)] = block[:, :SHARD]
        vectors[...] = spread[:, :WIDTH]
        rows = weight[(at[CORE] ^ at[YL]) * 4, SHARD:CARRY, BLOCK : 2 * BLOCK].astype(WIDE)
        for i in range(4):
            fc_bias[:, SHARD * i : SHARD * (i + 1)] = rows[i : i + 1, :SHARD]
        for k in range(8):
            token_copy(k).wait()

    rows = tokens[pl.ds(step * 2, 2)].reshape(2 * ROWS, WIDTH)
    hat, _ = normalize(rows.astype(WIDE))
    low = (hat * spread[0:1, :WIDTH] + spread[1:2, :WIDTH]).astype(LOW)
    normed[...] = low
    wide[:, :WIDTH] = low

    def write(k, block):
        blocks[:, block_at(k)] = block

    to_blocks(wide, at[ME], write)
    heads = pl.ds(pl.multiple_of(SPAN * at[MEMBER], SPAN), SPAN)
    total = jnp.dot(
        blocks[...], weight[...].reshape(8 * BLOCK, 3 * SPAN), preferred_element_type=WIDE
    )
    qkv[:, :SPAN] = (total[:, :SPAN] + spread[2:3, heads]).astype(LOW)
    qkv[:, SPAN : 2 * SPAN] = total[:, SPAN : 2 * SPAN].astype(LOW)
    qkv[:, 2 * SPAN :] = (total[:, 2 * SPAN :] + spread[3:4, heads]).astype(LOW)


Q_ROWS = 256


def first(at, tokens, weight):
    rows = 8 * ROWS
    still = lambda i: (0, 0)
    down = lambda i: (i, 0)
    return pl.pallas_call(
        first_kernel,
        grid=(rows // Q_ROWS,),
        in_specs=[SMEM] + [ANY] * 12,
        out_specs=[
            pl.BlockSpec((Q_ROWS, WIDTH), down),
            pl.BlockSpec((Q_ROWS, 3 * SPAN), down),
            pl.BlockSpec((8, WIDTH), still),
            pl.BlockSpec((1, FF_PART), still),
        ],
        out_shape=[
            like((rows, WIDTH)),
            like((rows, 3 * SPAN)),
            like((8, WIDTH), WIDE),
            like((1, FF_PART), WIDE),
        ],
        scratch_shapes=[
            pltpu.VMEM((8, ROWS, WIDTH), LOW),
            pltpu.VMEM((8, BLOCK, 3 * SPAN), LOW),
            pltpu.VMEM((Q_ROWS, WIDTH + 192), LOW),
            pltpu.VMEM((Q_ROWS, 8 * BLOCK), LOW),
            pltpu.VMEM((8, 8 * BLOCK), WIDE),
            pltpu.SemaphoreType.DMA((8,)),
            pltpu.SemaphoreType.DMA((8,)),
        ],
        compiler_params=pltpu.CompilerParams(vmem_limit_bytes=VMEM_LIMIT),
        cost_estimate=cost(0),
        name="first_norm_qkv",
    )(at, *tokens, *weight)


def visible(lengths, first_row, rows, keys):
    row = first_row + lax.broadcasted_iota(jnp.int32, (rows, 1), 0)
    key = lax.broadcasted_iota(jnp.int32, (1, keys), 1)
    start = jnp.zeros_like(row)
    bound = 0
    for i in range(3):
        bound = bound + lengths[0, i]
        start = jnp.where(row >= bound, bound, start)
    return (key <= row) & (key >= start)


ACROSS = (((1,), (1,)), ((), ()))


def by_block(body):
    for i in range(8 * ROWS // Q_ROWS):
        pl.when(pl.program_id(0) == i)(lambda i=i: body(i))


def slot_rows(at, chunk):
    return pl.ds(pl.multiple_of((chunk ^ at[MEMBER]) * ROWS, ROWS), ROWS)


def attend_kernel(at, lengths, q_ref, k_ref, v_ref, mixed_ref, logsum_ref):
    def block(i):
        keys = Q_ROWS * (i + 1)
        q, k, v = q_ref[...], k_ref[:keys, :], v_ref[:keys, :]
        allowed = visible(lengths, i * Q_ROWS, Q_ROWS, keys)
        lane = lax.broadcasted_iota(jnp.int32, q.shape, 1) // HEAD_DIM
        slim = lax.broadcasted_iota(jnp.int32, logsum_ref.shape, 1)
        mixed = jnp.zeros(q.shape, WIDE)
        logsums = jnp.zeros(logsum_ref.shape, WIDE)
        for head in range(TEAM_HEADS):
            own = lane == head
            q_own = jnp.where(own, q, jnp.zeros_like(q))
            scores = lax.dot_general(q_own, k, ACROSS, preferred_element_type=WIDE)
            scores = jnp.where(allowed, scores * (HEAD_DIM**-0.5), -1e30)
            top = jnp.max(scores, axis=-1, keepdims=True)
            powers = jnp.exp(scores - top)
            total = jnp.sum(powers, axis=-1, keepdims=True)
            probs = (powers * (1.0 / total)).astype(LOW)
            mixed = jnp.where(own, jnp.dot(probs, v, preferred_element_type=WIDE), mixed)
            logsums = jnp.where(slim == head, top + jnp.log(total), logsums)
        low = mixed.astype(LOW)
        for half in range(Q_ROWS // ROWS):
            rows = slot_rows(at, i * (Q_ROWS // ROWS) + half)
            mixed_ref[rows, :] = low[ROWS * half : ROWS * (half + 1)]
        logsum_ref[...] = logsums

    by_block(block)


def attend_back_kernel(
    at, lengths, q_ref, k_ref, v_ref, logsum_ref, dmix_ref, out_ref, dk_total, dv_total
):
    scale = HEAD_DIM**-0.5

    def block(i):
        keys = Q_ROWS * (i + 1)
        if i == 0:
            dk_total[...] = jnp.zeros_like(dk_total)
            dv_total[...] = jnp.zeros_like(dv_total)
        q, k, v = q_ref[...], k_ref[:keys, :], v_ref[:keys, :]
        count = Q_ROWS // ROWS
        dmix = jnp.concatenate([dmix_ref[slot_rows(at, i * count + n), :] for n in range(count)])
        allowed = visible(lengths, i * Q_ROWS, Q_ROWS, keys)
        lane = lax.broadcasted_iota(jnp.int32, q.shape, 1) // HEAD_DIM
        dq = jnp.zeros(q.shape, WIDE)
        for head in range(TEAM_HEADS):
            own = lane == head
            q_own = jnp.where(own, q, jnp.zeros_like(q))
            dmix_own = jnp.where(own, dmix, jnp.zeros_like(dmix))
            scores = lax.dot_general(q_own, k, ACROSS, preferred_element_type=WIDE) * scale
            scores = jnp.where(allowed, scores, -1e30)
            probs = jnp.exp(scores - logsum_ref[:, head : head + 1])
            d_probs = lax.dot_general(dmix_own, v, ACROSS, preferred_element_type=WIDE)
            term = jnp.sum(probs * d_probs, axis=-1, keepdims=True)
            d_scores = (probs * (d_probs - term)).astype(LOW)
            dq = jnp.where(own, jnp.dot(d_scores, k, preferred_element_type=WIDE), dq)
            dk_total[:keys, :] += lax.dot_general(
                d_scores, q_own, DOWN, preferred_element_type=WIDE
            )
            dv_total[:keys, :] += lax.dot_general(
                probs.astype(LOW), dmix_own, DOWN, preferred_element_type=WIDE
            )
        out_ref[Q_ROWS * i : Q_ROWS * (i + 1), :SPAN] = (dq * scale).astype(LOW)
        if i == 8 * ROWS // Q_ROWS - 1:
            out_ref[:, SPAN : 2 * SPAN] = (dk_total[...] * scale).astype(LOW)
            out_ref[:, 2 * SPAN :] = dv_total[...].astype(LOW)

    by_block(block)


def attend_specs(rows):
    return [
        SMEM,
        SMEM,
        pl.BlockSpec((Q_ROWS, SPAN), lambda i: (i, 0)),
        pl.BlockSpec((rows, SPAN), lambda i: (0, 1)),
        pl.BlockSpec((rows, SPAN), lambda i: (0, 2)),
    ]


def attend(places, qkv):
    rows = qkv.shape[0]
    return pl.pallas_call(
        attend_kernel,
        grid=(rows // Q_ROWS,),
        in_specs=attend_specs(rows),
        out_specs=[
            pl.BlockSpec((rows, SPAN), lambda i: (0, 0)),
            pl.BlockSpec((Q_ROWS, 128), lambda i: (i, 0)),
        ],
        out_shape=[
            jax.ShapeDtypeStruct((rows, SPAN), LOW),
            jax.ShapeDtypeStruct((rows, 128), WIDE),
        ],
        compiler_params=pltpu.CompilerParams(vmem_limit_bytes=VMEM_LIMIT),
        cost_estimate=cost(0),
        name="attend",
    )(*places, qkv, qkv, qkv)


def attend_back(places, qkv, logsum, dmix):
    rows = qkv.shape[0]
    whole = lambda i: (0, 0)
    return pl.pallas_call(
        attend_back_kernel,
        grid=(rows // Q_ROWS,),
        in_specs=attend_specs(rows)
        + [pl.BlockSpec((Q_ROWS, 128), lambda i: (i, 0)), pl.BlockSpec((rows, SPAN), whole)],
        out_specs=pl.BlockSpec((rows, 3 * SPAN), whole),
        out_shape=like((rows, 3 * SPAN)),
        scratch_shapes=[pltpu.VMEM((rows, SPAN), WIDE)] * 2,
        compiler_params=pltpu.CompilerParams(vmem_limit_bytes=VMEM_LIMIT),
        cost_estimate=cost(0),
        name="attend_back",
    )(*places, qkv, qkv, qkv, logsum, dmix)


def middle_kernel(at, tokens, vectors, *refs):
    pieces, mine_refs, other_refs, refs = refs[:4], refs[4:8], refs[8:12], refs[12:]
    middle, normed, mixed_out, mixed, blocks, wide, mine, other, *sems = refs
    copies = load(weight_pairs(mine_refs, mine), sems[0])
    copies += load(weight_pairs(other_refs, other), sems[1])
    clear_pad(mine)
    clear_pad(other)
    for d, piece in enumerate(pieces):
        mixed[:, block_at(d ^ at[MEMBER])] = piece[:, :SPAN]
        mixed[:, block_at((4 + d) ^ at[MEMBER])] = piece[:, SPAN:]

    def write_blocks(k, block):
        blocks[:, block_at(k)] = block

    to_blocks(mixed, at[ME], write_blocks)
    mixed_out[...] = mixed[:, :WIDTH]
    for copy in copies:
        copy.wait()
    flat = (8 * BLOCK, FF_PART)
    a = jnp.dot(blocks[...], mine[...].reshape(flat), preferred_element_type=WIDE)
    b = jnp.dot(blocks[...], other[...].reshape(flat), preferred_element_type=WIDE)
    wide[:, :FF_PART] = jnp.where(at[CORE] == 0, a, b)
    wide[:, FF_PART:] = jnp.where(at[CORE] == 0, b, a)
    total = tokens[...].astype(WIDE) + wide[...] + vectors[4:5, :]
    middle[...] = total
    hat, _ = normalize(total)
    normed[...] = (hat * vectors[5:6, :] + vectors[6:7, :]).astype(LOW)


OUT_WEIGHT_SCRATCH = [
    pltpu.VMEM((8, BLOCK, FF_PART), LOW),
    pltpu.VMEM((8, BLOCK, FF_PART), LOW),
    pltpu.SemaphoreType.DMA((8,)),
    pltpu.SemaphoreType.DMA((8,)),
]


def proj_pairs(own, first_half, second_half, target):
    rows = FF_PART // 2
    return (
        [(own.at[pl.ds(0, rows)], target.at[pl.ds(0, rows)]), (own.at[pl.ds(rows, rows)], target.at[pl.ds(rows, rows)])],
        [(first_half, target.at[pl.ds(0, rows)]), (second_half, target.at[pl.ds(rows, rows)])],
    )


def load_proj(at, refs, target, sems):
    own, got = proj_pairs(*refs, target)

    @pl.when(at[CORE] == at[YL])
    def _():
        for copy in load(own, sems):
            copy.wait()

    @pl.when(at[CORE] != at[YL])
    def _():
        for copy in load(got, sems):
            copy.wait()


def halves(i):
    return jnp.minimum(i, 1), 0


def late_halves(i):
    return jnp.maximum(i - 2, 0), 0


def write_half(step, near, far, value):
    @pl.when(step < 2)
    def _():
        near[:, :WIDTH] = value
        near[:, WIDTH:] = jnp.zeros((value.shape[0], LANES - WIDTH), LOW)

    @pl.when(step >= 2)
    def _():
        far[:, :WIDTH] = value
        far[:, WIDTH:] = jnp.zeros((value.shape[0], LANES - WIDTH), LOW)


def feed_kernel(at, bias, *refs):
    cot_ref, normed_refs, fc_refs, proj_refs = refs[0], refs[1:9], refs[9:13], refs[13:16]
    hidden, d_in, near, far, bias_sum, normed, cot, fc, proj, wide, blocks, tall, back, *sems = (
        refs[16:]
    )
    step = pl.program_id(0)

    def normed_copy(k):
        return pltpu.make_async_copy(normed_refs[k], normed.at[k], sems[0].at[k])

    def cot_copy(k):
        rows = pl.ds(pl.multiple_of((k ^ at[MEMBER]) * ROWS, ROWS), ROWS)
        return pltpu.make_async_copy(cot_ref.at[rows], cot.at[k], sems[3].at[k])

    own, got = proj_pairs(*proj_refs, proj)
    diagonal = at[CORE] == at[YL]

    def proj_copy(i):
        return pltpu.make_async_copy(got[i][0], got[i][1], sems[2].at[i])

    @pl.when(step == 0)
    def _():
        for k in range(2):
            normed_copy(k).start()
        copies = load(weight_pairs(fc_refs, fc), sems[1])
        clear_pad(fc)
        bias_sum[...] = jnp.zeros_like(bias_sum)
        wide[:, WIDTH:] = jnp.zeros((2 * ROWS, wide.shape[1] - WIDTH), LOW)
        for copy in copies:
            copy.wait()
        for k in range(2):
            cot_copy(k).start()

        @pl.when(diagonal)
        def _():
            load(own, sems[2])

        @pl.when(jnp.logical_not(diagonal))
        def _():
            load(got, sems[2])

    for k in range(8):

        @pl.when(step == k // 2)
        def _():
            normed_copy(k).wait()

        @pl.when(step + 1 == k // 2)
        def _():
            normed_copy(k).start()
            cot_copy(k).start()

    wide[:, :WIDTH] = normed[pl.ds(step * 2, 2)].reshape(2 * ROWS, WIDTH)

    def write(k, block):
        blocks[:, block_at(k)] = block

    to_blocks(wide, at[ME], write)
    weight = fc[...].reshape(8 * BLOCK, FF_PART)
    u = jnp.dot(blocks[...], weight, preferred_element_type=WIDE) + bias[...]
    for k in range(8):

        @pl.when(step == k // 2)
        def _():
            cot_copy(k).wait()

    @pl.when(step == 0)
    def _():
        proj_copy(0).wait()
        proj_copy(1).wait()

    cot_rows = cot[pl.ds(step * 2, 2)].reshape(2 * ROWS, WIDTH)
    d_hidden = lax.dot_general(cot_rows, proj[...], ACROSS, preferred_element_type=WIDE)
    factor = (2.0 / jnp.pi) ** 0.5
    square = u * u
    bent = jnp.tanh(factor * (u + 0.044715 * (square * u)))
    half = 0.5 * (1.0 + bent)
    hidden[...] = (u * half).astype(LOW)
    slope = half + (0.5 * factor) * u * (1.0 - bent * bent) * (1.0 + (3 * 0.044715) * square)
    low = (d_hidden * slope).astype(LOW)
    d_in[...] = low
    bias_sum[...] += jnp.sum(low.astype(WIDE), axis=0, keepdims=True)
    tall[...] = lax.dot_general(low, weight, ACROSS, preferred_element_type=WIDE).astype(LOW)
    from_blocks(tall, at[ME], back)
    write_half(step, near, far, back[...])


def feed(at, normed, cot, fc, proj, bias):
    rows = 8 * ROWS
    still = lambda i: (0, 0)
    down = lambda i: (i, 0)
    return pl.pallas_call(
        feed_kernel,
        grid=(rows // Q_ROWS,),
        in_specs=[SMEM, pl.BlockSpec((1, FF_PART), still)] + [ANY] * 16,
        out_specs=[
            pl.BlockSpec((Q_ROWS, FF_PART), down),
            pl.BlockSpec((Q_ROWS, FF_PART), down),
            pl.BlockSpec((Q_ROWS, LANES), halves),
            pl.BlockSpec((Q_ROWS, LANES), late_halves),
            pl.BlockSpec((1, FF_PART), still),
        ],
        out_shape=[
            like((rows, FF_PART)),
            like((rows, FF_PART)),
            like((rows // 2, LANES)),
            like((rows // 2, LANES)),
            like((1, FF_PART), WIDE),
        ],
        scratch_shapes=[
            pltpu.VMEM((8, ROWS, WIDTH), LOW),
            pltpu.VMEM((8, ROWS, WIDTH), LOW),
            pltpu.VMEM((8, BLOCK, FF_PART), LOW),
            pltpu.VMEM((FF_PART, WIDTH), LOW),
            pltpu.VMEM((Q_ROWS, WIDTH + 192), LOW),
            pltpu.VMEM((Q_ROWS, 8 * BLOCK), LOW),
            pltpu.VMEM((Q_ROWS, 8 * BLOCK), LOW),
            pltpu.VMEM((Q_ROWS, WIDTH), LOW),
            pltpu.SemaphoreType.DMA((8,)),
            pltpu.SemaphoreType.DMA((8,)),
            pltpu.SemaphoreType.DMA((2,)),
            pltpu.SemaphoreType.DMA((8,)),
        ],
        compiler_params=pltpu.CompilerParams(vmem_limit_bytes=VMEM_LIMIT),
        cost_estimate=cost(0),
        name="feed_forward_and_back",
    )(at, bias, cot, *normed, *fc, *proj)


def final_kernel(at, hidden, *refs):
    proj_refs, (near, far, proj, sems) = refs[:3], refs[3:]
    step = pl.program_id(0)

    @pl.when(step == 0)
    def _():
        load_proj(at, proj_refs, proj, sems)

    total = jnp.dot(hidden[...], proj[...], preferred_element_type=WIDE).astype(LOW)
    write_half(step, near, far, total)


def final_part(at, hidden, proj):
    rows = hidden.shape[0]
    return pl.pallas_call(
        final_kernel,
        grid=(rows // Q_ROWS,),
        in_specs=[SMEM, pl.BlockSpec((Q_ROWS, FF_PART), lambda i: (i, 0))] + [ANY] * 3,
        out_specs=[
            pl.BlockSpec((Q_ROWS, LANES), halves),
            pl.BlockSpec((Q_ROWS, LANES), late_halves),
        ],
        out_shape=[like((rows // 2, LANES))] * 2,
        scratch_shapes=[pltpu.VMEM((FF_PART, WIDTH), LOW), pltpu.SemaphoreType.DMA((2,))],
        compiler_params=pltpu.CompilerParams(vmem_limit_bytes=VMEM_LIMIT),
        cost_estimate=cost(0),
        name="feed_forward_out",
    )(at, hidden, *proj)


def padded_rows():
    return pl.BlockSpec((ROWS, LANES), lambda i: (0, 0))


def team_total(refs):
    total = refs[0][:, :WIDTH].astype(WIDE)
    for ref in refs[1:]:
        total = total + ref[:, :WIDTH].astype(WIDE)
    return total


def row_sum(value):
    return jnp.sum(value, axis=0, keepdims=True)


def pair_kernel(near, got, *outs):
    total = (near[...].astype(WIDE) + got[...].astype(WIDE)).astype(LOW)
    for d, out in enumerate(outs):

        @pl.when(pl.program_id(0) == d)
        def _():
            out[...] = total


def pair_sums(near, got):
    rows, columns = near.shape[0] // 4, near.shape[1]
    part = pl.BlockSpec((rows, columns), lambda i: (i + 1, 0))
    return pl.pallas_call(
        pair_kernel,
        grid=(3,),
        in_specs=[part] * 2,
        out_specs=[pl.BlockSpec((rows, columns), lambda i: (0, 0))] * 3,
        out_shape=[like((rows, columns))] * 3,
        compiler_params=pltpu.CompilerParams(vmem_limit_bytes=VMEM_LIMIT),
        cost_estimate=cost(0),
        name="pair_sums",
    )(near, got)


def output_kernel(middle, vectors, near, got, one, two, three, out):
    total = middle[...] + vectors[7:8, :]
    out[...] = (total + team_total([near, got, one, two, three])).astype(LOW)


def output_rows(middle, vectors, parts):
    part = pl.BlockSpec((ROWS, WIDTH), lambda i: (0, 0))
    return pl.pallas_call(
        output_kernel,
        grid=(1,),
        in_specs=[part, pl.BlockSpec((8, WIDTH), lambda i: (0, 0))] + [padded_rows()] * 5,
        out_specs=part,
        out_shape=like((ROWS, WIDTH)),
        compiler_params=pltpu.CompilerParams(vmem_limit_bytes=VMEM_LIMIT),
        cost_estimate=cost(0),
        name="output_rows",
    )(middle, vectors, *parts)


def out_grad_kernel(at, left, right, keep, give, total):
    total[:WIDTH, :] = lax.dot_general(
        left[...], right[...], DOWN, preferred_element_type=WIDE
    )
    for out, flip in ((keep, 0), (give, 4)):
        for d in range(4):
            start = pl.multiple_of((at[MEMBER] ^ (flip + d)) * SHARD, 8)
            out[CARRY * d : CARRY * (d + 1), :] = total[pl.ds(start, CARRY), :].astype(LOW)


def out_grad(at, left, right):
    return whole_call(
        out_grad_kernel,
        "out_grad",
        [like((4 * CARRY, WIDTH))] * 2,
        at,
        left,
        right,
        scratch=[pltpu.VMEM((WIDTH + CARRY - SHARD, WIDTH), WIDE)],
    )


def second_back_kernel(at, middle, cot, vectors, near, got, *refs):
    parts, mine_refs, other_refs, refs = refs[:3], refs[3:7], refs[7:11], refs[11:]
    (d_middle, d_branch, sums), pieces, refs = refs[:3], refs[3:7], refs[7:]
    wide, tall, narrow, mine, other, *sems = refs
    copies = load(weight_pairs(mine_refs, mine), sems[0])
    copies += load(weight_pairs(other_refs, other), sems[1])
    clear_pad(mine)
    clear_pad(other)
    d_second = team_total([near, got, *parts])
    hat, inverse = normalize(middle[...])
    d_cot = cot[...].astype(WIDE)
    total = d_cot + norm_back(d_second, hat, inverse, vectors[5:6, :])
    d_middle[...] = total
    low = total.astype(LOW)
    d_branch[...] = low
    sums[0:1, :] = row_sum(d_second * hat)
    sums[1:2, :] = row_sum(d_second)
    sums[2:3, :] = row_sum(low.astype(WIDE))
    sums[3:4, :] = row_sum(d_cot)
    sums[4:8, :] = jnp.zeros((4, WIDTH), WIDE)
    wide[...] = low
    left, right = wide[:, :FF_PART], wide[:, FF_PART:]
    first_core = at[CORE] == 0
    flat = (8 * BLOCK, FF_PART)
    across = (((1,), (1,)), ((), ()))
    for copy in copies:
        copy.wait()
    tall[...] = lax.dot_general(
        jnp.where(first_core, left, right),
        mine[...].reshape(flat),
        across,
        preferred_element_type=WIDE,
    ) + lax.dot_general(
        jnp.where(first_core, right, left),
        other[...].reshape(flat),
        across,
        preferred_element_type=WIDE,
    )
    narrow[:, WIDTH:] = jnp.zeros((ROWS, 8 * SPAN - WIDTH), LOW)
    from_blocks(tall, at[ME], narrow)
    for d, piece in enumerate(pieces):
        piece[:, :SPAN] = narrow[:, block_at(d ^ at[MEMBER])]
        piece[:, SPAN:] = narrow[:, block_at((4 + d) ^ at[MEMBER])]


def second_back(at, middle, cot, vectors, near, got, parts, mine, other):
    part = pl.BlockSpec((ROWS, WIDTH), lambda i: (0, 0))
    return pl.pallas_call(
        second_back_kernel,
        grid=(1,),
        in_specs=[SMEM, part, part, pl.BlockSpec((8, WIDTH), lambda i: (0, 0))]
        + [padded_rows()] * 5
        + [ANY] * 8,
        out_specs=[VMEM] * 7,
        out_shape=[like((ROWS, WIDTH), WIDE), like((ROWS, WIDTH)), like((8, WIDTH), WIDE)]
        + [like((ROWS, 2 * SPAN))] * 4,
        scratch_shapes=[
            pltpu.VMEM((ROWS, WIDTH), LOW),
            pltpu.VMEM((ROWS, 8 * BLOCK), WIDE),
            pltpu.VMEM((ROWS, 8 * SPAN), LOW),
        ]
        + OUT_WEIGHT_SCRATCH,
        compiler_params=pltpu.CompilerParams(vmem_limit_bytes=VMEM_LIMIT),
        cost_estimate=cost(0),
        name="second_norm_and_out_back",
    )(at, middle, cot, vectors, near, got, *parts, *mine, *other)


def first_back_kernel(at, d_qkv, *refs):
    weight_refs, (near, far, sums, weight, tall, back, sems) = refs[:4], refs[4:]
    step = pl.program_id(0)

    @pl.when(step == 0)
    def _():
        copies = load(weight_pairs(weight_refs, weight), sems)
        clear_pad(weight)
        sums[...] = row_sum(d_qkv[...].astype(WIDE))
        for copy in copies:
            copy.wait()

    rows = jnp.concatenate([d_qkv[slot_rows(at, 2 * step + n), :] for n in range(2)])
    tall[...] = lax.dot_general(
        rows, weight[...].reshape(8 * BLOCK, 3 * SPAN), ACROSS, preferred_element_type=WIDE
    ).astype(LOW)
    from_blocks(tall, at[ME], back)
    write_half(step, near, far, back[...])


def first_back(at, d_qkv, weight):
    rows = d_qkv.shape[0]
    whole = lambda i: (0, 0)
    return pl.pallas_call(
        first_back_kernel,
        grid=(rows // Q_ROWS,),
        in_specs=[SMEM, pl.BlockSpec((rows, 3 * SPAN), whole)] + [ANY] * 4,
        out_specs=[
            pl.BlockSpec((Q_ROWS, LANES), halves),
            pl.BlockSpec((Q_ROWS, LANES), late_halves),
            pl.BlockSpec((1, 3 * SPAN), whole),
        ],
        out_shape=[
            like((rows // 2, LANES)),
            like((rows // 2, LANES)),
            like((1, 3 * SPAN), WIDE),
        ],
        scratch_shapes=[
            pltpu.VMEM((8, BLOCK, 3 * SPAN), LOW),
            pltpu.VMEM((Q_ROWS, 8 * BLOCK), LOW),
            pltpu.VMEM((Q_ROWS, WIDTH), LOW),
            pltpu.SemaphoreType.DMA((8,)),
        ],
        compiler_params=pltpu.CompilerParams(vmem_limit_bytes=VMEM_LIMIT),
        cost_estimate=cost(0),
        name="qkv_back",
    )(at, d_qkv, *weight)


SUMS = (PIECE, FF_PART)


def input_kernel(at, tokens, d_middle, vectors, second_sums, fc_sum, qkv_sum, *refs):
    parts, (grad, sums, held) = refs[:5], refs[5:]
    d_first = team_total(parts)
    hat, inverse = normalize(tokens[...].astype(WIDE))
    grad[...] = (d_middle[...] + norm_back(d_first, hat, inverse, vectors[0:1, :])).astype(LOW)
    held[...] = jnp.zeros(SUMS, WIDE)
    rows = [row_sum(d_first * hat), row_sum(d_first)] + [second_sums[i : i + 1, :] for i in range(4)]
    for i, row in enumerate(rows):
        held[2 * i : 2 * i + 1, :] = row[:, :FF_PART]
        held[2 * i + 1 : 2 * i + 2, :] = row[:, FF_PART:]
    held[pl.ds(16 + at[MEMBER], 1), :] = fc_sum[...]
    held[pl.ds(24 + at[MEMBER], 1), :SPAN] = qkv_sum[:, :SPAN]
    held[pl.ds(32 + at[MEMBER], 1), :SPAN] = qkv_sum[:, 2 * SPAN :]
    sums[0] = held[...].astype(LOW)


def input_back(at, tokens, d_middle, vectors, second_sums, fc_sum, qkv_sum, parts):
    still = lambda i: (0, 0)
    part = pl.BlockSpec((ROWS, WIDTH), still)
    rows = pl.BlockSpec((8, WIDTH), still)
    return pl.pallas_call(
        input_kernel,
        grid=(1,),
        in_specs=[
            SMEM,
            part,
            part,
            rows,
            rows,
            pl.BlockSpec((1, FF_PART), still),
            pl.BlockSpec((1, 3 * SPAN), still),
        ]
        + [padded_rows()] * 5,
        out_specs=[part, pl.BlockSpec((1,) + SUMS, lambda i: (0, 0, 0))],
        out_shape=[like((ROWS, WIDTH)), like((1,) + SUMS)],
        scratch_shapes=[pltpu.VMEM(SUMS, WIDE)],
        compiler_params=pltpu.CompilerParams(vmem_limit_bytes=VMEM_LIMIT),
        cost_estimate=cost(0),
        name="first_norm_back",
    )(at, tokens, d_middle, vectors, second_sums, fc_sum, qkv_sum, *parts)


def feed_grad_kernel(at, hidden, d_in, cot_ref, *refs):
    normed_refs, (out, normed, cot, total, tall, *sems) = refs[:8], refs[8:]
    pairs = [(normed_refs[k], normed.at[k]) for k in range(8)]
    first_copies = load(pairs, sems[0])
    pairs = [
        (cot_ref.at[pl.ds(pl.multiple_of((k ^ at[MEMBER]) * ROWS, ROWS), ROWS)], cot.at[k])
        for k in range(8)
    ]
    second_copies = load(pairs, sems[1])
    for copy in first_copies:
        copy.wait()
    total[...] = lax.dot_general(
        normed[...].reshape(8 * ROWS, WIDTH), d_in[...], DOWN, preferred_element_type=WIDE
    )
    for k in range(8):
        for q in range(4):
            start = pl.multiple_of((k ^ at[ME]) * SHARD + PIECE_STEP * q, 8)
            out[16 * q + k] = total[pl.ds(start, PIECE), :].astype(LOW)
    for copy in second_copies:
        copy.wait()
    tall[...] = lax.dot_general(
        hidden[...], cot[...].reshape(8 * ROWS, WIDTH), DOWN, preferred_element_type=WIDE
    )
    for q in range(4):
        for half in range(2):
            lanes = slice(FF_PART * half, FF_PART * (half + 1))
            for k in range(4):
                start = SHARD * q + PIECE_STEP * k
                out[16 * q + 8 + 4 * half + k] = tall[start : start + PIECE, lanes].astype(LOW)


def feed_grad(at, normed, d_in, hidden, cot):
    rows = 8 * ROWS
    return pl.pallas_call(
        feed_grad_kernel,
        in_specs=[SMEM, VMEM, VMEM] + [ANY] * 9,
        out_specs=VMEM,
        out_shape=like((64, PIECE, FF_PART)),
        scratch_shapes=[
            pltpu.VMEM((8, ROWS, WIDTH), LOW),
            pltpu.VMEM((8, ROWS, WIDTH), LOW),
            pltpu.VMEM((WIDTH, FF_PART), WIDE),
            pltpu.VMEM((FF_PART, WIDTH), WIDE),
            pltpu.SemaphoreType.DMA((8,)),
            pltpu.SemaphoreType.DMA((8,)),
        ],
        compiler_params=pltpu.CompilerParams(vmem_limit_bytes=VMEM_LIMIT),
        cost_estimate=cost(0),
        name="feed_forward_grad",
    )(at, hidden, d_in, cot, *normed)


def qkv_grad_kernel(at, normed, d_qkv, near, got, one, two, three, *refs):
    outs, (total, tall) = refs[:4], refs[4:]
    total[:, 3 * SPAN :] = jnp.zeros((WIDTH, FF_PART - 3 * SPAN), WIDE)
    total[:, : 3 * SPAN] = lax.dot_general(
        normed[...], d_qkv[...], DOWN, preferred_element_type=WIDE
    )
    tall[...] = team_total([near, got, one, two, three])
    for d, out in enumerate(outs):
        place = pl.multiple_of((at[X] ^ d) * PIECE_STEP, 8)
        for k in range(8):
            start = pl.multiple_of((k ^ at[ME]) * SHARD + place, 8)
            out[k] = total[pl.ds(start, PIECE), :].astype(LOW)
        piece = tall[pl.ds(place, PIECE), :].astype(LOW)
        out[8] = piece[:, :FF_PART]
        out[9] = piece[:, FF_PART:]


def qkv_grad(at, normed, d_qkv, out_parts):
    part = pl.BlockSpec((CARRY, WIDTH), lambda i: (0, 0))
    return pl.pallas_call(
        qkv_grad_kernel,
        grid=(1,),
        in_specs=[SMEM, VMEM, VMEM] + [part] * 5,
        out_specs=[VMEM] * 4,
        out_shape=[like((10, PIECE, FF_PART))] * 4,
        scratch_shapes=[pltpu.VMEM((WIDTH, FF_PART), WIDE), pltpu.VMEM((CARRY, WIDTH), WIDE)],
        compiler_params=pltpu.CompilerParams(vmem_limit_bytes=VMEM_LIMIT),
        cost_estimate=cost(0),
        name="qkv_and_out_grad",
    )(at, normed, d_qkv, *out_parts)


def added(refs, k):
    total = refs[0][k].astype(WIDE)
    for ref in refs[1:]:
        total = total + ref[k].astype(WIDE)
    return total.astype(LOW)


def feed_mid_kernel(at, total, half_got, keep, give_fc, give_proj):
    own = at[CORE] == at[YL]
    keep[:4] = total[:4]
    give_fc[...] = total[4:8]
    mine, other = total[pl.ds(8 + 4 * at[CORE], 4)], half_got[...]
    keep[4:] = jnp.where(own, mine, other)
    give_proj[...] = jnp.where(own, other, mine)


def add_halves_kernel(at, keep, first_half, second_half, out):
    count = first_half.shape[0]
    for k in range(keep.shape[0]):
        half = (first_half, k) if k < count else (second_half, k - count)
        out[k] = (keep[k].astype(WIDE) + half[0][half[1]].astype(WIDE)).astype(LOW)


def split_sum_kernel(at, one, two, *outs):
    place = 0
    for out in outs:
        for k in range(out.shape[0]):
            out[k] = added((one, two), place)
            place += 1


def sum_blocks_kernel(*refs):
    parts, outs = refs[1:5], refs[5:]
    place = 0
    for out in outs:
        for k in range(out.shape[0]):
            out[k] = added(parts, place)
            place += 1


def qkv_x_kernel(at, *refs):
    parts, (keep, give_one, give_two) = refs[:4], refs[4:]
    for k in range(4):
        keep[k] = added(parts, k)
        value = added(parts, 4 + k)
        if k < 3:
            give_one[k] = value
        else:
            give_two[0] = value
    for k in range(2):
        value = added(parts, 8 + k)
        keep[4 + k] = value
        give_two[1 + k] = value


def qkv_z_kernel(at, own, sums, one, two, three, rest, out):
    out[0] = own[0]
    total = sums[0].astype(WIDE)
    for k, got in enumerate((one, two, three)):
        out[1 + k] = got[0]
        total = total + got[1].astype(WIDE)
    out[4:6] = rest[...]
    out[6] = total.astype(LOW)


def feed_z_kernel(at, own, one, two, three, rest, out):
    for k, got in enumerate((own, one, two, three)):
        out[k] = got[0]
    out[4:] = rest[...]


def place_kernel(plan, at, *refs):
    mine, other = refs[:4], refs[4:8]
    outs, held, scratch = (refs[8:10], refs[10], ()) if plan is fc_columns else (
        refs[8:19],
        refs[19],
        refs[20:],
    )
    for k in range(4):
        held[0, k] = mine[k][...]
        held[1, k] = other[k][...]
    for q in range(4):
        count = PIECE_STEP if q < 3 else PIECE
        for c in range(2):
            for z in range(4):
                block = held[c ^ at[CORE], q ^ at[X], z ^ at[Z]].astype(WIDE)
                for start, stop, target in plan(c * 4 + z):
                    outs[0][
                        PIECE_STEP * q : PIECE_STEP * q + count, target : target + stop - start
                    ] = block[:count, start:stop]
    if plan is fc_columns:
        for q in range(4):
            for c in range(2):
                for k in range(4):
                    count = PIECE_STEP if k < 3 else PIECE
                    row = SHARD * q + PIECE_STEP * k
                    block = held[c ^ at[CORE], q ^ at[X], 4 + k].astype(WIDE)
                    outs[1][row : row + count, FF_PART * c : FF_PART * (c + 1)] = block[:count]
    else:
        core = at[CORE] ^ jnp.where(at[CORE] == at[YL], 0, 1) ^ at[CORE]
        for q in range(4):
            count = PIECE_STEP if q < 3 else PIECE
            for half in range(2):
                block = held[core, q ^ at[X], 4 + half].astype(WIDE)
                outs[1][
                    PIECE_STEP * q : PIECE_STEP * q + count,
                    FF_PART * half : FF_PART * (half + 1),
                ] = block[:count]
        total = held[0, 0, 6].astype(WIDE)
        for core in range(2):
            for k in range(4):
                if core + k:
                    total = total + held[core, k, 6].astype(WIDE)
        place_vectors(at, total, *outs[2:], *scratch)


def place_vectors(at, total, *refs):
    outs, (small, joined) = refs[:9], refs[9:]
    small[...] = total
    for i in range(6):
        row = small[pl.ds(2 * i + at[ME] // 4, 1), :]
        for k in range(4):

            @pl.when(at[ME] % 4 == k)
            def _():
                outs[i][...] = row[:, SHARD * k : SHARD * (k + 1)].reshape(SHARD)

    outs[6][...] = small[pl.ds(16 + at[ME], 1), :].reshape(FF_PART)
    for n in range(2):
        for k in range(8):
            at_row = 24 + 8 * n + k
            joined[:, SPAN * k : SPAN * (k + 1)] = small[at_row : at_row + 1, :SPAN]
        for k in range(8):

            @pl.when(at[ME] == k)
            def _():
                outs[7 + n][...] = joined[:, SHARD * k : SHARD * (k + 1)].reshape(SHARD)


def fc_columns(j):
    return [(0, FF_PART, FF_PART * j)]


def qkv_columns(j):
    count = min(SPAN, WIDTH - SPAN * j)
    if count <= 0:
        return []
    return [(SPAN * p, SPAN * p + count, WIDTH * p + SPAN * j) for p in range(3)]


def gather_rows(block, *gates, late=()):
    beside = c_swap(block)
    sent = after(block, *gates)
    near = {d: z_swap(sent, d) for d in (1, 3, 2)}
    far = {d: c_swap(after(near[d], *late)) for d in (1, 3, 2)}
    return [block, near[1], near[2], near[3], beside, far[1], far[2], far[3]], list(near.values())


def team_parts(near, far, c_gates=(), z_gates=()):
    got = c_swap(after(far, *c_gates))
    sent = after(pair_sums(near, got), *z_gates)
    came = [z_swap(sent[d - 1], d) for d in (1, 3, 2)]
    return [near, got] + came, sent, came


def z_blocks(own, sends, *gates):
    sends = after(sends, *gates)
    near = {d: z_swap(sends[d], d) for d in (1, 3, 2)}
    near[0] = own
    return near


def far_blocks(near, *gates):
    near = after(near, *gates)
    one, two = jnp.stack([near[0], near[1]]), jnp.stack([near[2], near[3]])
    return [one, two, y_swap(one, 1), y_swap(two, 3)]


def spread_x(value, swap):
    got = [swap(value, d) for d in (1, 3)]
    two = swap(after(value, got), 2)
    return [value, got[0], two, got[1]]


def add(values):
    total = values[0].astype(WIDE)
    for value in values[1:]:
        total = total + value.astype(WIDE)
    return total.astype(LOW)


def local(
    tokens,
    lengths,
    ln1_gain,
    ln1_bias,
    qkv_weight,
    q_bias,
    v_bias,
    out_weight,
    out_bias,
    ln2_gain,
    ln2_bias,
    fc_weight,
    fc_bias,
    proj_weight,
    proj_bias,
    cotangent,
):
    c, x, yl, z = (lax.axis_index(a) for a in ("c", "x", "yl", "z"))
    me, member = yl * 4 + z, c * 4 + z
    at = jnp.stack([me, member, c, x, yl, z]).astype(jnp.int32)

    vectors = [ln1_gain, ln1_bias, q_bias, v_bias, out_bias, ln2_gain, ln2_bias, proj_bias, fc_bias]
    own_tokens = turn(tokens)
    qkv_sends = whole_call_any(
        prepare_qkv_kernel,
        "prepare_qkv",
        [like((CARRY, 3 * SPAN))] * 4,
        [at, qkv_weight],
        vectors,
        scratch=[pltpu.VMEM(v.shape, LOW) for v in vectors] + [pltpu.SemaphoreType.DMA((9,))],
    )
    qkv_near = z_blocks(qkv_sends[0], qkv_sends)
    half = proj_weight.shape[0] // 2
    proj_sends = proj_weight[:half], proj_weight[half:]

    other_lengths = c_swap(lengths)
    places = at, jnp.where(c == yl, lengths, other_lengths)

    out_half, *fc_sends = whole_call(
        prepare_rest_kernel,
        "prepare_rest",
        [like((CARRY, FF_PART))] * 5,
        at,
        after(fc_weight, qkv_sends),
        out_weight,
    )
    weight_qkv = far_blocks(qkv_near)
    all_tokens, tokens_came = gather_rows(
        own_tokens, qkv_near, out_half, fc_sends, places, proj_sends, late=(weight_qkv,)
    )
    own_cotangent = turn(after(cotangent, qkv_near))
    all_cotangent = lax.all_gather(
        after(own_cotangent, tokens_came), ("c", "z"), axis=0, tiled=True
    )
    out_near = z_blocks(out_half, [out_half] * 4, tokens_came)
    proj_sent = after(proj_sends, tokens_came)
    proj_pieces = [
        proj_weight,
        y_swap_some(proj_sent[0], 1, True),
        y_swap_some(proj_sent[1], 3, True),
    ]

    normed_first, qkv, vectors_all, fc_bias_own = first(at, all_tokens, weight_qkv)
    qkv = after(qkv, out_near, proj_pieces)
    out_mine = far_blocks(out_near, qkv)
    fc_near = z_blocks(fc_sends[0], fc_sends, qkv)
    mixed_heads, logsum = attend(places, qkv)
    mixed_heads = after(mixed_heads, out_mine, fc_near)

    mixed_near = mixed_heads[: 4 * ROWS]
    mixed_got = c_swap(mixed_heads[4 * ROWS :])
    mixed_sent = [
        jnp.concatenate([v[ROWS * d : ROWS * (d + 1)] for v in (mixed_near, mixed_got)], axis=1)
        for d in range(4)
    ]
    mixed_pieces = [mixed_sent[0]] + [z_swap(mixed_sent[d], d) for d in (1, 2, 3)]
    out_other = [c_swap(after(piece, mixed_sent)) for piece in out_mine]
    middle, normed_second, mixed = whole_call_any(
        middle_kernel,
        "out_and_second_norm",
        [like((ROWS, WIDTH), WIDE), like((ROWS, WIDTH)), like((ROWS, WIDTH))],
        [at, own_tokens, vectors_all] + mixed_pieces,
        out_mine + out_other,
        scratch=[
            pltpu.VMEM((ROWS, 8 * SPAN), LOW),
            pltpu.VMEM((ROWS, 8 * BLOCK), LOW),
            pltpu.VMEM((ROWS, WIDTH), WIDE),
        ]
        + OUT_WEIGHT_SCRATCH,
    )

    all_second, second_came = gather_rows(normed_second)
    weight_fc = far_blocks(fc_near, normed_second)
    hidden, d_hidden_in, d_second_near, d_second_far, fc_bias_sum = feed(
        at, all_second, all_cotangent, weight_fc, proj_pieces, fc_bias_own
    )
    d_second_parts, d_second_sent, d_second_came = team_parts(d_second_near, d_second_far)

    hidden_late = after(hidden, d_second_sent)
    feed_pieces = feed_grad(at, all_second, d_hidden_in, hidden_late, all_cotangent)
    feed_total = lax.psum_scatter(
        after(feed_pieces, d_second_came), "x", scatter_dimension=0, tiled=True
    )

    d_middle, d_branch, second_sums, *d_mixed = second_back(
        at,
        middle,
        own_cotangent,
        after(vectors_all, feed_pieces),
        d_second_parts[0],
        d_second_parts[1],
        d_second_parts[2:],
        out_mine,
        out_other,
    )
    d_got = [d_mixed[0]] + [z_swap(d_mixed[d], d) for d in (1, 2, 3)]
    out_keep, out_give = out_grad(at, mixed, d_branch)
    out_got = c_swap(after(out_give, d_got))
    out_sent = pair_sums(out_keep, out_got)
    d_keep = jnp.concatenate([v[:, :SPAN] for v in d_got])
    d_give = jnp.concatenate([v[:, SPAN:] for v in d_got])
    d_mixed_heads = jnp.concatenate([d_keep, c_swap(d_give)])
    out_sent = after(out_sent, d_give)
    out_came = [z_swap(out_sent[d - 1], d) for d in (1, 3, 2)]
    d_mixed_heads = after(d_mixed_heads, out_sent)
    d_qkv = attend_back(places, qkv, logsum, d_mixed_heads)

    def blocks_call(body, name, counts, *args):
        outs = [like((count, PIECE, FF_PART)) for count in counts]
        return whole_call(body, name, outs, at, *args)

    d_qkv = after(d_qkv, out_came)
    qkv_pieces = qkv_grad(at, normed_first, d_qkv, [out_keep, out_got] + out_came)
    qkv_got = [x_swap(qkv_pieces[d], d) for d in (1, 3)]
    feed_total = after(feed_total, qkv_pieces)
    half_got = c_swap(lax.dynamic_slice_in_dim(feed_total, 12 - 4 * c, 4, 0))
    feed_keep, give_fc, give_proj = blocks_call(
        feed_mid_kernel, "feed_mid", [8, 4, 4], feed_total, half_got
    )
    feed_y = [y_swap(give_fc, 1), y_swap(give_proj, 3)]
    d_first_near, d_first_far, qkv_sums = first_back(at, after(d_qkv, give_fc), weight_qkv)
    qkv_got.append(x_swap(after(qkv_pieces[2], qkv_got), 2))
    d_first_parts, d_first_sent, d_first_came = team_parts(
        d_first_near, d_first_far, (qkv_got[:2], feed_y)
    )
    (feed_half,) = blocks_call(
        add_halves_kernel, "feed_half", [8], after(feed_keep, d_first_sent), *feed_y
    )
    feed_last = y_swap(feed_half, 2)
    final_near, final_far = final_part(at, after(hidden, feed_half), proj_pieces)
    grad_low, sums = input_back(
        at, own_tokens, d_middle, vectors_all, second_sums, fc_bias_sum, qkv_sums, d_first_parts
    )
    input_grad = turn(grad_low).astype(WIDE)
    sums_y = [y_swap(sums, 1), y_swap(sums, 3)]

    qkv_keep, give_one, give_two = blocks_call(
        qkv_x_kernel, "qkv_x", [6, 3, 3], after(qkv_pieces[0], sums, feed_last), *qkv_got
    )
    qkv_y = [y_swap(give_one, 1), y_swap(give_two, 3)]
    feed_own, feed_one, feed_two, feed_three, feed_rest = blocks_call(
        split_sum_kernel, "feed_y", [1, 1, 1, 1, 4], after(feed_half, give_one), feed_last
    )
    feed_z = [z_swap(part, d) for d, part in ((1, feed_one), (2, feed_two), (3, feed_three))]
    sums_y.append(y_swap(after(sums, sums_y), 2))
    (qkv_half,) = blocks_call(add_halves_kernel, "qkv_half", [6], qkv_keep, *qkv_y)
    qkv_last = y_swap(qkv_half, 2)
    (feed_rows,) = blocks_call(
        feed_z_kernel, "feed_z", [8], after(feed_own, qkv_half), *feed_z, feed_rest
    )
    feed_rows = spread_x(feed_rows, x_swap)
    (sums_total,) = blocks_call(sum_blocks_kernel, "sums_y", [1], sums, *sums_y)
    qkv_own, qkv_one, qkv_two, qkv_three, qkv_rest = blocks_call(
        split_sum_kernel, "qkv_y", [1, 1, 1, 1, 2], qkv_half, qkv_last
    )
    qkv_z = [
        z_swap(jnp.concatenate([part, sums_total]), d)
        for d, part in ((1, qkv_one), (2, qkv_two), (3, qkv_three))
    ]
    (qkv_rows,) = blocks_call(
        qkv_z_kernel, "qkv_z", [7], qkv_own, sums_total, *qkv_z, qkv_rest
    )
    qkv_rows = spread_x(qkv_rows, x_swap)
    final_parts, final_sent, final_came = team_parts(final_near, final_far, (), (qkv_z,))
    output = turn(output_rows(middle, vectors_all, final_parts))
    feed_other = [c_swap(part) for part in feed_rows]
    qkv_other = [c_swap(part) for part in qkv_rows]

    grad_fc, grad_proj = whole_call(
        functools.partial(place_kernel, fc_columns),
        "place_fc",
        [like((SHARD, 8 * FF_PART), WIDE), like((FF_PART, WIDTH), WIDE)],
        at,
        *feed_rows,
        *feed_other,
        scratch=[pltpu.VMEM((2, 4, 8) + SUMS, LOW)],
    )
    vector_shapes = [like((SHARD,), WIDE)] * 6 + [like((FF_PART,), WIDE)]
    vector_shapes += [like((SHARD,), WIDE)] * 2
    grad_qkv, grad_out, *vector_grads = whole_call(
        functools.partial(place_kernel, qkv_columns),
        "place_qkv",
        [like((SHARD, 3 * WIDTH), WIDE), like((SHARD, WIDTH), WIDE)] + vector_shapes,
        at,
        *qkv_rows,
        *qkv_other,
        scratch=[
            pltpu.VMEM((2, 4, 7) + SUMS, LOW),
            pltpu.VMEM(SUMS, WIDE),
            pltpu.VMEM((1, 8 * SPAN), WIDE),
        ],
    )

    g_gain_one, g_bias_one, g_gain_two, g_bias_two, g_out_b, g_proj_b = vector_grads[:6]
    g_fc_b, g_query_b, g_value_b = vector_grads[6:]

    return (
        output,
        input_grad,
        g_gain_one,
        g_bias_one,
        grad_qkv,
        g_query_b,
        g_value_b,
        grad_out,
        g_out_b,
        g_gain_two,
        g_bias_two,
        grad_fc,
        g_fc_b,
        grad_proj,
        g_proj_b,
    )


def solution(mesh):
    fine = Mesh(mesh.devices.reshape(2, 4, 2, 2, 4), ("yh", "x", "c", "yl", "z"))
    group, owner = ("yh", "x", "c"), ("yl", "z")
    everyone = group + owner
    vector, matrix = P(owner), P(owner, None)
    rows = P(everyone, None)
    return jax.shard_map(
        local,
        mesh=fine,
        in_specs=(
            rows,
            P(group, None),
            vector,
            vector,
            matrix,
            vector,
            vector,
            matrix,
            vector,
            vector,
            vector,
            matrix,
            vector,
            matrix,
            vector,
            rows,
        ),
        out_specs=(
            rows,
            rows,
            vector,
            vector,
            matrix,
            vector,
            vector,
            matrix,
            vector,
            vector,
            vector,
            matrix,
            vector,
            matrix,
            vector,
        ),
        check_vma=False,
    )
```

```python
import jax
import jax.numpy as jnp
from jax import lax
from jax.experimental import pallas as pl
from jax.experimental.pallas import tpu as pltpu
from jax.sharding import Mesh
from jax.sharding import PartitionSpec as P

HEADS = 25
HEAD_DIM = 64
EPSILON = 1e-05
LOW = jnp.bfloat16
WIDE = jnp.float32

TEAM_HEADS = 4
SPAN = TEAM_HEADS * HEAD_DIM
SHARD = 200
BLOCK = 256
CARRY = 208
WIDTH = 1600
LANES = 1664
ROWS = 128
FF_PART = 800
PIECE = 56
PIECE_STEP = 48
VMEM_LIMIT = 60 * 1024 * 1024
SMALL_LIMIT = 24 * 1024 * 1024


def after(value, *others):
    if not jax.tree.leaves(others):
        return value
    return lax.optimization_barrier((value, others))[0]


def z_swap(value, step):
    return lax.ppermute(value, "z", [(i, i ^ step) for i in range(4)])


def x_swap(value, step):
    return lax.ppermute(value, "x", [(i, i ^ step) for i in range(4)])


def y_swap(value, step):
    return lax.ppermute(value, ("yh", "yl"), [(i, i ^ step) for i in range(4)])


def c_swap(value):
    return lax.ppermute(value, "c", [(0, 1), (1, 0)])


def team_swap(value, slot):
    return lax.ppermute(value, ("c", "z"), [(i, i ^ slot) for i in range(8)])


def turn(value):
    return lax.ppermute(value, ("c", "yl"), [(0, 0), (1, 2), (2, 1), (3, 3)])


def y_swap_some(value, step, sender_diagonal):
    pairs = []
    for yh in range(2):
        for c in range(2):
            for yl in range(2):
                if (c == yl) == sender_diagonal:
                    y = (yh * 2 + yl) ^ step
                    pairs.append((yh * 4 + c * 2 + yl, (y // 2) * 4 + c * 2 + y % 2))
    return lax.ppermute(value, ("yh", "c", "yl"), pairs)


def x_swap_diagonal(value, step):
    pairs = []
    for x in range(4):
        for c in range(2):
            pairs.append((x * 4 + c * 3, (x ^ step) * 4 + c * 3))
    return lax.ppermute(value, ("x", "c", "yl"), pairs)


def pick(blocks, index):
    return lax.dynamic_index_in_dim(blocks, index, 0, keepdims=False)


DOWN = (((0,), (0,)), ((), ()))


ME, MEMBER, CORE, X, YL, Z = range(6)

def cost(microseconds):
    return pl.CostEstimate(flops=microseconds * 10**9, bytes_accessed=0, transcendentals=0)


SMEM = pl.BlockSpec(memory_space=pltpu.SMEM)
VMEM = pl.BlockSpec(memory_space=pltpu.VMEM)
ANY = pl.BlockSpec(memory_space=pltpu.HBM)


def like(shape, dtype=LOW):
    return jax.ShapeDtypeStruct(shape, dtype)


def whole_call(body, name, outs, *args, scratch=(), limit=SMALL_LIMIT):
    return pl.pallas_call(
        body,
        in_specs=[SMEM] + [VMEM] * (len(args) - 1),
        out_specs=[VMEM] * len(outs),
        out_shape=list(outs),
        scratch_shapes=list(scratch),
        compiler_params=pltpu.CompilerParams(vmem_limit_bytes=limit),
        cost_estimate=cost(0),
        name=name,
    )(*args)


def whole_call_any(body, name, outs, args, others, scratch=()):
    return pl.pallas_call(
        body,
        in_specs=[SMEM] + [VMEM] * (len(args) - 1) + [ANY] * len(others),
        out_specs=[VMEM] * len(outs),
        out_shape=list(outs),
        scratch_shapes=list(scratch),
        compiler_params=pltpu.CompilerParams(vmem_limit_bytes=VMEM_LIMIT),
        cost_estimate=cost(0),
        name=name,
    )(*args, *others)


def block_at(index):
    return pl.ds(pl.multiple_of(index * BLOCK, BLOCK), BLOCK)


def to_blocks(source, mine, write):
    lane = lax.broadcasted_iota(jnp.int32, (source.shape[0], BLOCK), 1)
    for s in range(8):
        block = source[:, SHARD * s : SHARD * s + BLOCK]
        write(s ^ mine, jnp.where(lane < SHARD, block, jnp.zeros_like(block)))


def from_blocks(source, mine, target):
    for s in range(8):
        block = source[:, block_at(s ^ mine)]
        target[:, SHARD * s : SHARD * s + SHARD] = block[:, :SHARD].astype(target.dtype)


def prepare_qkv_kernel(at, weight, *refs):
    held, outs, vectors, sems = refs[:9], refs[9:13], refs[13:22], refs[22]
    copies = load(list(zip(held, vectors)), sems)
    for copy in copies:
        copy.wait()
    lane = lax.broadcasted_iota(jnp.int32, (SHARD, SPAN), 1)
    for d, out in enumerate(outs):
        j = at[CORE] * 4 + (at[Z] ^ d)
        valid = lane < WIDTH - SPAN * j
        none = jnp.zeros((SHARD, SPAN), LOW)
        query = weight[:, pl.ds(pl.multiple_of(SPAN * j, SPAN), SPAN)]
        out[:SHARD, :SPAN] = jnp.where(valid, query, none)
        key = weight[:, pl.ds(pl.multiple_of(WIDTH - 64 + SPAN * j, SPAN), SPAN + 128)]
        out[:SHARD, SPAN : 2 * SPAN] = jnp.where(valid, key[:, 64 : 64 + SPAN], none)

        @pl.when(j < 6)
        def _():
            start = pl.multiple_of(2 * WIDTH + SPAN * j, 128)
            out[:SHARD, 2 * SPAN :] = weight[:, pl.ds(start, SPAN)]

        @pl.when(j >= 6)
        def _():
            out[:SHARD, 2 * SPAN :] = none

        @pl.when(j == 6)
        def _():
            out[:SHARD, 2 * SPAN : 2 * SPAN + 64] = weight[:, 3 * WIDTH - 64 :]

        out[SHARD:, :] = jnp.zeros((CARRY - SHARD, 3 * SPAN), LOW)
        for i, vector in enumerate(vectors[:8]):
            out[SHARD + i : SHARD + i + 1, :SHARD] = vector[...].reshape(1, SHARD)
        for i in range(4):
            part = vectors[8][SHARD * i : SHARD * (i + 1)]
            out[SHARD + i : SHARD + i + 1, BLOCK : BLOCK + SHARD] = part.reshape(1, SHARD)


def prepare_rest_kernel(at, fc, outer, out_half, *outs):
    pad = jnp.zeros((CARRY - SHARD, FF_PART), LOW)
    for half in range(2):

        @pl.when(at[CORE] == half)
        def _():
            out_half[:SHARD, :] = outer[:, FF_PART * half : FF_PART * (half + 1)]

    out_half[SHARD:, :] = pad
    for r in range(4):
        start, shift = FF_PART * r // 128 * 128, FF_PART * r % 128
        start = pl.multiple_of(at[CORE] * (4 * FF_PART) + start, 128)
        part = fc[:, pl.ds(start, 896)][:, shift : shift + FF_PART]
        for d, out in enumerate(outs):

            @pl.when((at[Z] ^ d) == r)
            def _():
                out[:SHARD, :] = part
                out[SHARD:, :] = pad


def normalize(inputs):
    average = jnp.mean(inputs, axis=-1, keepdims=True)
    centred = inputs - average
    spread = jnp.mean(centred * centred, axis=-1, keepdims=True)
    inverse = lax.rsqrt(spread + EPSILON)
    return centred * inverse, inverse


def norm_back(d_normed, hat, inverse, gain):
    e = d_normed * gain
    return inverse * (
        e
        - jnp.mean(e, axis=-1, keepdims=True)
        - hat * jnp.mean(e * hat, axis=-1, keepdims=True)
    )


def load(pairs, sems):
    copies = [pltpu.make_async_copy(f, t, sems.at[i]) for i, (f, t) in enumerate(pairs)]
    for copy in copies:
        copy.start()
    return copies


def weight_pairs(pieces, target):
    pairs, k = [], 0
    for piece in pieces:
        for one in [piece] if len(piece.shape) == 2 else [piece.at[0], piece.at[1]]:
            pairs.append((one, target.at[k, pl.ds(0, CARRY)]))
            k += 1
    return pairs


def clear_pad(target):
    target[:, CARRY:, :] = jnp.zeros((8, BLOCK - CARRY, target.shape[2]), LOW)


def first_kernel(at, *refs):
    token_refs, weight_refs, refs = refs[:8], refs[8:12], refs[12:]
    normed, qkv, vectors, fc_bias, tokens, weight, wide, blocks, spread, *sems = refs
    step = pl.program_id(0)

    def token_copy(k):
        target = tokens.at[k ^ at[MEMBER]]
        return pltpu.make_async_copy(token_refs[k], target, sems[1].at[k])

    @pl.when(step == 0)
    def _():
        for k in range(8):
            token_copy(k).start()
        copies = load(weight_pairs(weight_refs, weight), sems[0])
        clear_pad(weight)
        spread[...] = jnp.zeros_like(spread)
        wide[:, WIDTH:] = jnp.zeros((wide.shape[0], wide.shape[1] - WIDTH), LOW)
        for copy in copies:
            copy.wait()
        for k in range(8):
            block = weight[k ^ at[ME], SHARD:CARRY, :BLOCK].astype(WIDE)
            spread[:, SHARD * k : SHARD * (k + 1)] = block[:, :SHARD]
        vectors[...] = spread[:, :WIDTH]
        rows = weight[(at[CORE] ^ at[YL]) * 4, SHARD:CARRY, BLOCK : 2 * BLOCK].astype(WIDE)
        for i in range(4):
            fc_bias[:, SHARD * i : SHARD * (i + 1)] = rows[i : i + 1, :SHARD]
        for k in range(8):
            token_copy(k).wait()

    rows = tokens[pl.ds(step * 2, 2)].reshape(2 * ROWS, WIDTH)
    hat, _ = normalize(rows.astype(WIDE))
    low = (hat * spread[0:1, :WIDTH] + spread[1:2, :WIDTH]).astype(LOW)
    normed[...] = low
    wide[:, :WIDTH] = low

    def write(k, block):
        blocks[:, block_at(k)] = block

    to_blocks(wide, at[ME], write)
    heads = pl.ds(pl.multiple_of(SPAN * at[MEMBER], SPAN), SPAN)
    total = jnp.dot(
        blocks[...], weight[...].reshape(8 * BLOCK, 3 * SPAN), preferred_element_type=WIDE
    )
    qkv[:, :SPAN] = (total[:, :SPAN] + spread[2:3, heads]).astype(LOW)
    qkv[:, SPAN : 2 * SPAN] = total[:, SPAN : 2 * SPAN].astype(LOW)
    qkv[:, 2 * SPAN :] = (total[:, 2 * SPAN :] + spread[3:4, heads]).astype(LOW)


Q_ROWS = 256


def first(at, tokens, weight):
    rows = 8 * ROWS
    still = lambda i: (0, 0)
    down = lambda i: (i, 0)
    return pl.pallas_call(
        first_kernel,
        grid=(rows // Q_ROWS,),
        in_specs=[SMEM] + [ANY] * 12,
        out_specs=[
            pl.BlockSpec((Q_ROWS, WIDTH), down),
            pl.BlockSpec((Q_ROWS, 3 * SPAN), down),
            pl.BlockSpec((8, WIDTH), still),
            pl.BlockSpec((1, FF_PART), still),
        ],
        out_shape=[
            like((rows, WIDTH)),
            like((rows, 3 * SPAN)),
            like((8, WIDTH), WIDE),
            like((1, FF_PART), WIDE),
        ],
        scratch_shapes=[
            pltpu.VMEM((8, ROWS, WIDTH), LOW),
            pltpu.VMEM((8, BLOCK, 3 * SPAN), LOW),
            pltpu.VMEM((Q_ROWS, WIDTH + 192), LOW),
            pltpu.VMEM((Q_ROWS, 8 * BLOCK), LOW),
            pltpu.VMEM((8, 8 * BLOCK), WIDE),
            pltpu.SemaphoreType.DMA((8,)),
            pltpu.SemaphoreType.DMA((8,)),
        ],
        compiler_params=pltpu.CompilerParams(vmem_limit_bytes=VMEM_LIMIT),
        cost_estimate=cost(0),
        name="first_norm_qkv",
    )(at, *tokens, *weight)


def visible(lengths, first_row, rows, keys):
    row = first_row + lax.broadcasted_iota(jnp.int32, (rows, 1), 0)
    key = lax.broadcasted_iota(jnp.int32, (1, keys), 1)
    start = jnp.zeros_like(row)
    bound = 0
    for i in range(3):
        bound = bound + lengths[0, i]
        start = jnp.where(row >= bound, bound, start)
    return (key <= row) & (key >= start)


ACROSS = (((1,), (1,)), ((), ()))


def by_block(body):
    for i in range(8 * ROWS // Q_ROWS):
        pl.when(pl.program_id(0) == i)(lambda i=i: body(i))


def slot_rows(at, chunk):
    return pl.ds(pl.multiple_of((chunk ^ at[MEMBER]) * ROWS, ROWS), ROWS)


def attend_kernel(at, lengths, q_ref, k_ref, v_ref, mixed_ref, logsum_ref):
    def block(i):
        keys = Q_ROWS * (i + 1)
        q, k, v = q_ref[...], k_ref[:keys, :], v_ref[:keys, :]
        allowed = visible(lengths, i * Q_ROWS, Q_ROWS, keys)
        lane = lax.broadcasted_iota(jnp.int32, q.shape, 1) // HEAD_DIM
        slim = lax.broadcasted_iota(jnp.int32, logsum_ref.shape, 1)
        mixed = jnp.zeros(q.shape, WIDE)
        logsums = jnp.zeros(logsum_ref.shape, WIDE)
        for head in range(TEAM_HEADS):
            own = lane == head
            q_own = jnp.where(own, q, jnp.zeros_like(q))
            scores = lax.dot_general(q_own, k, ACROSS, preferred_element_type=WIDE)
            scores = jnp.where(allowed, scores * (HEAD_DIM**-0.5), -1e30)
            top = jnp.max(scores, axis=-1, keepdims=True)
            powers = jnp.exp(scores - top)
            total = jnp.sum(powers, axis=-1, keepdims=True)
            probs = (powers * (1.0 / total)).astype(LOW)
            mixed = jnp.where(own, jnp.dot(probs, v, preferred_element_type=WIDE), mixed)
            logsums = jnp.where(slim == head, top + jnp.log(total), logsums)
        low = mixed.astype(LOW)
        for half in range(Q_ROWS // ROWS):
            rows = slot_rows(at, i * (Q_ROWS // ROWS) + half)
            mixed_ref[rows, :] = low[ROWS * half : ROWS * (half + 1)]
        logsum_ref[...] = logsums

    by_block(block)


def attend_back_kernel(
    at, lengths, q_ref, k_ref, v_ref, logsum_ref, dmix_ref, out_ref, dk_total, dv_total
):
    scale = HEAD_DIM**-0.5

    def block(i):
        keys = Q_ROWS * (i + 1)
        if i == 0:
            dk_total[...] = jnp.zeros_like(dk_total)
            dv_total[...] = jnp.zeros_like(dv_total)
        q, k, v = q_ref[...], k_ref[:keys, :], v_ref[:keys, :]
        count = Q_ROWS // ROWS
        dmix = jnp.concatenate([dmix_ref[slot_rows(at, i * count + n), :] for n in range(count)])
        allowed = visible(lengths, i * Q_ROWS, Q_ROWS, keys)
        lane = lax.broadcasted_iota(jnp.int32, q.shape, 1) // HEAD_DIM
        dq = jnp.zeros(q.shape, WIDE)
        for head in range(TEAM_HEADS):
            own = lane == head
            q_own = jnp.where(own, q, jnp.zeros_like(q))
            dmix_own = jnp.where(own, dmix, jnp.zeros_like(dmix))
            scores = lax.dot_general(q_own, k, ACROSS, preferred_element_type=WIDE) * scale
            scores = jnp.where(allowed, scores, -1e30)
            probs = jnp.exp(scores - logsum_ref[:, head : head + 1])
            d_probs = lax.dot_general(dmix_own, v, ACROSS, preferred_element_type=WIDE)
            term = jnp.sum(probs * d_probs, axis=-1, keepdims=True)
            d_scores = (probs * (d_probs - term)).astype(LOW)
            dq = jnp.where(own, jnp.dot(d_scores, k, preferred_element_type=WIDE), dq)
            dk_total[:keys, :] += lax.dot_general(
                d_scores, q_own, DOWN, preferred_element_type=WIDE
            )
            dv_total[:keys, :] += lax.dot_general(
                probs.astype(LOW), dmix_own, DOWN, preferred_element_type=WIDE
            )
        out_ref[Q_ROWS * i : Q_ROWS * (i + 1), :SPAN] = (dq * scale).astype(LOW)
        if i == 8 * ROWS // Q_ROWS - 1:
            out_ref[:, SPAN : 2 * SPAN] = (dk_total[...] * scale).astype(LOW)
            out_ref[:, 2 * SPAN :] = dv_total[...].astype(LOW)

    by_block(block)


def attend_specs(rows):
    return [
        SMEM,
        SMEM,
        pl.BlockSpec((Q_ROWS, SPAN), lambda i: (i, 0)),
        pl.BlockSpec((rows, SPAN), lambda i: (0, 1)),
        pl.BlockSpec((rows, SPAN), lambda i: (0, 2)),
    ]


def attend(places, qkv):
    rows = qkv.shape[0]
    return pl.pallas_call(
        attend_kernel,
        grid=(rows // Q_ROWS,),
        in_specs=attend_specs(rows),
        out_specs=[
            pl.BlockSpec((rows, SPAN), lambda i: (0, 0)),
            pl.BlockSpec((Q_ROWS, 128), lambda i: (i, 0)),
        ],
        out_shape=[
            jax.ShapeDtypeStruct((rows, SPAN), LOW),
            jax.ShapeDtypeStruct((rows, 128), WIDE),
        ],
        compiler_params=pltpu.CompilerParams(vmem_limit_bytes=VMEM_LIMIT),
        cost_estimate=cost(0),
        name="attend",
    )(*places, qkv, qkv, qkv)


def attend_back(places, qkv, logsum, dmix):
    rows = qkv.shape[0]
    whole = lambda i: (0, 0)
    return pl.pallas_call(
        attend_back_kernel,
        grid=(rows // Q_ROWS,),
        in_specs=attend_specs(rows)
        + [pl.BlockSpec((Q_ROWS, 128), lambda i: (i, 0)), pl.BlockSpec((rows, SPAN), whole)],
        out_specs=pl.BlockSpec((rows, 3 * SPAN), whole),
        out_shape=like((rows, 3 * SPAN)),
        scratch_shapes=[pltpu.VMEM((rows, SPAN), WIDE)] * 2,
        compiler_params=pltpu.CompilerParams(vmem_limit_bytes=VMEM_LIMIT),
        cost_estimate=cost(0),
        name="attend_back",
    )(*places, qkv, qkv, qkv, logsum, dmix)


def middle_kernel(at, tokens, vectors, *refs):
    pieces, mine_refs, other_refs, refs = refs[:4], refs[4:8], refs[8:12], refs[12:]
    middle, normed, mixed_out, mixed, blocks, wide, mine, other, *sems = refs
    copies = load(weight_pairs(mine_refs, mine), sems[0])
    copies += load(weight_pairs(other_refs, other), sems[1])
    clear_pad(mine)
    clear_pad(other)
    for d, piece in enumerate(pieces):
        mixed[:, block_at(d ^ at[MEMBER])] = piece[:, :SPAN]
        mixed[:, block_at((4 + d) ^ at[MEMBER])] = piece[:, SPAN:]

    def write_blocks(k, block):
        blocks[:, block_at(k)] = block

    to_blocks(mixed, at[ME], write_blocks)
    mixed_out[...] = mixed[:, :WIDTH]
    for copy in copies:
        copy.wait()
    flat = (8 * BLOCK, FF_PART)
    a = jnp.dot(blocks[...], mine[...].reshape(flat), preferred_element_type=WIDE)
    b = jnp.dot(blocks[...], other[...].reshape(flat), preferred_element_type=WIDE)
    wide[:, :FF_PART] = jnp.where(at[CORE] == 0, a, b)
    wide[:, FF_PART:] = jnp.where(at[CORE] == 0, b, a)
    total = tokens[...].astype(WIDE) + wide[...] + vectors[4:5, :]
    middle[...] = total
    hat, _ = normalize(total)
    normed[...] = (hat * vectors[5:6, :] + vectors[6:7, :]).astype(LOW)


OUT_WEIGHT_SCRATCH = [
    pltpu.VMEM((8, BLOCK, FF_PART), LOW),
    pltpu.VMEM((8, BLOCK, FF_PART), LOW),
    pltpu.SemaphoreType.DMA((8,)),
    pltpu.SemaphoreType.DMA((8,)),
]


def proj_pairs(own, first_half, second_half, target):
    rows = FF_PART // 2
    return (
        [(own.at[pl.ds(0, rows)], target.at[pl.ds(0, rows)]), (own.at[pl.ds(rows, rows)], target.at[pl.ds(rows, rows)])],
        [(first_half, target.at[pl.ds(0, rows)]), (second_half, target.at[pl.ds(rows, rows)])],
    )


def load_proj(at, refs, target, sems):
    own, got = proj_pairs(*refs, target)

    @pl.when(at[CORE] == at[YL])
    def _():
        for copy in load(own, sems):
            copy.wait()

    @pl.when(at[CORE] != at[YL])
    def _():
        for copy in load(got, sems):
            copy.wait()


def halves(i):
    return jnp.minimum(i, 1), 0


def late_halves(i):
    return jnp.maximum(i - 2, 0), 0


def write_half(step, near, far, value):
    @pl.when(step < 2)
    def _():
        near[:, :WIDTH] = value
        near[:, WIDTH:] = jnp.zeros((value.shape[0], LANES - WIDTH), LOW)

    @pl.when(step >= 2)
    def _():
        far[:, :WIDTH] = value
        far[:, WIDTH:] = jnp.zeros((value.shape[0], LANES - WIDTH), LOW)


def feed_kernel(at, bias, *refs):
    cot_refs, normed_refs, fc_refs, proj_refs = refs[:8], refs[8:16], refs[16:20], refs[20:23]
    hidden, d_in, near, far, bias_sum, normed, cot, fc, proj, wide, blocks, tall, back, *sems = (
        refs[23:]
    )
    step = pl.program_id(0)

    def normed_copy(k):
        return pltpu.make_async_copy(normed_refs[k], normed.at[k], sems[0].at[k])

    def cot_copy(k):
        return pltpu.make_async_copy(cot_refs[k], cot.at[k], sems[3].at[k])

    own, got = proj_pairs(*proj_refs, proj)
    diagonal = at[CORE] == at[YL]

    def proj_copy(i):
        return pltpu.make_async_copy(got[i][0], got[i][1], sems[2].at[i])

    @pl.when(step == 0)
    def _():
        for k in range(2):
            normed_copy(k).start()
        copies = load(weight_pairs(fc_refs, fc), sems[1])
        clear_pad(fc)
        bias_sum[...] = jnp.zeros_like(bias_sum)
        wide[:, WIDTH:] = jnp.zeros((2 * ROWS, wide.shape[1] - WIDTH), LOW)
        for copy in copies:
            copy.wait()
        for k in range(2):
            cot_copy(k).start()

        @pl.when(diagonal)
        def _():
            load(own, sems[2])

        @pl.when(jnp.logical_not(diagonal))
        def _():
            load(got, sems[2])

    for k in range(8):

        @pl.when(step == k // 2)
        def _():
            normed_copy(k).wait()

        @pl.when(step + 1 == k // 2)
        def _():
            normed_copy(k).start()
            cot_copy(k).start()

    wide[:, :WIDTH] = normed[pl.ds(step * 2, 2)].reshape(2 * ROWS, WIDTH)

    def write(k, block):
        blocks[:, block_at(k)] = block

    to_blocks(wide, at[ME], write)
    weight = fc[...].reshape(8 * BLOCK, FF_PART)
    u = jnp.dot(blocks[...], weight, preferred_element_type=WIDE) + bias[...]
    for k in range(8):

        @pl.when(step == k // 2)
        def _():
            cot_copy(k).wait()

    @pl.when(step == 0)
    def _():
        proj_copy(0).wait()
        proj_copy(1).wait()

    cot_rows = cot[pl.ds(step * 2, 2)].reshape(2 * ROWS, WIDTH)
    d_hidden = lax.dot_general(cot_rows, proj[...], ACROSS, preferred_element_type=WIDE)
    factor = (2.0 / jnp.pi) ** 0.5
    square = u * u
    bent = jnp.tanh(factor * (u + 0.044715 * (square * u)))
    half = 0.5 * (1.0 + bent)
    hidden[...] = (u * half).astype(LOW)
    slope = half + (0.5 * factor) * u * (1.0 - bent * bent) * (1.0 + (3 * 0.044715) * square)
    low = (d_hidden * slope).astype(LOW)
    d_in[...] = low
    bias_sum[...] += jnp.sum(low.astype(WIDE), axis=0, keepdims=True)
    tall[...] = lax.dot_general(low, weight, ACROSS, preferred_element_type=WIDE).astype(LOW)
    from_blocks(tall, at[ME], back)
    write_half(step, near, far, back[...])


def feed(at, normed, cot, fc, proj, bias):
    rows = 8 * ROWS
    still = lambda i: (0, 0)
    down = lambda i: (i, 0)
    return pl.pallas_call(
        feed_kernel,
        grid=(rows // Q_ROWS,),
        in_specs=[SMEM, pl.BlockSpec((1, FF_PART), still)] + [ANY] * 23,
        out_specs=[
            pl.BlockSpec((Q_ROWS, FF_PART), down),
            pl.BlockSpec((Q_ROWS, FF_PART), down),
            pl.BlockSpec((Q_ROWS, LANES), halves),
            pl.BlockSpec((Q_ROWS, LANES), late_halves),
            pl.BlockSpec((1, FF_PART), still),
        ],
        out_shape=[
            like((rows, FF_PART)),
            like((rows, FF_PART)),
            like((rows // 2, LANES)),
            like((rows // 2, LANES)),
            like((1, FF_PART), WIDE),
        ],
        scratch_shapes=[
            pltpu.VMEM((8, ROWS, WIDTH), LOW),
            pltpu.VMEM((8, ROWS, WIDTH), LOW),
            pltpu.VMEM((8, BLOCK, FF_PART), LOW),
            pltpu.VMEM((FF_PART, WIDTH), LOW),
            pltpu.VMEM((Q_ROWS, WIDTH + 192), LOW),
            pltpu.VMEM((Q_ROWS, 8 * BLOCK), LOW),
            pltpu.VMEM((Q_ROWS, 8 * BLOCK), LOW),
            pltpu.VMEM((Q_ROWS, WIDTH), LOW),
            pltpu.SemaphoreType.DMA((8,)),
            pltpu.SemaphoreType.DMA((8,)),
            pltpu.SemaphoreType.DMA((2,)),
            pltpu.SemaphoreType.DMA((8,)),
        ],
        compiler_params=pltpu.CompilerParams(vmem_limit_bytes=VMEM_LIMIT),
        cost_estimate=cost(0),
        name="feed_forward_and_back",
    )(at, bias, *cot, *normed, *fc, *proj)


def final_kernel(at, hidden, *refs):
    proj_refs, (near, far, proj, sems) = refs[:3], refs[3:]
    step = pl.program_id(0)

    @pl.when(step == 0)
    def _():
        load_proj(at, proj_refs, proj, sems)

    total = jnp.dot(hidden[...], proj[...], preferred_element_type=WIDE).astype(LOW)
    write_half(step, near, far, total)


def final_part(at, hidden, proj):
    rows = hidden.shape[0]
    return pl.pallas_call(
        final_kernel,
        grid=(rows // Q_ROWS,),
        in_specs=[SMEM, pl.BlockSpec((Q_ROWS, FF_PART), lambda i: (i, 0))] + [ANY] * 3,
        out_specs=[
            pl.BlockSpec((Q_ROWS, LANES), halves),
            pl.BlockSpec((Q_ROWS, LANES), late_halves),
        ],
        out_shape=[like((rows // 2, LANES))] * 2,
        scratch_shapes=[pltpu.VMEM((FF_PART, WIDTH), LOW), pltpu.SemaphoreType.DMA((2,))],
        compiler_params=pltpu.CompilerParams(vmem_limit_bytes=VMEM_LIMIT),
        cost_estimate=cost(0),
        name="feed_forward_out",
    )(at, hidden, *proj)


def padded_rows():
    return pl.BlockSpec((ROWS, LANES), lambda i: (0, 0))


def team_total(refs):
    total = refs[0][:, :WIDTH].astype(WIDE)
    for ref in refs[1:]:
        total = total + ref[:, :WIDTH].astype(WIDE)
    return total


def row_sum(value):
    return jnp.sum(value, axis=0, keepdims=True)


def output_kernel(middle, vectors, near, got, one, two, three, out):
    total = middle[...] + vectors[7:8, :]
    out[...] = (total + team_total([near, got, one, two, three])).astype(LOW)


def output_rows(middle, vectors, parts):
    part = pl.BlockSpec((ROWS, WIDTH), lambda i: (0, 0))
    return pl.pallas_call(
        output_kernel,
        grid=(1,),
        in_specs=[part, pl.BlockSpec((8, WIDTH), lambda i: (0, 0))] + [padded_rows()] * 5,
        out_specs=part,
        out_shape=like((ROWS, WIDTH)),
        compiler_params=pltpu.CompilerParams(vmem_limit_bytes=SMALL_LIMIT),
        cost_estimate=cost(0),
        name="output_rows",
    )(middle, vectors, *parts)


def out_grad_kernel(at, left, left_other, right, right_other, *refs):
    outs, total = refs[:4], refs[4]
    first_core = at[CORE] == 0

    def half(ref):
        value = ref[...]
        return jnp.where(first_core, value[:, :FF_PART], value[:, FF_PART:])

    total[:FF_PART, :] = lax.dot_general(
        jnp.concatenate([half(left), half(left_other)]),
        jnp.concatenate([right[...], right_other[...]]),
        DOWN,
        preferred_element_type=WIDE,
    )
    for d, out in enumerate(outs):
        start = pl.multiple_of((at[Z] ^ d) * SHARD, 8)
        out[...] = total[pl.ds(start, CARRY), :].astype(LOW)


def out_grad(at, left, left_other, right, right_other):
    return whole_call(
        out_grad_kernel,
        "out_grad",
        [like((CARRY, WIDTH))] * 4,
        at,
        left,
        left_other,
        right,
        right_other,
        scratch=[pltpu.VMEM((FF_PART + CARRY - SHARD, WIDTH), WIDE)],
        limit=VMEM_LIMIT,
    )


def out_sum_kernel(at, own, one, two, three, *refs):
    outs, total = refs[:4], refs[4]
    total[...] = team_total([own, one, two, three])
    for d, out in enumerate(outs):
        start = pl.multiple_of((at[X] ^ d) * PIECE_STEP, 8)
        piece = total[pl.ds(start, PIECE), :].astype(LOW)
        out[0] = piece[:, :FF_PART]
        out[1] = piece[:, FF_PART:]


def second_back_kernel(at, middle, cot, vectors, near, got, *refs):
    parts, mine_refs, other_refs, refs = refs[:3], refs[3:7], refs[7:11], refs[11:]
    (d_middle, d_branch, sums), pieces, refs = refs[:3], refs[3:7], refs[7:]
    wide, tall, narrow, mine, other, *sems = refs
    copies = load(weight_pairs(mine_refs, mine), sems[0])
    copies += load(weight_pairs(other_refs, other), sems[1])
    clear_pad(mine)
    clear_pad(other)
    d_second = team_total([near, got, *parts])
    hat, inverse = normalize(middle[...])
    d_cot = cot[...].astype(WIDE)
    total = d_cot + norm_back(d_second, hat, inverse, vectors[5:6, :])
    d_middle[...] = total
    low = total.astype(LOW)
    d_branch[...] = low
    sums[0:1, :] = row_sum(d_second * hat)
    sums[1:2, :] = row_sum(d_second)
    sums[2:3, :] = row_sum(low.astype(WIDE))
    sums[3:4, :] = row_sum(d_cot)
    sums[4:8, :] = jnp.zeros((4, WIDTH), WIDE)
    wide[...] = low
    left, right = wide[:, :FF_PART], wide[:, FF_PART:]
    first_core = at[CORE] == 0
    flat = (8 * BLOCK, FF_PART)
    across = (((1,), (1,)), ((), ()))
    for copy in copies:
        copy.wait()
    tall[...] = lax.dot_general(
        jnp.where(first_core, left, right),
        mine[...].reshape(flat),
        across,
        preferred_element_type=WIDE,
    ) + lax.dot_general(
        jnp.where(first_core, right, left),
        other[...].reshape(flat),
        across,
        preferred_element_type=WIDE,
    )
    narrow[:, WIDTH:] = jnp.zeros((ROWS, 8 * SPAN - WIDTH), LOW)
    from_blocks(tall, at[ME], narrow)
    for d, piece in enumerate(pieces):
        piece[:, :SPAN] = narrow[:, block_at(d ^ at[MEMBER])]
        piece[:, SPAN:] = narrow[:, block_at((4 + d) ^ at[MEMBER])]


def second_back(at, middle, cot, vectors, near, got, parts, mine, other):
    part = pl.BlockSpec((ROWS, WIDTH), lambda i: (0, 0))
    return pl.pallas_call(
        second_back_kernel,
        grid=(1,),
        in_specs=[SMEM, part, part, pl.BlockSpec((8, WIDTH), lambda i: (0, 0))]
        + [padded_rows()] * 5
        + [ANY] * 8,
        out_specs=[VMEM] * 7,
        out_shape=[like((ROWS, WIDTH), WIDE), like((ROWS, WIDTH)), like((8, WIDTH), WIDE)]
        + [like((ROWS, 2 * SPAN))] * 4,
        scratch_shapes=[
            pltpu.VMEM((ROWS, WIDTH), LOW),
            pltpu.VMEM((ROWS, 8 * BLOCK), WIDE),
            pltpu.VMEM((ROWS, 8 * SPAN), LOW),
        ]
        + OUT_WEIGHT_SCRATCH,
        compiler_params=pltpu.CompilerParams(vmem_limit_bytes=VMEM_LIMIT),
        cost_estimate=cost(0),
        name="second_norm_and_out_back",
    )(at, middle, cot, vectors, near, got, *parts, *mine, *other)


def first_back_kernel(at, d_qkv, *refs):
    weight_refs, (near, far, sums, weight, tall, back, sems) = refs[:4], refs[4:]
    step = pl.program_id(0)

    @pl.when(step == 0)
    def _():
        copies = load(weight_pairs(weight_refs, weight), sems)
        clear_pad(weight)
        sums[...] = row_sum(d_qkv[...].astype(WIDE))
        for copy in copies:
            copy.wait()

    rows = jnp.concatenate([d_qkv[slot_rows(at, 2 * step + n), :] for n in range(2)])
    tall[...] = lax.dot_general(
        rows, weight[...].reshape(8 * BLOCK, 3 * SPAN), ACROSS, preferred_element_type=WIDE
    ).astype(LOW)
    from_blocks(tall, at[ME], back)
    write_half(step, near, far, back[...])


def first_back(at, d_qkv, weight):
    rows = d_qkv.shape[0]
    whole = lambda i: (0, 0)
    return pl.pallas_call(
        first_back_kernel,
        grid=(rows // Q_ROWS,),
        in_specs=[SMEM, pl.BlockSpec((rows, 3 * SPAN), whole)] + [ANY] * 4,
        out_specs=[
            pl.BlockSpec((Q_ROWS, LANES), halves),
            pl.BlockSpec((Q_ROWS, LANES), late_halves),
            pl.BlockSpec((1, 3 * SPAN), whole),
        ],
        out_shape=[
            like((rows // 2, LANES)),
            like((rows // 2, LANES)),
            like((1, 3 * SPAN), WIDE),
        ],
        scratch_shapes=[
            pltpu.VMEM((8, BLOCK, 3 * SPAN), LOW),
            pltpu.VMEM((Q_ROWS, 8 * BLOCK), LOW),
            pltpu.VMEM((Q_ROWS, WIDTH), LOW),
            pltpu.SemaphoreType.DMA((8,)),
        ],
        compiler_params=pltpu.CompilerParams(vmem_limit_bytes=VMEM_LIMIT),
        cost_estimate=cost(0),
        name="qkv_back",
    )(at, d_qkv, *weight)


SUMS = (PIECE, FF_PART)


def input_kernel(at, tokens, d_middle, vectors, second_sums, fc_sum, qkv_sum, *refs):
    parts, (grad, sums, held) = refs[:5], refs[5:]
    d_first = team_total(parts)
    hat, inverse = normalize(tokens[...].astype(WIDE))
    grad[...] = (d_middle[...] + norm_back(d_first, hat, inverse, vectors[0:1, :])).astype(LOW)
    held[...] = jnp.zeros(SUMS, WIDE)
    rows = [row_sum(d_first * hat), row_sum(d_first)] + [second_sums[i : i + 1, :] for i in range(4)]
    for i, row in enumerate(rows):
        held[2 * i : 2 * i + 1, :] = row[:, :FF_PART]
        held[2 * i + 1 : 2 * i + 2, :] = row[:, FF_PART:]
    held[pl.ds(16 + at[MEMBER], 1), :] = fc_sum[...]
    held[pl.ds(24 + at[MEMBER], 1), :SPAN] = qkv_sum[:, :SPAN]
    held[pl.ds(32 + at[MEMBER], 1), :SPAN] = qkv_sum[:, 2 * SPAN :]
    sums[0] = held[...].astype(LOW)


def input_back(at, tokens, d_middle, vectors, second_sums, fc_sum, qkv_sum, parts):
    still = lambda i: (0, 0)
    part = pl.BlockSpec((ROWS, WIDTH), still)
    rows = pl.BlockSpec((8, WIDTH), still)
    return pl.pallas_call(
        input_kernel,
        grid=(1,),
        in_specs=[
            SMEM,
            part,
            part,
            rows,
            rows,
            pl.BlockSpec((1, FF_PART), still),
            pl.BlockSpec((1, 3 * SPAN), still),
        ]
        + [padded_rows()] * 5,
        out_specs=[part, pl.BlockSpec((1,) + SUMS, lambda i: (0, 0, 0))],
        out_shape=[like((ROWS, WIDTH)), like((1,) + SUMS)],
        scratch_shapes=[pltpu.VMEM(SUMS, WIDE)],
        compiler_params=pltpu.CompilerParams(vmem_limit_bytes=SMALL_LIMIT),
        cost_estimate=cost(0),
        name="first_norm_back",
    )(at, tokens, d_middle, vectors, second_sums, fc_sum, qkv_sum, *parts)


def feed_grad_kernel(at, hidden, d_in, *refs):
    cot_refs, normed_refs, (out, normed, cot, total, tall, *sems) = refs[:8], refs[8:16], refs[16:]
    pairs = [(normed_refs[k], normed.at[k]) for k in range(8)]
    first_copies = load(pairs, sems[0])
    pairs = [(cot_refs[k], cot.at[k]) for k in range(8)]
    second_copies = load(pairs, sems[1])
    for copy in first_copies:
        copy.wait()
    total[...] = lax.dot_general(
        normed[...].reshape(8 * ROWS, WIDTH), d_in[...], DOWN, preferred_element_type=WIDE
    )
    for k in range(8):
        for q in range(4):
            start = pl.multiple_of((k ^ at[ME]) * SHARD + PIECE_STEP * q, 8)
            out[16 * q + k] = total[pl.ds(start, PIECE), :].astype(LOW)
    for copy in second_copies:
        copy.wait()
    tall[...] = lax.dot_general(
        hidden[...], cot[...].reshape(8 * ROWS, WIDTH), DOWN, preferred_element_type=WIDE
    )
    for q in range(4):
        for half in range(2):
            lanes = slice(FF_PART * half, FF_PART * (half + 1))
            for k in range(4):
                start = SHARD * q + PIECE_STEP * k
                out[16 * q + 8 + 4 * half + k] = tall[start : start + PIECE, lanes].astype(LOW)


def feed_grad(at, normed, d_in, hidden, cot):
    rows = 8 * ROWS
    return pl.pallas_call(
        feed_grad_kernel,
        in_specs=[SMEM, VMEM, VMEM] + [ANY] * 16,
        out_specs=VMEM,
        out_shape=like((64, PIECE, FF_PART)),
        scratch_shapes=[
            pltpu.VMEM((8, ROWS, WIDTH), LOW),
            pltpu.VMEM((8, ROWS, WIDTH), LOW),
            pltpu.VMEM((WIDTH, FF_PART), WIDE),
            pltpu.VMEM((FF_PART, WIDTH), WIDE),
            pltpu.SemaphoreType.DMA((8,)),
            pltpu.SemaphoreType.DMA((8,)),
        ],
        compiler_params=pltpu.CompilerParams(vmem_limit_bytes=VMEM_LIMIT),
        cost_estimate=cost(0),
        name="feed_forward_grad",
    )(at, hidden, d_in, *cot, *normed)


def qkv_grad_kernel(at, normed, d_qkv, *refs):
    outs, total = refs[:4], refs[4]
    total[:, 3 * SPAN :] = jnp.zeros((WIDTH, FF_PART - 3 * SPAN), WIDE)
    total[:, : 3 * SPAN] = lax.dot_general(
        normed[...], d_qkv[...], DOWN, preferred_element_type=WIDE
    )
    for d, out in enumerate(outs):
        place = pl.multiple_of((at[X] ^ d) * PIECE_STEP, 8)
        for k in range(8):
            start = pl.multiple_of((k ^ at[ME]) * SHARD + place, 8)
            out[k] = total[pl.ds(start, PIECE), :].astype(LOW)


def added(refs, k):
    total = refs[0][k].astype(WIDE)
    for ref in refs[1:]:
        total = total + ref[k].astype(WIDE)
    return total.astype(LOW)


def feed_mid_kernel(at, total, half_got, keep, give_fc, give_proj):
    own = at[CORE] == at[YL]
    keep[:4] = total[:4]
    give_fc[...] = total[4:8]
    mine, other = total[pl.ds(8 + 4 * at[CORE], 4)], half_got[...]
    keep[4:] = jnp.where(own, mine, other)
    give_proj[...] = jnp.where(own, other, mine)


def add_halves_kernel(at, keep, first_half, second_half, out):
    count = first_half.shape[0]
    for k in range(keep.shape[0]):
        half = (first_half, k) if k < count else (second_half, k - count)
        out[k] = (keep[k].astype(WIDE) + half[0][half[1]].astype(WIDE)).astype(LOW)


def split_sum_kernel(at, one, two, *outs):
    place = 0
    for out in outs:
        for k in range(out.shape[0]):
            out[k] = added((one, two), place)
            place += 1


def qkv_x_kernel(at, *refs):
    parts, out_parts, sums, (keep, give_one, give_two) = refs[:4], refs[4:8], refs[8], refs[9:]
    for k in range(3):
        keep[k] = added(parts, k)
        give_one[k] = added(parts, 4 + k)
    keep[3] = sums[0]
    give_one[3] = sums[0]
    keep[4] = added(parts, 3)
    give_two[0] = added(parts, 7)
    for k in range(2):
        value = added(out_parts, k)
        keep[5 + k] = value
        give_two[1 + k] = value


def qkv_y_kernel(at, half, last, own, one, two, three, rest, sums):
    pair = (half, last)
    own[0] = added(pair, 0)
    total = added(pair, 3)
    sums[0] = total
    for out, place in ((one, 1), (two, 2), (three, 4)):
        out[0] = added(pair, place)
        out[1] = total
    for k in range(2):
        rest[k] = added(pair, 5 + k)


def qkv_z_kernel(at, own, sums, one, two, three, rest, out):
    out[0] = own[0]
    total = sums[0].astype(WIDE)
    for k, got in enumerate((one, two, three)):
        out[1 + k] = got[0]
        total = total + got[1].astype(WIDE)
    out[4:6] = rest[...]
    out[6] = total.astype(LOW)


def feed_z_kernel(at, own, one, two, three, rest, out):
    for k, got in enumerate((own, one, two, three)):
        out[k] = got[0]
    out[4:] = rest[...]


def place_feed_kernel(at, mine, other, fc, proj):
    for c in range(2):
        for q in range(4):
            count = PIECE_STEP if q < 3 else PIECE

            def block(k):
                return jnp.where(at[CORE] == c, mine[q, k], other[q, k]).astype(WIDE)

            for z in range(4):
                j = c * 4 + z
                fc[PIECE_STEP * q : PIECE_STEP * q + count, FF_PART * j : FF_PART * (j + 1)] = block(
                    z ^ at[Z]
                )[:count]
            for k in range(4):
                rows = PIECE_STEP if k < 3 else PIECE
                row = SHARD * q + PIECE_STEP * k
                proj[row : row + rows, FF_PART * c : FF_PART * (c + 1)] = block(4 + k)[:rows]


def place_qkv_kernel(at, *refs):
    mine, other, (qkv, out), refs = refs[:4], refs[4:8], refs[8:10], refs[10:]
    vectors, held, scratch = refs[:9], refs[9], refs[10:]
    for k in range(4):
        held[0, k] = mine[k][...]
        held[1, k] = other[k][...]
    own = jnp.where(at[CORE] == at[YL], 0, 1)
    for q in range(4):
        count = PIECE_STEP if q < 3 else PIECE
        rows = slice(PIECE_STEP * q, PIECE_STEP * q + count)
        for c in range(2):
            for z in range(4):
                block = held[c ^ at[CORE], q ^ at[X], z ^ at[Z]].astype(WIDE)
                for start, stop, target in qkv_columns(c * 4 + z):
                    qkv[rows, target : target + stop - start] = block[:count, start:stop]
        for half in range(2):
            block = held[own, q ^ at[X], 4 + half].astype(WIDE)
            out[rows, FF_PART * half : FF_PART * (half + 1)] = block[:count]
    total = held[0, 0, 6].astype(WIDE)
    for core in range(2):
        for k in range(4):
            if core + k:
                total = total + held[core, k, 6].astype(WIDE)
    place_vectors(at, total, *vectors, *scratch)


def place_vectors(at, total, *refs):
    outs, (small, joined) = refs[:9], refs[9:]
    small[...] = total
    for i in range(6):
        row = small[pl.ds(2 * i + at[ME] // 4, 1), :]
        for k in range(4):

            @pl.when(at[ME] % 4 == k)
            def _():
                outs[i][...] = row[:, SHARD * k : SHARD * (k + 1)].reshape(SHARD)

    outs[6][...] = small[pl.ds(16 + at[ME], 1), :].reshape(FF_PART)
    for n in range(2):
        for k in range(8):
            at_row = 24 + 8 * n + k
            joined[:, SPAN * k : SPAN * (k + 1)] = small[at_row : at_row + 1, :SPAN]
        for k in range(8):

            @pl.when(at[ME] == k)
            def _():
                outs[7 + n][...] = joined[:, SHARD * k : SHARD * (k + 1)].reshape(SHARD)


def qkv_columns(j):
    count = min(SPAN, WIDTH - SPAN * j)
    if count <= 0:
        return []
    return [(SPAN * p, SPAN * p + count, WIDTH * p + SPAN * j) for p in range(3)]


def gather_rows(block, *gates, late=()):
    beside = c_swap(block)
    sent = after(block, *gates)
    near = {d: z_swap(sent, d) for d in (1, 3, 2)}
    far = {d: c_swap(after(near[d], *late)) for d in (1, 3, 2)}
    return [block, near[1], near[2], near[3], beside, far[1], far[2], far[3]], list(near.values())


def team_parts(near, far, c_gates=(), z_gates=()):
    got = c_swap(after(far, *c_gates))
    pair = [add([v[ROWS * d : ROWS * (d + 1)] for v in (near, got)]) for d in (1, 2, 3)]
    sent = after(pair, *z_gates)
    came = [z_swap(sent[d - 1], d) for d in (1, 3, 2)]
    return [near, got] + came, sent, came


def z_blocks(own, sends, *gates):
    sends = after(sends, *gates)
    near = {d: z_swap(sends[d], d) for d in (1, 3, 2)}
    near[0] = own
    return near


def far_blocks(near, *gates):
    near = after(near, *gates)
    one, two = jnp.stack([near[0], near[1]]), jnp.stack([near[2], near[3]])
    return [one, two, y_swap(one, 1), y_swap(two, 3)]


def spread_x(value, swap):
    got = [swap(value, d) for d in (1, 3)]
    two = swap(after(value, got), 2)
    return [value, got[0], two, got[1]]


def add(values):
    total = values[0].astype(WIDE)
    for value in values[1:]:
        total = total + value.astype(WIDE)
    return total.astype(LOW)


def local(
    tokens,
    lengths,
    ln1_gain,
    ln1_bias,
    qkv_weight,
    q_bias,
    v_bias,
    out_weight,
    out_bias,
    ln2_gain,
    ln2_bias,
    fc_weight,
    fc_bias,
    proj_weight,
    proj_bias,
    cotangent,
):
    c, x, yl, z = (lax.axis_index(a) for a in ("c", "x", "yl", "z"))
    me, member = yl * 4 + z, c * 4 + z
    at = jnp.stack([me, member, c, x, yl, z]).astype(jnp.int32)

    vectors = [ln1_gain, ln1_bias, q_bias, v_bias, out_bias, ln2_gain, ln2_bias, proj_bias, fc_bias]
    own_tokens = turn(tokens)
    qkv_sends = whole_call_any(
        prepare_qkv_kernel,
        "prepare_qkv",
        [like((CARRY, 3 * SPAN))] * 4,
        [at, qkv_weight],
        vectors,
        scratch=[pltpu.VMEM(v.shape, LOW) for v in vectors] + [pltpu.SemaphoreType.DMA((9,))],
    )
    half = proj_weight.shape[0] // 2
    proj_sends = proj_weight[:half], proj_weight[half:]

    out_half, *fc_sends = whole_call(
        prepare_rest_kernel,
        "prepare_rest",
        [like((CARRY, FF_PART))] * 5,
        at,
        after(fc_weight, qkv_sends),
        out_weight,
    )
    all_tokens, tokens_came = gather_rows(own_tokens)
    qkv_near = z_blocks(qkv_sends[0], qkv_sends, own_tokens)
    other_lengths = c_swap(after(lengths, tokens_came[0]))
    places = at, jnp.where(c == yl, lengths, other_lengths)
    weight_qkv = far_blocks(qkv_near, out_half, fc_sends, places, proj_sends)
    own_cotangent = turn(after(cotangent, own_tokens))
    out_near = z_blocks(out_half, [out_half] * 4, qkv_near, all_tokens, own_cotangent)
    proj_sent = after(proj_sends, weight_qkv, out_near)
    proj_pieces = [
        proj_weight,
        y_swap_some(proj_sent[0], 1, True),
        y_swap_some(proj_sent[1], 3, True),
    ]

    normed_first, qkv, vectors_all, fc_bias_own = first(at, all_tokens, after(weight_qkv, out_near))
    all_cotangent, cotangent_came = gather_rows(own_cotangent, out_near, late=(qkv,))
    qkv = after(qkv, cotangent_came, proj_pieces)
    out_mine = far_blocks(out_near, qkv)
    fc_near = z_blocks(fc_sends[0], fc_sends, qkv)
    mixed_heads, logsum = attend(places, qkv)
    mixed_heads = after(mixed_heads, out_mine, fc_near)
    out_other = [c_swap(after(piece, mixed_heads)) for piece in out_mine]

    mixed_near = mixed_heads[: 4 * ROWS]
    mixed_got = after(c_swap(mixed_heads[4 * ROWS :]), out_other)
    mixed_sent = [
        jnp.concatenate([v[ROWS * d : ROWS * (d + 1)] for v in (mixed_near, mixed_got)], axis=1)
        for d in range(4)
    ]
    mixed_pieces = [mixed_sent[0]] + [z_swap(mixed_sent[d], d) for d in (1, 2, 3)]
    middle, normed_second, mixed = whole_call_any(
        middle_kernel,
        "out_and_second_norm",
        [like((ROWS, WIDTH), WIDE), like((ROWS, WIDTH)), like((ROWS, WIDTH))],
        [at, own_tokens, vectors_all] + mixed_pieces,
        out_mine + out_other,
        scratch=[
            pltpu.VMEM((ROWS, 8 * SPAN), LOW),
            pltpu.VMEM((ROWS, 8 * BLOCK), LOW),
            pltpu.VMEM((ROWS, WIDTH), WIDE),
        ]
        + OUT_WEIGHT_SCRATCH,
    )

    all_second, second_came = gather_rows(normed_second)
    weight_fc = far_blocks(fc_near, normed_second)
    mixed_other = c_swap(after(mixed, second_came))
    hidden, d_hidden_in, d_second_near, d_second_far, fc_bias_sum = feed(
        at, all_second, all_cotangent, weight_fc, proj_pieces, fc_bias_own
    )
    d_second_parts, d_second_sent, d_second_came = team_parts(d_second_near, d_second_far)

    hidden_late = after(hidden, d_second_sent)
    feed_pieces = feed_grad(at, all_second, d_hidden_in, hidden_late, all_cotangent)
    feed_total = lax.psum_scatter(
        after(feed_pieces, d_second_came), "x", scatter_dimension=0, tiled=True
    )

    d_middle, d_branch, second_sums, *d_mixed = second_back(
        at,
        middle,
        own_cotangent,
        after(vectors_all, feed_pieces),
        d_second_parts[0],
        d_second_parts[1],
        d_second_parts[2:],
        out_mine,
        out_other,
    )
    d_got = [d_mixed[0]] + [z_swap(d_mixed[d], d) for d in (1, 2, 3)]
    out_sent = out_grad(at, mixed, mixed_other, d_branch, c_swap(d_branch))
    d_keep = jnp.concatenate([v[:, :SPAN] for v in d_got])
    d_give = jnp.concatenate([v[:, SPAN:] for v in d_got])
    d_mixed_heads = jnp.concatenate([d_keep, c_swap(after(d_give, out_sent))])
    out_late = after(out_sent, d_give)
    out_came = [z_swap(out_late[d], d) for d in (1, 3)]
    d_qkv = attend_back(places, qkv, logsum, d_mixed_heads)
    d_qkv = after(d_qkv, out_came)
    out_came.append(z_swap(after(out_late[2], out_came), 2))

    def blocks_call(body, name, counts, *args):
        outs = [like((count, PIECE, FF_PART)) for count in counts]
        return whole_call(body, name, outs, at, *args)

    qkv_pieces = whole_call(
        qkv_grad_kernel,
        "qkv_grad",
        [like((8, PIECE, FF_PART))] * 4,
        at,
        normed_first,
        d_qkv,
        scratch=[pltpu.VMEM((WIDTH, FF_PART), WIDE)],
        limit=VMEM_LIMIT,
    )
    qkv_got = [x_swap(qkv_pieces[d], d) for d in (1, 3)]
    d_first_near, d_first_far, qkv_sums = first_back(at, after(d_qkv, qkv_pieces), weight_qkv)
    qkv_got.append(x_swap(after(qkv_pieces[2], qkv_got), 2))
    d_first_parts, d_first_sent, d_first_came = team_parts(
        d_first_near, d_first_far, (qkv_got[:2], out_came)
    )
    out_pieces = whole_call(
        out_sum_kernel,
        "out_sum",
        [like((2, PIECE, FF_PART))] * 4,
        at,
        out_sent[0],
        *after(out_came, d_first_sent),
        scratch=[pltpu.VMEM((CARRY, WIDTH), WIDE)],
    )
    out_x = [x_swap(out_pieces[d], d) for d in (1, 3)]
    feed_total = after(feed_total, d_first_sent)
    half_got = c_swap(lax.dynamic_slice_in_dim(feed_total, 12 - 4 * c, 4, 0))
    feed_keep, give_fc, give_proj = blocks_call(
        feed_mid_kernel, "feed_mid", [8, 4, 4], feed_total, half_got
    )
    feed_y = [y_swap(give_fc, 1), y_swap(give_proj, 3)]
    (feed_half,) = blocks_call(
        add_halves_kernel, "feed_half", [8], after(feed_keep, d_first_came[0]), *feed_y
    )
    feed_last = y_swap(feed_half, 2)
    grad_low, sums = input_back(
        at,
        own_tokens,
        d_middle,
        after(vectors_all, feed_half, out_x),
        second_sums,
        fc_bias_sum,
        qkv_sums,
        d_first_parts,
    )
    out_x.append(x_swap(after(out_pieces[2], sums), 2))
    grad_turned = turn(grad_low)
    input_grad = grad_turned.astype(WIDE)

    qkv_keep, give_one, give_two = blocks_call(
        qkv_x_kernel,
        "qkv_x",
        [7, 4, 3],
        qkv_pieces[0],
        *qkv_got,
        out_pieces[0],
        *out_x,
        sums,
    )
    qkv_y = [y_swap(give_one, 1), y_swap(give_two, 3)]
    feed_own, feed_one, feed_two, feed_three, feed_rest = blocks_call(
        split_sum_kernel, "feed_y", [1, 1, 1, 1, 4], after(feed_half, give_one), feed_last
    )
    feed_z = [z_swap(part, d) for d, part in ((1, feed_one), (2, feed_two), (3, feed_three))]
    final_near, final_far = final_part(at, after(hidden, feed_own), proj_pieces)
    (qkv_half,) = blocks_call(add_halves_kernel, "qkv_half", [7], after(qkv_keep, final_far), *qkv_y)
    qkv_last = y_swap(qkv_half, 2)
    (feed_rows,) = blocks_call(
        feed_z_kernel, "feed_z", [8], after(feed_own, qkv_half), *feed_z, feed_rest
    )
    feed_rows = lax.all_gather(feed_rows, "x", axis=0)
    final_parts, final_sent, final_came = team_parts(final_near, after(final_far, qkv_half))
    qkv_own, qkv_one, qkv_two, qkv_three, qkv_rest, sums_total = blocks_call(
        qkv_y_kernel, "qkv_y", [1, 2, 2, 2, 2, 1], after(qkv_half, final_sent, grad_turned), qkv_last
    )
    qkv_z = [z_swap(part, d) for d, part in ((1, qkv_one), (2, qkv_two), (3, qkv_three))]
    (qkv_rows,) = blocks_call(
        qkv_z_kernel, "qkv_z", [7], after(qkv_own, final_came), sums_total, *qkv_z, qkv_rest
    )
    qkv_rows = spread_x(qkv_rows, x_swap)
    output_low = output_rows(middle, after(vectors_all, qkv_rows[0]), final_parts)
    output = turn(output_low)
    grad_fc, grad_proj = whole_call(
        place_feed_kernel,
        "place_feed",
        [like((SHARD, 8 * FF_PART), WIDE), like((FF_PART, WIDTH), WIDE)],
        at,
        feed_rows,
        c_swap(after(feed_rows, qkv_rows[1], qkv_rows[3])),
        limit=VMEM_LIMIT,
    )
    qkv_other = [c_swap(after(part, output, grad_fc)) for part in qkv_rows]
    vector_shapes = [like((SHARD,), WIDE)] * 6 + [like((FF_PART,), WIDE)]
    vector_shapes += [like((SHARD,), WIDE)] * 2
    grad_qkv, grad_out, *vector_grads = whole_call(
        place_qkv_kernel,
        "place_qkv",
        [like((SHARD, 3 * WIDTH), WIDE), like((SHARD, WIDTH), WIDE)] + vector_shapes,
        at,
        *qkv_rows,
        *qkv_other,
        scratch=[
            pltpu.VMEM((2, 4, 7) + SUMS, LOW),
            pltpu.VMEM(SUMS, WIDE),
            pltpu.VMEM((1, 8 * SPAN), WIDE),
        ],
        limit=VMEM_LIMIT,
    )

    g_gain_one, g_bias_one, g_gain_two, g_bias_two, g_out_b, g_proj_b = vector_grads[:6]
    g_fc_b, g_query_b, g_value_b = vector_grads[6:]

    return (
        output,
        input_grad,
        g_gain_one,
        g_bias_one,
        grad_qkv,
        g_query_b,
        g_value_b,
        grad_out,
        g_out_b,
        g_gain_two,
        g_bias_two,
        grad_fc,
        g_fc_b,
        grad_proj,
        g_proj_b,
    )


def solution(mesh):
    fine = Mesh(mesh.devices.reshape(2, 4, 2, 2, 4), ("yh", "x", "c", "yl", "z"))
    group, owner = ("yh", "x", "c"), ("yl", "z")
    everyone = group + owner
    vector, matrix = P(owner), P(owner, None)
    rows = P(everyone, None)
    return jax.shard_map(
        local,
        mesh=fine,
        in_specs=(
            rows,
            P(group, None),
            vector,
            vector,
            matrix,
            vector,
            vector,
            matrix,
            vector,
            vector,
            vector,
            matrix,
            vector,
            matrix,
            vector,
            rows,
        ),
        out_specs=(
            rows,
            rows,
            vector,
            vector,
            matrix,
            vector,
            vector,
            matrix,
            vector,
            vector,
            vector,
            matrix,
            vector,
            matrix,
            vector,
        ),
        check_vma=False,
    )
```

```python
import jax
import jax.numpy as jnp
from jax import lax
from jax.experimental import pallas as pl
from jax.experimental.pallas import tpu as pltpu
from jax.sharding import Mesh
from jax.sharding import PartitionSpec as P

HEADS = 25
HEAD_DIM = 64
EPSILON = 1e-05
LOW = jnp.bfloat16
WIDE = jnp.float32

TEAM_HEADS = 4
SPAN = TEAM_HEADS * HEAD_DIM
SHARD = 200
BLOCK = 256
CARRY = 208
WIDTH = 1600
LANES = 1664
ROWS = 128
FF_PART = 800
PIECE = 56
PIECE_STEP = 48
VMEM_LIMIT = 60 * 1024 * 1024
SMALL_LIMIT = 24 * 1024 * 1024


def after(value, *others):
    if not jax.tree.leaves(others):
        return value
    return lax.optimization_barrier((value, others))[0]


def z_swap(value, step):
    return lax.ppermute(value, "z", [(i, i ^ step) for i in range(4)])


def x_swap(value, step):
    return lax.ppermute(value, "x", [(i, i ^ step) for i in range(4)])


def y_swap(value, step):
    return lax.ppermute(value, ("yh", "yl"), [(i, i ^ step) for i in range(4)])


def c_swap(value):
    return lax.ppermute(value, "c", [(0, 1), (1, 0)])


def team_swap(value, slot):
    return lax.ppermute(value, ("c", "z"), [(i, i ^ slot) for i in range(8)])


def turn(value):
    return lax.ppermute(value, ("c", "yl"), [(0, 0), (1, 2), (2, 1), (3, 3)])


def y_swap_some(value, step, sender_diagonal):
    pairs = []
    for yh in range(2):
        for c in range(2):
            for yl in range(2):
                if (c == yl) == sender_diagonal:
                    y = (yh * 2 + yl) ^ step
                    pairs.append((yh * 4 + c * 2 + yl, (y // 2) * 4 + c * 2 + y % 2))
    return lax.ppermute(value, ("yh", "c", "yl"), pairs)


def x_swap_diagonal(value, step):
    pairs = []
    for x in range(4):
        for c in range(2):
            pairs.append((x * 4 + c * 3, (x ^ step) * 4 + c * 3))
    return lax.ppermute(value, ("x", "c", "yl"), pairs)


def pick(blocks, index):
    return lax.dynamic_index_in_dim(blocks, index, 0, keepdims=False)


DOWN = (((0,), (0,)), ((), ()))


ME, MEMBER, CORE, X, YL, Z = range(6)

def cost(microseconds):
    return pl.CostEstimate(flops=microseconds * 10**9, bytes_accessed=0, transcendentals=0)


SMEM = pl.BlockSpec(memory_space=pltpu.SMEM)
VMEM = pl.BlockSpec(memory_space=pltpu.VMEM)
ANY = pl.BlockSpec(memory_space=pltpu.HBM)


def like(shape, dtype=LOW):
    return jax.ShapeDtypeStruct(shape, dtype)


def whole_call(body, name, outs, *args, scratch=(), limit=SMALL_LIMIT):
    return pl.pallas_call(
        body,
        in_specs=[SMEM] + [VMEM] * (len(args) - 1),
        out_specs=[VMEM] * len(outs),
        out_shape=list(outs),
        scratch_shapes=list(scratch),
        compiler_params=pltpu.CompilerParams(vmem_limit_bytes=limit),
        cost_estimate=cost(0),
        name=name,
    )(*args)


def held_call(body, name, outs, at, *args, scratch=(), rows=None):
    count, made = len(args), len(outs)
    heights = [a.shape[0] if rows is None else min(rows, a.shape[0]) for a in args]

    def run(at_ref, *refs):
        sources, results, rest = refs[:count], refs[count : count + made], refs[count + made :]
        targets, others, sems = rest[:count], rest[count:-1], rest[-1]
        pairs = [(f.at[pl.ds(0, h)], t) for f, h, t in zip(sources, heights, targets)]
        for copy in load(pairs, sems):
            copy.wait()
        body(at_ref, *targets, *results, *others)

    return pl.pallas_call(
        run,
        in_specs=[SMEM] + [ANY] * count,
        out_specs=[VMEM] * made,
        out_shape=list(outs),
        scratch_shapes=[pltpu.VMEM((h,) + a.shape[1:], a.dtype) for a, h in zip(args, heights)]
        + list(scratch)
        + [pltpu.SemaphoreType.DMA((count,))],
        compiler_params=pltpu.CompilerParams(vmem_limit_bytes=VMEM_LIMIT),
        cost_estimate=cost(0),
        name=name,
    )(at, *args)


def whole_call_any(body, name, outs, args, others, scratch=()):
    return pl.pallas_call(
        body,
        in_specs=[SMEM] + [VMEM] * (len(args) - 1) + [ANY] * len(others),
        out_specs=[VMEM] * len(outs),
        out_shape=list(outs),
        scratch_shapes=list(scratch),
        compiler_params=pltpu.CompilerParams(vmem_limit_bytes=VMEM_LIMIT),
        cost_estimate=cost(0),
        name=name,
    )(*args, *others)


def block_at(index):
    return pl.ds(pl.multiple_of(index * BLOCK, BLOCK), BLOCK)


def to_blocks(source, mine, write):
    lane = lax.broadcasted_iota(jnp.int32, (source.shape[0], BLOCK), 1)
    for s in range(8):
        block = source[:, SHARD * s : SHARD * s + BLOCK]
        write(s ^ mine, jnp.where(lane < SHARD, block, jnp.zeros_like(block)))


def from_blocks(source, mine, target):
    for s in range(8):
        block = source[:, block_at(s ^ mine)]
        target[:, SHARD * s : SHARD * s + SHARD] = block[:, :SHARD].astype(target.dtype)


def prepare_qkv_kernel(at, weight, *refs):
    held, outs, vectors, sems = refs[:9], refs[9:13], refs[13:22], refs[22]
    copies = load(list(zip(held, vectors)), sems)
    for copy in copies:
        copy.wait()
    lane = lax.broadcasted_iota(jnp.int32, (SHARD, SPAN), 1)
    for d, out in enumerate(outs):
        j = at[CORE] * 4 + (at[Z] ^ d)
        valid = lane < WIDTH - SPAN * j
        none = jnp.zeros((SHARD, SPAN), LOW)
        query = weight[:, pl.ds(pl.multiple_of(SPAN * j, SPAN), SPAN)]
        out[:SHARD, :SPAN] = jnp.where(valid, query, none)
        key = weight[:, pl.ds(pl.multiple_of(WIDTH - 64 + SPAN * j, SPAN), SPAN + 128)]
        out[:SHARD, SPAN : 2 * SPAN] = jnp.where(valid, key[:, 64 : 64 + SPAN], none)

        @pl.when(j < 6)
        def _():
            start = pl.multiple_of(2 * WIDTH + SPAN * j, 128)
            out[:SHARD, 2 * SPAN :] = weight[:, pl.ds(start, SPAN)]

        @pl.when(j >= 6)
        def _():
            out[:SHARD, 2 * SPAN :] = none

        @pl.when(j == 6)
        def _():
            out[:SHARD, 2 * SPAN : 2 * SPAN + 64] = weight[:, 3 * WIDTH - 64 :]

        out[SHARD:, :] = jnp.zeros((CARRY - SHARD, 3 * SPAN), LOW)
        for i, vector in enumerate(vectors[:8]):
            out[SHARD + i : SHARD + i + 1, :SHARD] = vector[...].reshape(1, SHARD)
        for i in range(4):
            part = vectors[8][SHARD * i : SHARD * (i + 1)]
            out[SHARD + i : SHARD + i + 1, BLOCK : BLOCK + SHARD] = part.reshape(1, SHARD)


def prepare_rest_kernel(at, fc, outer, out_half, *outs):
    pad = jnp.zeros((CARRY - SHARD, FF_PART), LOW)
    for half in range(2):

        @pl.when(at[CORE] == half)
        def _():
            out_half[:SHARD, :] = outer[:, FF_PART * half : FF_PART * (half + 1)]

    out_half[SHARD:, :] = pad
    for r in range(4):
        start, shift = FF_PART * r // 128 * 128, FF_PART * r % 128
        start = pl.multiple_of(at[CORE] * (4 * FF_PART) + start, 128)
        part = fc[:, pl.ds(start, 896)][:, shift : shift + FF_PART]
        for d, out in enumerate(outs):

            @pl.when((at[Z] ^ d) == r)
            def _():
                out[:SHARD, :] = part
                out[SHARD:, :] = pad


def normalize(inputs):
    average = jnp.mean(inputs, axis=-1, keepdims=True)
    centred = inputs - average
    spread = jnp.mean(centred * centred, axis=-1, keepdims=True)
    inverse = lax.rsqrt(spread + EPSILON)
    return centred * inverse, inverse


def norm_back(d_normed, hat, inverse, gain):
    e = d_normed * gain
    return inverse * (
        e
        - jnp.mean(e, axis=-1, keepdims=True)
        - hat * jnp.mean(e * hat, axis=-1, keepdims=True)
    )


def load(pairs, sems):
    copies = [pltpu.make_async_copy(f, t, sems.at[i]) for i, (f, t) in enumerate(pairs)]
    for copy in copies:
        copy.start()
    return copies


def weight_pairs(pieces, target):
    pairs, k = [], 0
    for piece in pieces:
        for one in [piece] if len(piece.shape) == 2 else [piece.at[0], piece.at[1]]:
            pairs.append((one, target.at[k, pl.ds(0, CARRY)]))
            k += 1
    return pairs


def clear_pad(target):
    target[:, CARRY:, :] = jnp.zeros((8, BLOCK - CARRY, target.shape[2]), LOW)


def first_kernel(at, *refs):
    token_refs, weight_refs, refs = refs[:8], refs[8:12], refs[12:]
    normed, qkv, vectors, fc_bias, tokens, weight, wide, blocks, spread, *sems = refs
    step = pl.program_id(0)

    def token_copy(k):
        target = tokens.at[k ^ at[MEMBER]]
        return pltpu.make_async_copy(token_refs[k], target, sems[1].at[k])

    @pl.when(step == 0)
    def _():
        for k in range(8):
            token_copy(k).start()
        copies = load(weight_pairs(weight_refs, weight), sems[0])
        clear_pad(weight)
        spread[...] = jnp.zeros_like(spread)
        wide[:, WIDTH:] = jnp.zeros((wide.shape[0], wide.shape[1] - WIDTH), LOW)
        for copy in copies:
            copy.wait()
        for k in range(8):
            block = weight[k ^ at[ME], SHARD:CARRY, :BLOCK].astype(WIDE)
            spread[:, SHARD * k : SHARD * (k + 1)] = block[:, :SHARD]
        vectors[...] = spread[:, :WIDTH]
        rows = weight[(at[CORE] ^ at[YL]) * 4, SHARD:CARRY, BLOCK : 2 * BLOCK].astype(WIDE)
        for i in range(4):
            fc_bias[:, SHARD * i : SHARD * (i + 1)] = rows[i : i + 1, :SHARD]
        for k in range(8):
            token_copy(k).wait()

    rows = tokens[pl.ds(step * 2, 2)].reshape(2 * ROWS, WIDTH)
    hat, _ = normalize(rows.astype(WIDE))
    low = (hat * spread[0:1, :WIDTH] + spread[1:2, :WIDTH]).astype(LOW)
    normed[...] = low
    wide[:, :WIDTH] = low

    def write(k, block):
        blocks[:, block_at(k)] = block

    to_blocks(wide, at[ME], write)
    heads = pl.ds(pl.multiple_of(SPAN * at[MEMBER], SPAN), SPAN)
    total = jnp.dot(
        blocks[...], weight[...].reshape(8 * BLOCK, 3 * SPAN), preferred_element_type=WIDE
    )
    qkv[:, :SPAN] = (total[:, :SPAN] + spread[2:3, heads]).astype(LOW)
    qkv[:, SPAN : 2 * SPAN] = total[:, SPAN : 2 * SPAN].astype(LOW)
    qkv[:, 2 * SPAN :] = (total[:, 2 * SPAN :] + spread[3:4, heads]).astype(LOW)


Q_ROWS = 256


def first(at, tokens, weight):
    rows = 8 * ROWS
    still = lambda i: (0, 0)
    down = lambda i: (i, 0)
    return pl.pallas_call(
        first_kernel,
        grid=(rows // Q_ROWS,),
        in_specs=[SMEM] + [ANY] * 12,
        out_specs=[
            pl.BlockSpec((Q_ROWS, WIDTH), down),
            pl.BlockSpec((Q_ROWS, 3 * SPAN), down),
            pl.BlockSpec((8, WIDTH), still),
            pl.BlockSpec((1, FF_PART), still),
        ],
        out_shape=[
            like((rows, WIDTH)),
            like((rows, 3 * SPAN)),
            like((8, WIDTH), WIDE),
            like((1, FF_PART), WIDE),
        ],
        scratch_shapes=[
            pltpu.VMEM((8, ROWS, WIDTH), LOW),
            pltpu.VMEM((8, BLOCK, 3 * SPAN), LOW),
            pltpu.VMEM((Q_ROWS, WIDTH + 192), LOW),
            pltpu.VMEM((Q_ROWS, 8 * BLOCK), LOW),
            pltpu.VMEM((8, 8 * BLOCK), WIDE),
            pltpu.SemaphoreType.DMA((8,)),
            pltpu.SemaphoreType.DMA((8,)),
        ],
        compiler_params=pltpu.CompilerParams(vmem_limit_bytes=VMEM_LIMIT),
        cost_estimate=cost(0),
        name="first_norm_qkv",
    )(at, *tokens, *weight)


def visible(lengths, first_row, rows, keys):
    row = first_row + lax.broadcasted_iota(jnp.int32, (rows, 1), 0)
    key = lax.broadcasted_iota(jnp.int32, (1, keys), 1)
    start = jnp.zeros_like(row)
    bound = 0
    for i in range(3):
        bound = bound + lengths[0, i]
        start = jnp.where(row >= bound, bound, start)
    return (key <= row) & (key >= start)


ACROSS = (((1,), (1,)), ((), ()))


def by_block(body):
    for i in range(8 * ROWS // Q_ROWS):
        pl.when(pl.program_id(0) == i)(lambda i=i: body(i))


def slot_rows(at, chunk):
    return pl.ds(pl.multiple_of((chunk ^ at[MEMBER]) * ROWS, ROWS), ROWS)


def attend_kernel(at, lengths, q_ref, k_ref, v_ref, mixed_ref, logsum_ref):
    def block(i):
        keys = Q_ROWS * (i + 1)
        q, k, v = q_ref[...], k_ref[:keys, :], v_ref[:keys, :]
        allowed = visible(lengths, i * Q_ROWS, Q_ROWS, keys)
        lane = lax.broadcasted_iota(jnp.int32, q.shape, 1) // HEAD_DIM
        slim = lax.broadcasted_iota(jnp.int32, logsum_ref.shape, 1)
        mixed = jnp.zeros(q.shape, WIDE)
        logsums = jnp.zeros(logsum_ref.shape, WIDE)
        for head in range(TEAM_HEADS):
            own = lane == head
            q_own = jnp.where(own, q, jnp.zeros_like(q))
            scores = lax.dot_general(q_own, k, ACROSS, preferred_element_type=WIDE)
            scores = jnp.where(allowed, scores * (HEAD_DIM**-0.5), -1e30)
            top = jnp.max(scores, axis=-1, keepdims=True)
            powers = jnp.exp(scores - top)
            total = jnp.sum(powers, axis=-1, keepdims=True)
            probs = (powers * (1.0 / total)).astype(LOW)
            mixed = jnp.where(own, jnp.dot(probs, v, preferred_element_type=WIDE), mixed)
            logsums = jnp.where(slim == head, top + jnp.log(total), logsums)
        low = mixed.astype(LOW)
        for half in range(Q_ROWS // ROWS):
            rows = slot_rows(at, i * (Q_ROWS // ROWS) + half)
            mixed_ref[rows, :] = low[ROWS * half : ROWS * (half + 1)]
        logsum_ref[...] = logsums

    by_block(block)


def attend_back_kernel(
    at, lengths, q_ref, k_ref, v_ref, logsum_ref, dmix_ref, out_ref, dk_total, dv_total
):
    scale = HEAD_DIM**-0.5

    def block(i):
        keys = Q_ROWS * (i + 1)
        if i == 0:
            dk_total[...] = jnp.zeros_like(dk_total)
            dv_total[...] = jnp.zeros_like(dv_total)
        q, k, v = q_ref[...], k_ref[:keys, :], v_ref[:keys, :]
        count = Q_ROWS // ROWS
        dmix = jnp.concatenate([dmix_ref[slot_rows(at, i * count + n), :] for n in range(count)])
        allowed = visible(lengths, i * Q_ROWS, Q_ROWS, keys)
        lane = lax.broadcasted_iota(jnp.int32, q.shape, 1) // HEAD_DIM
        dq = jnp.zeros(q.shape, WIDE)
        for head in range(TEAM_HEADS):
            own = lane == head
            q_own = jnp.where(own, q, jnp.zeros_like(q))
            dmix_own = jnp.where(own, dmix, jnp.zeros_like(dmix))
            scores = lax.dot_general(q_own, k, ACROSS, preferred_element_type=WIDE) * scale
            scores = jnp.where(allowed, scores, -1e30)
            probs = jnp.exp(scores - logsum_ref[:, head : head + 1])
            d_probs = lax.dot_general(dmix_own, v, ACROSS, preferred_element_type=WIDE)
            term = jnp.sum(probs * d_probs, axis=-1, keepdims=True)
            d_scores = (probs * (d_probs - term)).astype(LOW)
            dq = jnp.where(own, jnp.dot(d_scores, k, preferred_element_type=WIDE), dq)
            dk_total[:keys, :] += lax.dot_general(
                d_scores, q_own, DOWN, preferred_element_type=WIDE
            )
            dv_total[:keys, :] += lax.dot_general(
                probs.astype(LOW), dmix_own, DOWN, preferred_element_type=WIDE
            )
        out_ref[Q_ROWS * i : Q_ROWS * (i + 1), :SPAN] = (dq * scale).astype(LOW)
        if i == 8 * ROWS // Q_ROWS - 1:
            out_ref[:, SPAN : 2 * SPAN] = (dk_total[...] * scale).astype(LOW)
            out_ref[:, 2 * SPAN :] = dv_total[...].astype(LOW)

    by_block(block)


def attend_specs(rows):
    return [
        SMEM,
        SMEM,
        pl.BlockSpec((Q_ROWS, SPAN), lambda i: (i, 0)),
        pl.BlockSpec((rows, SPAN), lambda i: (0, 1)),
        pl.BlockSpec((rows, SPAN), lambda i: (0, 2)),
    ]


def attend(places, qkv):
    rows = qkv.shape[0]
    return pl.pallas_call(
        attend_kernel,
        grid=(rows // Q_ROWS,),
        in_specs=attend_specs(rows),
        out_specs=[
            pl.BlockSpec((rows, SPAN), lambda i: (0, 0)),
            pl.BlockSpec((Q_ROWS, 128), lambda i: (i, 0)),
        ],
        out_shape=[
            jax.ShapeDtypeStruct((rows, SPAN), LOW),
            jax.ShapeDtypeStruct((rows, 128), WIDE),
        ],
        compiler_params=pltpu.CompilerParams(vmem_limit_bytes=VMEM_LIMIT),
        cost_estimate=cost(0),
        name="attend",
    )(*places, qkv, qkv, qkv)


def attend_back(places, qkv, logsum, dmix):
    rows = qkv.shape[0]
    whole = lambda i: (0, 0)
    return pl.pallas_call(
        attend_back_kernel,
        grid=(rows // Q_ROWS,),
        in_specs=attend_specs(rows)
        + [pl.BlockSpec((Q_ROWS, 128), lambda i: (i, 0)), pl.BlockSpec((rows, SPAN), whole)],
        out_specs=pl.BlockSpec((rows, 3 * SPAN), whole),
        out_shape=like((rows, 3 * SPAN)),
        scratch_shapes=[pltpu.VMEM((rows, SPAN), WIDE)] * 2,
        compiler_params=pltpu.CompilerParams(vmem_limit_bytes=VMEM_LIMIT),
        cost_estimate=cost(0),
        name="attend_back",
    )(*places, qkv, qkv, qkv, logsum, dmix)


def middle_kernel(at, tokens, vectors, *refs):
    pieces, mine_refs, other_refs, refs = refs[:4], refs[4:8], refs[8:12], refs[12:]
    middle, normed, mixed_out, mixed, blocks, wide, mine, other, *sems = refs
    copies = load(weight_pairs(mine_refs, mine), sems[0])
    copies += load(weight_pairs(other_refs, other), sems[1])
    clear_pad(mine)
    clear_pad(other)
    for d, piece in enumerate(pieces):
        mixed[:, block_at(d ^ at[MEMBER])] = piece[:, :SPAN]
        mixed[:, block_at((4 + d) ^ at[MEMBER])] = piece[:, SPAN:]

    def write_blocks(k, block):
        blocks[:, block_at(k)] = block

    to_blocks(mixed, at[ME], write_blocks)
    mixed_out[...] = mixed[:, :WIDTH]
    for copy in copies[:8]:
        copy.wait()
    flat = (8 * BLOCK, FF_PART)
    a = jnp.dot(blocks[...], mine[...].reshape(flat), preferred_element_type=WIDE)
    for copy in copies[8:]:
        copy.wait()
    b = jnp.dot(blocks[...], other[...].reshape(flat), preferred_element_type=WIDE)
    wide[:, :FF_PART] = jnp.where(at[CORE] == 0, a, b)
    wide[:, FF_PART:] = jnp.where(at[CORE] == 0, b, a)
    total = tokens[...].astype(WIDE) + wide[...] + vectors[4:5, :]
    middle[...] = total
    hat, _ = normalize(total)
    normed[...] = (hat * vectors[5:6, :] + vectors[6:7, :]).astype(LOW)


OUT_WEIGHT_SCRATCH = [
    pltpu.VMEM((8, BLOCK, FF_PART), LOW),
    pltpu.VMEM((8, BLOCK, FF_PART), LOW),
    pltpu.SemaphoreType.DMA((8,)),
    pltpu.SemaphoreType.DMA((8,)),
]


def proj_pairs(own, first_half, second_half, target):
    rows = FF_PART // 2
    return (
        [(own.at[pl.ds(0, rows)], target.at[pl.ds(0, rows)]), (own.at[pl.ds(rows, rows)], target.at[pl.ds(rows, rows)])],
        [(first_half, target.at[pl.ds(0, rows)]), (second_half, target.at[pl.ds(rows, rows)])],
    )


def load_proj(at, refs, target, sems):
    own, got = proj_pairs(*refs, target)

    @pl.when(at[CORE] == at[YL])
    def _():
        for copy in load(own, sems):
            copy.wait()

    @pl.when(at[CORE] != at[YL])
    def _():
        for copy in load(got, sems):
            copy.wait()


def halves(i):
    return jnp.minimum(i, 1), 0


def late_halves(i):
    return jnp.maximum(i - 2, 0), 0


def write_half(step, near, far, value):
    @pl.when(step < 2)
    def _():
        near[:, :WIDTH] = value
        near[:, WIDTH:] = jnp.zeros((value.shape[0], LANES - WIDTH), LOW)

    @pl.when(step >= 2)
    def _():
        far[:, :WIDTH] = value
        far[:, WIDTH:] = jnp.zeros((value.shape[0], LANES - WIDTH), LOW)


def feed_kernel(at, bias, *refs):
    cot_refs, normed_refs, fc_refs, proj_refs = refs[:8], refs[8:16], refs[16:20], refs[20:23]
    hidden, d_in, near, far, bias_sum, normed, cot, fc, proj, wide, blocks, tall, back, *sems = (
        refs[23:]
    )
    step = pl.program_id(0)

    def normed_copy(k):
        return pltpu.make_async_copy(normed_refs[k], normed.at[k], sems[0].at[k])

    def cot_copy(k):
        return pltpu.make_async_copy(cot_refs[k], cot.at[k], sems[3].at[k])

    own, got = proj_pairs(*proj_refs, proj)
    diagonal = at[CORE] == at[YL]

    def proj_copy(i):
        return pltpu.make_async_copy(got[i][0], got[i][1], sems[2].at[i])

    @pl.when(step == 0)
    def _():
        for k in range(2):
            normed_copy(k).start()
        copies = load(weight_pairs(fc_refs, fc), sems[1])
        clear_pad(fc)
        bias_sum[...] = jnp.zeros_like(bias_sum)
        wide[:, WIDTH:] = jnp.zeros((2 * ROWS, wide.shape[1] - WIDTH), LOW)
        for copy in copies:
            copy.wait()
        for k in range(2):
            cot_copy(k).start()

        @pl.when(diagonal)
        def _():
            load(own, sems[2])

        @pl.when(jnp.logical_not(diagonal))
        def _():
            load(got, sems[2])

    for k in range(8):

        @pl.when(step == k // 2)
        def _():
            normed_copy(k).wait()

        @pl.when(step + 1 == k // 2)
        def _():
            normed_copy(k).start()
            cot_copy(k).start()

    wide[:, :WIDTH] = normed[pl.ds(step * 2, 2)].reshape(2 * ROWS, WIDTH)

    def write(k, block):
        blocks[:, block_at(k)] = block

    to_blocks(wide, at[ME], write)
    weight = fc[...].reshape(8 * BLOCK, FF_PART)
    u = jnp.dot(blocks[...], weight, preferred_element_type=WIDE) + bias[...]
    for k in range(8):

        @pl.when(step == k // 2)
        def _():
            cot_copy(k).wait()

    @pl.when(step == 0)
    def _():
        proj_copy(0).wait()
        proj_copy(1).wait()

    cot_rows = cot[pl.ds(step * 2, 2)].reshape(2 * ROWS, WIDTH)
    d_hidden = lax.dot_general(cot_rows, proj[...], ACROSS, preferred_element_type=WIDE)
    factor = (2.0 / jnp.pi) ** 0.5
    square = u * u
    bent = jnp.tanh(factor * (u + 0.044715 * (square * u)))
    half = 0.5 * (1.0 + bent)
    hidden[...] = (u * half).astype(LOW)
    slope = half + (0.5 * factor) * u * (1.0 - bent * bent) * (1.0 + (3 * 0.044715) * square)
    low = (d_hidden * slope).astype(LOW)
    d_in[...] = low
    bias_sum[...] += jnp.sum(low.astype(WIDE), axis=0, keepdims=True)
    tall[...] = lax.dot_general(low, weight, ACROSS, preferred_element_type=WIDE).astype(LOW)
    from_blocks(tall, at[ME], back)
    write_half(step, near, far, back[...])


def feed(at, normed, cot, fc, proj, bias):
    rows = 8 * ROWS
    still = lambda i: (0, 0)
    down = lambda i: (i, 0)
    return pl.pallas_call(
        feed_kernel,
        grid=(rows // Q_ROWS,),
        in_specs=[SMEM, pl.BlockSpec((1, FF_PART), still)] + [ANY] * 23,
        out_specs=[
            pl.BlockSpec((Q_ROWS, FF_PART), down),
            pl.BlockSpec((Q_ROWS, FF_PART), down),
            pl.BlockSpec((Q_ROWS, LANES), halves),
            pl.BlockSpec((Q_ROWS, LANES), late_halves),
            pl.BlockSpec((1, FF_PART), still),
        ],
        out_shape=[
            like((rows, FF_PART)),
            like((rows, FF_PART)),
            like((rows // 2, LANES)),
            like((rows // 2, LANES)),
            like((1, FF_PART), WIDE),
        ],
        scratch_shapes=[
            pltpu.VMEM((8, ROWS, WIDTH), LOW),
            pltpu.VMEM((8, ROWS, WIDTH), LOW),
            pltpu.VMEM((8, BLOCK, FF_PART), LOW),
            pltpu.VMEM((FF_PART, WIDTH), LOW),
            pltpu.VMEM((Q_ROWS, WIDTH + 192), LOW),
            pltpu.VMEM((Q_ROWS, 8 * BLOCK), LOW),
            pltpu.VMEM((Q_ROWS, 8 * BLOCK), LOW),
            pltpu.VMEM((Q_ROWS, WIDTH), LOW),
            pltpu.SemaphoreType.DMA((8,)),
            pltpu.SemaphoreType.DMA((8,)),
            pltpu.SemaphoreType.DMA((2,)),
            pltpu.SemaphoreType.DMA((8,)),
        ],
        compiler_params=pltpu.CompilerParams(vmem_limit_bytes=VMEM_LIMIT),
        cost_estimate=cost(0),
        name="feed_forward_and_back",
    )(at, bias, *cot, *normed, *fc, *proj)


def final_kernel(at, hidden, *refs):
    proj_refs, (near, far, proj, sems) = refs[:3], refs[3:]
    step = pl.program_id(0)

    @pl.when(step == 0)
    def _():
        load_proj(at, proj_refs, proj, sems)

    total = jnp.dot(hidden[...], proj[...], preferred_element_type=WIDE).astype(LOW)
    write_half(step, near, far, total)


def final_part(at, hidden, proj):
    rows = hidden.shape[0]
    return pl.pallas_call(
        final_kernel,
        grid=(rows // Q_ROWS,),
        in_specs=[SMEM, pl.BlockSpec((Q_ROWS, FF_PART), lambda i: (i, 0))] + [ANY] * 3,
        out_specs=[
            pl.BlockSpec((Q_ROWS, LANES), halves),
            pl.BlockSpec((Q_ROWS, LANES), late_halves),
        ],
        out_shape=[like((rows // 2, LANES))] * 2,
        scratch_shapes=[pltpu.VMEM((FF_PART, WIDTH), LOW), pltpu.SemaphoreType.DMA((2,))],
        compiler_params=pltpu.CompilerParams(vmem_limit_bytes=VMEM_LIMIT),
        cost_estimate=cost(0),
        name="feed_forward_out",
    )(at, hidden, *proj)


def padded_rows():
    return pl.BlockSpec((ROWS, LANES), lambda i: (0, 0))


def team_total(refs):
    total = refs[0][:, :WIDTH].astype(WIDE)
    for ref in refs[1:]:
        total = total + ref[:, :WIDTH].astype(WIDE)
    return total


def row_sum(value):
    return jnp.sum(value, axis=0, keepdims=True)


def output_kernel(at, middle, vectors, near, got, one, two, three, out):
    total = middle[...] + vectors[7:8, :]
    total = total + team_total([near, got, one, two, three])
    out[...] = jnp.transpose(total).astype(LOW)


def out_grad_kernel(at, left, left_other, right, right_other, *refs):
    outs, total = refs[:4], refs[4]
    first_core = at[CORE] == 0

    def half(ref):
        value = ref[...]
        return jnp.where(first_core, value[:, :FF_PART], value[:, FF_PART:])

    total[:FF_PART, :] = lax.dot_general(
        jnp.concatenate([half(left), half(left_other)]),
        jnp.concatenate([right[...], right_other[...]]),
        DOWN,
        preferred_element_type=WIDE,
    )
    for d, out in enumerate(outs):
        start = pl.multiple_of((at[Z] ^ d) * SHARD, 8)
        out[...] = total[pl.ds(start, CARRY), :].astype(LOW)


def out_grad(at, left, left_other, right, right_other):
    return whole_call(
        out_grad_kernel,
        "out_grad",
        [like((CARRY, WIDTH))] * 4,
        at,
        left,
        left_other,
        right,
        right_other,
        scratch=[pltpu.VMEM((FF_PART + CARRY - SHARD, WIDTH), WIDE)],
        limit=VMEM_LIMIT,
    )


def out_sum_kernel(at, own, one, two, three, out, total):
    total[...] = team_total([own, one, two, three])
    for q in range(4):
        piece = total[PIECE_STEP * q : PIECE_STEP * q + PIECE, :].astype(LOW)
        out[2 * q] = piece[:, :FF_PART]
        out[2 * q + 1] = piece[:, FF_PART:]


def second_back_kernel(at, middle, cot, vectors, near, got, *refs):
    parts, mine_refs, other_refs, refs = refs[:3], refs[3:7], refs[7:11], refs[11:]
    (d_middle, d_branch, sums), pieces, refs = refs[:3], refs[3:7], refs[7:]
    wide, tall, narrow, mine, other, *sems = refs
    copies = load(weight_pairs(mine_refs, mine), sems[0])
    copies += load(weight_pairs(other_refs, other), sems[1])
    clear_pad(mine)
    clear_pad(other)
    d_second = team_total([near, got, *parts])
    hat, inverse = normalize(middle[...])
    d_cot = cot[...].astype(WIDE)
    total = d_cot + norm_back(d_second, hat, inverse, vectors[5:6, :])
    d_middle[...] = total
    low = total.astype(LOW)
    d_branch[...] = low
    sums[0:1, :] = row_sum(d_second * hat)
    sums[1:2, :] = row_sum(d_second)
    sums[2:3, :] = row_sum(low.astype(WIDE))
    sums[3:4, :] = row_sum(d_cot)
    sums[4:8, :] = jnp.zeros((4, WIDTH), WIDE)
    wide[...] = low
    left, right = wide[:, :FF_PART], wide[:, FF_PART:]
    first_core = at[CORE] == 0
    flat = (8 * BLOCK, FF_PART)
    across = (((1,), (1,)), ((), ()))
    for copy in copies[:8]:
        copy.wait()
    part = lax.dot_general(
        jnp.where(first_core, left, right),
        mine[...].reshape(flat),
        across,
        preferred_element_type=WIDE,
    )
    for copy in copies[8:]:
        copy.wait()
    tall[...] = part + lax.dot_general(
        jnp.where(first_core, right, left),
        other[...].reshape(flat),
        across,
        preferred_element_type=WIDE,
    )
    narrow[:, WIDTH:] = jnp.zeros((ROWS, 8 * SPAN - WIDTH), LOW)
    from_blocks(tall, at[ME], narrow)
    for d, piece in enumerate(pieces):
        piece[:, :SPAN] = narrow[:, block_at(d ^ at[MEMBER])]
        piece[:, SPAN:] = narrow[:, block_at((4 + d) ^ at[MEMBER])]


def second_back(at, middle, cot, vectors, near, got, parts, mine, other):
    part = pl.BlockSpec((ROWS, WIDTH), lambda i: (0, 0))
    return pl.pallas_call(
        second_back_kernel,
        grid=(1,),
        in_specs=[SMEM, part, part, pl.BlockSpec((8, WIDTH), lambda i: (0, 0))]
        + [padded_rows()] * 5
        + [ANY] * 8,
        out_specs=[VMEM] * 7,
        out_shape=[like((ROWS, WIDTH), WIDE), like((ROWS, WIDTH)), like((8, WIDTH), WIDE)]
        + [like((ROWS, 2 * SPAN))] * 4,
        scratch_shapes=[
            pltpu.VMEM((ROWS, WIDTH), LOW),
            pltpu.VMEM((ROWS, 8 * BLOCK), WIDE),
            pltpu.VMEM((ROWS, 8 * SPAN), LOW),
        ]
        + OUT_WEIGHT_SCRATCH,
        compiler_params=pltpu.CompilerParams(vmem_limit_bytes=VMEM_LIMIT),
        cost_estimate=cost(0),
        name="second_norm_and_out_back",
    )(at, middle, cot, vectors, near, got, *parts, *mine, *other)


def first_back_kernel(at, d_qkv, *refs):
    weight_refs, (near, far, sums, weight, tall, back, sems) = refs[:4], refs[4:]
    step = pl.program_id(0)

    @pl.when(step == 0)
    def _():
        copies = load(weight_pairs(weight_refs, weight), sems)
        clear_pad(weight)
        sums[...] = row_sum(d_qkv[...].astype(WIDE))
        for copy in copies:
            copy.wait()

    rows = jnp.concatenate([d_qkv[slot_rows(at, 2 * step + n), :] for n in range(2)])
    tall[...] = lax.dot_general(
        rows, weight[...].reshape(8 * BLOCK, 3 * SPAN), ACROSS, preferred_element_type=WIDE
    ).astype(LOW)
    from_blocks(tall, at[ME], back)
    write_half(step, near, far, back[...])


def first_back(at, d_qkv, weight):
    rows = d_qkv.shape[0]
    whole = lambda i: (0, 0)
    return pl.pallas_call(
        first_back_kernel,
        grid=(rows // Q_ROWS,),
        in_specs=[SMEM, pl.BlockSpec((rows, 3 * SPAN), whole)] + [ANY] * 4,
        out_specs=[
            pl.BlockSpec((Q_ROWS, LANES), halves),
            pl.BlockSpec((Q_ROWS, LANES), late_halves),
            pl.BlockSpec((1, 3 * SPAN), whole),
        ],
        out_shape=[
            like((rows // 2, LANES)),
            like((rows // 2, LANES)),
            like((1, 3 * SPAN), WIDE),
        ],
        scratch_shapes=[
            pltpu.VMEM((8, BLOCK, 3 * SPAN), LOW),
            pltpu.VMEM((Q_ROWS, 8 * BLOCK), LOW),
            pltpu.VMEM((Q_ROWS, WIDTH), LOW),
            pltpu.SemaphoreType.DMA((8,)),
        ],
        compiler_params=pltpu.CompilerParams(vmem_limit_bytes=VMEM_LIMIT),
        cost_estimate=cost(0),
        name="qkv_back",
    )(at, d_qkv, *weight)


SUMS = (PIECE, FF_PART)


def input_kernel(at, tokens, d_middle, vectors, second_sums, fc_sum, qkv_sum, *refs):
    parts, (grad, sums, held) = refs[:5], refs[5:]
    d_first = team_total(parts)
    hat, inverse = normalize(tokens[...].astype(WIDE))
    total = d_middle[...] + norm_back(d_first, hat, inverse, vectors[0:1, :])
    grad[...] = jnp.transpose(total).astype(LOW)
    held[...] = jnp.zeros(SUMS, WIDE)
    rows = [row_sum(d_first * hat), row_sum(d_first)] + [second_sums[i : i + 1, :] for i in range(4)]
    for i, row in enumerate(rows):
        held[2 * i : 2 * i + 1, :] = row[:, :FF_PART]
        held[2 * i + 1 : 2 * i + 2, :] = row[:, FF_PART:]
    held[pl.ds(16 + at[MEMBER], 1), :] = fc_sum[...]
    held[pl.ds(24 + at[MEMBER], 1), :SPAN] = qkv_sum[:, :SPAN]
    held[pl.ds(32 + at[MEMBER], 1), :SPAN] = qkv_sum[:, 2 * SPAN :]
    sums[0] = held[...].astype(LOW)


def input_back(at, tokens, d_middle, vectors, second_sums, fc_sum, qkv_sum, parts):
    still = lambda i: (0, 0)
    part = pl.BlockSpec((ROWS, WIDTH), still)
    rows = pl.BlockSpec((8, WIDTH), still)
    return pl.pallas_call(
        input_kernel,
        grid=(1,),
        in_specs=[
            SMEM,
            part,
            part,
            rows,
            rows,
            pl.BlockSpec((1, FF_PART), still),
            pl.BlockSpec((1, 3 * SPAN), still),
        ]
        + [padded_rows()] * 5,
        out_specs=[
            pl.BlockSpec((WIDTH, ROWS), still),
            pl.BlockSpec((1,) + SUMS, lambda i: (0, 0, 0)),
        ],
        out_shape=[like((WIDTH, ROWS)), like((1,) + SUMS)],
        scratch_shapes=[pltpu.VMEM(SUMS, WIDE)],
        compiler_params=pltpu.CompilerParams(vmem_limit_bytes=SMALL_LIMIT),
        cost_estimate=cost(0),
        name="first_norm_back",
    )(at, tokens, d_middle, vectors, second_sums, fc_sum, qkv_sum, *parts)


def feed_grad_kernel(at, hidden, d_in, *refs):
    cot_refs, normed_refs, (out, normed, cot, total, tall, *sems) = refs[:8], refs[8:16], refs[16:]
    pairs = [(normed_refs[k], normed.at[k]) for k in range(8)]
    first_copies = load(pairs, sems[0])
    pairs = [(cot_refs[k], cot.at[k]) for k in range(8)]
    second_copies = load(pairs, sems[1])
    for copy in first_copies:
        copy.wait()
    total[...] = lax.dot_general(
        normed[...].reshape(8 * ROWS, WIDTH), d_in[...], DOWN, preferred_element_type=WIDE
    )
    for k in range(8):
        for q in range(4):
            start = pl.multiple_of((k ^ at[ME]) * SHARD + PIECE_STEP * q, 8)
            out[16 * q + k] = total[pl.ds(start, PIECE), :].astype(LOW)
    for copy in second_copies:
        copy.wait()
    tall[...] = lax.dot_general(
        hidden[...], cot[...].reshape(8 * ROWS, WIDTH), DOWN, preferred_element_type=WIDE
    )
    for q in range(4):
        for half in range(2):
            lanes = slice(FF_PART * half, FF_PART * (half + 1))
            for k in range(4):
                start = SHARD * q + PIECE_STEP * k
                out[16 * q + 8 + 4 * half + k] = tall[start : start + PIECE, lanes].astype(LOW)


def feed_grad(at, normed, d_in, hidden, cot):
    rows = 8 * ROWS
    return pl.pallas_call(
        feed_grad_kernel,
        in_specs=[SMEM, VMEM, VMEM] + [ANY] * 16,
        out_specs=VMEM,
        out_shape=like((64, PIECE, FF_PART)),
        scratch_shapes=[
            pltpu.VMEM((8, ROWS, WIDTH), LOW),
            pltpu.VMEM((8, ROWS, WIDTH), LOW),
            pltpu.VMEM((WIDTH, FF_PART), WIDE),
            pltpu.VMEM((FF_PART, WIDTH), WIDE),
            pltpu.SemaphoreType.DMA((8,)),
            pltpu.SemaphoreType.DMA((8,)),
        ],
        compiler_params=pltpu.CompilerParams(vmem_limit_bytes=VMEM_LIMIT),
        cost_estimate=cost(0),
        name="feed_forward_grad",
    )(at, hidden, d_in, *cot, *normed)


def qkv_grad_kernel(at, normed, d_qkv, *refs):
    outs, total = refs[:4], refs[4]
    total[:, 3 * SPAN :] = jnp.zeros((WIDTH, FF_PART - 3 * SPAN), WIDE)
    total[:, : 3 * SPAN] = lax.dot_general(
        normed[...], d_qkv[...], DOWN, preferred_element_type=WIDE
    )
    for d, out in enumerate(outs):
        place = pl.multiple_of((at[X] ^ d) * PIECE_STEP, 8)
        for k in range(8):
            start = pl.multiple_of((k ^ at[ME]) * SHARD + place, 8)
            out[k] = total[pl.ds(start, PIECE), :].astype(LOW)


def added(refs, k):
    total = refs[0][k].astype(WIDE)
    for ref in refs[1:]:
        total = total + ref[k].astype(WIDE)
    return total.astype(LOW)


def feed_mid_kernel(at, total, half_got, keep, give_fc, give_proj):
    own = at[CORE] == at[YL]
    keep[:4] = total[:4]
    give_fc[...] = total[4:8]
    mine, other = total[pl.ds(8 + 4 * at[CORE], 4)], half_got[...]
    keep[4:] = jnp.where(own, mine, other)
    give_proj[...] = jnp.where(own, other, mine)


def add_halves_kernel(at, keep, first_half, second_half, out):
    count = first_half.shape[0]
    for k in range(keep.shape[0]):
        half = (first_half, k) if k < count else (second_half, k - count)
        out[k] = (keep[k].astype(WIDE) + half[0][half[1]].astype(WIDE)).astype(LOW)


def split_sum_kernel(at, one, two, *outs):
    place = 0
    for out in outs:
        for k in range(out.shape[0]):
            out[k] = added((one, two), place)
            place += 1


def qkv_x_kernel(at, *refs):
    parts, out_total, sums, (keep, give_one, give_two) = refs[:4], refs[4], refs[5], refs[6:]
    for k in range(3):
        keep[k] = added(parts, k)
        give_one[k] = added(parts, 4 + k)
    keep[3] = sums[0]
    give_one[3] = sums[0]
    keep[4] = added(parts, 3)
    give_two[0] = added(parts, 7)
    for k in range(2):
        keep[5 + k] = out_total[k]
        give_two[1 + k] = out_total[k]


def qkv_y_kernel(at, half, last, own, one, two, three, rest, sums):
    pair = (half, last)
    own[0] = added(pair, 0)
    total = added(pair, 3)
    sums[0] = total
    for out, place in ((one, 1), (two, 2), (three, 4)):
        out[0] = added(pair, place)
        out[1] = total
    for k in range(2):
        rest[k] = added(pair, 5 + k)


def qkv_z_kernel(at, own, sums, one, two, three, rest, out):
    out[0] = own[0]
    total = sums[0].astype(WIDE)
    for k, got in enumerate((one, two, three)):
        out[1 + k] = got[0]
        total = total + got[1].astype(WIDE)
    out[4:6] = rest[...]
    out[6] = total.astype(LOW)


def feed_z_kernel(at, own, one, two, three, rest, out):
    for k, got in enumerate((own, one, two, three)):
        out[k] = got[0]
    out[4:] = rest[...]


def place_feed_kernel(at, mine, other, fc, proj):
    for c in range(2):
        for q in range(4):
            count = PIECE_STEP if q < 3 else PIECE

            def block(k):
                return jnp.where(at[CORE] == c, mine[q, k], other[q, k]).astype(WIDE)

            for z in range(4):
                j = c * 4 + z
                fc[PIECE_STEP * q : PIECE_STEP * q + count, FF_PART * j : FF_PART * (j + 1)] = block(
                    z ^ at[Z]
                )[:count]
            for k in range(4):
                rows = PIECE_STEP if k < 3 else PIECE
                row = SHARD * q + PIECE_STEP * k
                proj[row : row + rows, FF_PART * c : FF_PART * (c + 1)] = block(4 + k)[:rows]


def place_qkv_kernel(at, *refs):
    mine, other, (qkv, out), refs = refs[:4], refs[4:8], refs[8:10], refs[10:]
    vectors, held, scratch = refs[:9], refs[9], refs[10:]
    for k in range(4):
        held[0, k] = mine[k][...]
        held[1, k] = other[k][...]
    own = jnp.where(at[CORE] == at[YL], 0, 1)
    for q in range(4):
        count = PIECE_STEP if q < 3 else PIECE
        rows = slice(PIECE_STEP * q, PIECE_STEP * q + count)
        for c in range(2):
            for z in range(4):
                block = held[c ^ at[CORE], q ^ at[X], z ^ at[Z]].astype(WIDE)
                for start, stop, target in qkv_columns(c * 4 + z):
                    qkv[rows, target : target + stop - start] = block[:count, start:stop]
        for half in range(2):
            block = held[own, q ^ at[X], 4 + half].astype(WIDE)
            out[rows, FF_PART * half : FF_PART * (half + 1)] = block[:count]
    total = held[0, 0, 6].astype(WIDE)
    for core in range(2):
        for k in range(4):
            if core + k:
                total = total + held[core, k, 6].astype(WIDE)
    place_vectors(at, total, *vectors, *scratch)


def place_vectors(at, total, *refs):
    outs, (small, joined) = refs[:9], refs[9:]
    small[...] = total
    for i in range(6):
        row = small[pl.ds(2 * i + at[ME] // 4, 1), :]
        for k in range(4):

            @pl.when(at[ME] % 4 == k)
            def _():
                outs[i][...] = row[:, SHARD * k : SHARD * (k + 1)].reshape(SHARD)

    outs[6][...] = small[pl.ds(16 + at[ME], 1), :].reshape(FF_PART)
    for n in range(2):
        for k in range(8):
            at_row = 24 + 8 * n + k
            joined[:, SPAN * k : SPAN * (k + 1)] = small[at_row : at_row + 1, :SPAN]
        for k in range(8):

            @pl.when(at[ME] == k)
            def _():
                outs[7 + n][...] = joined[:, SHARD * k : SHARD * (k + 1)].reshape(SHARD)


def qkv_columns(j):
    count = min(SPAN, WIDTH - SPAN * j)
    if count <= 0:
        return []
    return [(SPAN * p, SPAN * p + count, WIDTH * p + SPAN * j) for p in range(3)]


def gather_rows(block, *gates, late=()):
    beside = c_swap(block)
    sent = after(block, *gates)
    near = {d: z_swap(sent, d) for d in (1, 3, 2)}
    far = {d: c_swap(after(near[d], *late)) for d in (1, 3, 2)}
    return [block, near[1], near[2], near[3], beside, far[1], far[2], far[3]], list(near.values())


def team_parts(near, far, c_gates=(), z_gates=()):
    got = c_swap(after(far, *c_gates))
    pair = [add([v[ROWS * d : ROWS * (d + 1)] for v in (near, got)]) for d in (1, 2, 3)]
    sent = after(pair, *z_gates)
    came = [z_swap(sent[d - 1], d) for d in (1, 3, 2)]
    return [near, got] + came, sent, came


def z_blocks(own, sends, *gates):
    sends = after(sends, *gates)
    near = {d: z_swap(sends[d], d) for d in (1, 3, 2)}
    near[0] = own
    return near


def far_blocks(near, *gates):
    near = after(near, *gates)
    one, two = jnp.stack([near[0], near[1]]), jnp.stack([near[2], near[3]])
    return [one, two, y_swap(one, 1), y_swap(two, 3)]


def spread_x(value, swap):
    got = [swap(value, d) for d in (1, 3)]
    two = swap(after(value, got), 2)
    return [value, got[0], two, got[1]]


def add(values):
    total = values[0].astype(WIDE)
    for value in values[1:]:
        total = total + value.astype(WIDE)
    return total.astype(LOW)


def local(
    tokens,
    lengths,
    ln1_gain,
    ln1_bias,
    qkv_weight,
    q_bias,
    v_bias,
    out_weight,
    out_bias,
    ln2_gain,
    ln2_bias,
    fc_weight,
    fc_bias,
    proj_weight,
    proj_bias,
    cotangent,
):
    c, x, yl, z = (lax.axis_index(a) for a in ("c", "x", "yl", "z"))
    me, member = yl * 4 + z, c * 4 + z
    at = jnp.stack([me, member, c, x, yl, z]).astype(jnp.int32)

    vectors = [ln1_gain, ln1_bias, q_bias, v_bias, out_bias, ln2_gain, ln2_bias, proj_bias, fc_bias]
    own_tokens = turn(tokens)
    qkv_sends = whole_call_any(
        prepare_qkv_kernel,
        "prepare_qkv",
        [like((CARRY, 3 * SPAN))] * 4,
        [at, qkv_weight],
        vectors,
        scratch=[pltpu.VMEM(v.shape, LOW) for v in vectors] + [pltpu.SemaphoreType.DMA((9,))],
    )
    half = proj_weight.shape[0] // 2
    proj_sends = proj_weight[:half], proj_weight[half:]

    out_half, *fc_sends = whole_call(
        prepare_rest_kernel,
        "prepare_rest",
        [like((CARRY, FF_PART))] * 5,
        at,
        after(fc_weight, qkv_sends),
        out_weight,
    )
    all_tokens, tokens_came = gather_rows(own_tokens)
    qkv_near = z_blocks(qkv_sends[0], qkv_sends, own_tokens)
    other_lengths = c_swap(after(lengths, tokens_came[0]))
    places = at, jnp.where(c == yl, lengths, other_lengths)
    weight_qkv = far_blocks(qkv_near, out_half, fc_sends, places, proj_sends)
    own_cotangent = turn(after(cotangent, own_tokens))
    out_near = z_blocks(out_half, [out_half] * 4, qkv_near, all_tokens, own_cotangent)
    proj_sent = after(proj_sends, weight_qkv, out_near)
    proj_pieces = [
        proj_weight,
        y_swap_some(proj_sent[0], 1, True),
        y_swap_some(proj_sent[1], 3, True),
    ]

    normed_first, qkv, vectors_all, fc_bias_own = first(at, all_tokens, after(weight_qkv, out_near))
    all_cotangent, cotangent_came = gather_rows(own_cotangent, out_near, late=(qkv,))
    qkv = after(qkv, cotangent_came, proj_pieces)
    out_mine = far_blocks(out_near, qkv)
    fc_near = z_blocks(fc_sends[0], fc_sends, qkv)
    mixed_heads, logsum = attend(places, qkv)
    mixed_heads = after(mixed_heads, out_mine, fc_near)
    out_other = [c_swap(after(piece, mixed_heads)) for piece in out_mine]

    mixed_near = mixed_heads[: 4 * ROWS]
    mixed_got = after(c_swap(mixed_heads[4 * ROWS :]), out_other)
    mixed_sent = [
        jnp.concatenate([v[ROWS * d : ROWS * (d + 1)] for v in (mixed_near, mixed_got)], axis=1)
        for d in range(4)
    ]
    mixed_pieces = [mixed_sent[0]] + [z_swap(mixed_sent[d], d) for d in (1, 2, 3)]
    middle, normed_second, mixed = whole_call_any(
        middle_kernel,
        "out_and_second_norm",
        [like((ROWS, WIDTH), WIDE), like((ROWS, WIDTH)), like((ROWS, WIDTH))],
        [at, own_tokens, vectors_all] + mixed_pieces,
        out_mine + out_other,
        scratch=[
            pltpu.VMEM((ROWS, 8 * SPAN), LOW),
            pltpu.VMEM((ROWS, 8 * BLOCK), LOW),
            pltpu.VMEM((ROWS, WIDTH), WIDE),
        ]
        + OUT_WEIGHT_SCRATCH,
    )

    all_second, second_came = gather_rows(normed_second)
    weight_fc = far_blocks(fc_near, normed_second)
    mixed_other = c_swap(after(mixed, second_came))
    hidden, d_hidden_in, d_second_near, d_second_far, fc_bias_sum = feed(
        at, all_second, all_cotangent, weight_fc, proj_pieces, fc_bias_own
    )
    d_second_parts, d_second_sent, d_second_came = team_parts(d_second_near, d_second_far)

    hidden_late = after(hidden, d_second_sent)
    feed_pieces = feed_grad(at, all_second, d_hidden_in, hidden_late, all_cotangent)
    feed_total = lax.psum_scatter(
        after(feed_pieces, d_second_came), "x", scatter_dimension=0, tiled=True
    )

    d_middle, d_branch, second_sums, *d_mixed = second_back(
        at,
        middle,
        own_cotangent,
        after(vectors_all, feed_pieces),
        d_second_parts[0],
        d_second_parts[1],
        d_second_parts[2:],
        out_mine,
        out_other,
    )
    d_got = [d_mixed[0]] + [z_swap(d_mixed[d], d) for d in (1, 2, 3)]
    out_sent = out_grad(at, mixed, mixed_other, d_branch, c_swap(d_branch))
    d_keep = jnp.concatenate([v[:, :SPAN] for v in d_got])
    d_give = jnp.concatenate([v[:, SPAN:] for v in d_got])
    d_mixed_heads = jnp.concatenate([d_keep, c_swap(after(d_give, out_sent))])
    out_late = after(out_sent, d_give)
    out_came = [z_swap(out_late[d], d) for d in (1, 3)]
    d_qkv = attend_back(places, qkv, logsum, d_mixed_heads)
    d_qkv = after(d_qkv, out_came)
    out_came.append(z_swap(after(out_late[2], out_came), 2))

    def blocks_call(body, name, counts, *args):
        outs = [like((count, PIECE, FF_PART)) for count in counts]
        return whole_call(body, name, outs, at, *args)

    qkv_pieces = whole_call(
        qkv_grad_kernel,
        "qkv_grad",
        [like((8, PIECE, FF_PART))] * 4,
        at,
        normed_first,
        d_qkv,
        scratch=[pltpu.VMEM((WIDTH, FF_PART), WIDE)],
        limit=VMEM_LIMIT,
    )
    qkv_got = [x_swap(qkv_pieces[d], d) for d in (1, 3)]
    d_first_near, d_first_far, qkv_sums = first_back(at, after(d_qkv, qkv_pieces), weight_qkv)
    qkv_got.append(x_swap(after(qkv_pieces[2], qkv_got), 2))
    d_first_parts, d_first_sent, d_first_came = team_parts(
        d_first_near, d_first_far, (qkv_got[:2], out_came)
    )
    (out_pieces,) = held_call(
        out_sum_kernel,
        "out_sum",
        [like((8, PIECE, FF_PART))],
        at,
        out_sent[0],
        *out_came,
        scratch=[pltpu.VMEM((CARRY, WIDTH), WIDE)],
    )
    out_total = lax.psum_scatter(out_pieces, "x", scatter_dimension=0, tiled=True)
    feed_total = after(feed_total, d_first_sent)
    half_got = c_swap(lax.dynamic_slice_in_dim(feed_total, 12 - 4 * c, 4, 0))
    feed_keep, give_fc, give_proj = blocks_call(
        feed_mid_kernel, "feed_mid", [8, 4, 4], feed_total, half_got
    )
    feed_y = [y_swap(give_fc, 1), y_swap(give_proj, 3)]
    (feed_half,) = blocks_call(
        add_halves_kernel, "feed_half", [8], after(feed_keep, d_first_came), *feed_y
    )
    feed_last = y_swap(feed_half, 2)
    grad_low, sums = input_back(
        at,
        own_tokens,
        d_middle,
        after(vectors_all, feed_half),
        second_sums,
        fc_bias_sum,
        qkv_sums,
        d_first_parts,
    )
    grad_turned = turn(grad_low)
    input_grad = jnp.transpose(grad_turned.astype(WIDE))

    qkv_keep, give_one, give_two = held_call(
        qkv_x_kernel,
        "qkv_x",
        [like((count, PIECE, FF_PART)) for count in (7, 4, 3)],
        at,
        qkv_pieces[0],
        *qkv_got,
        out_total,
        sums,
    )
    qkv_y = [y_swap(give_one, 1), y_swap(give_two, 3)]
    feed_own, feed_one, feed_two, feed_three, feed_rest = blocks_call(
        split_sum_kernel, "feed_y", [1, 1, 1, 1, 4], after(feed_half, give_one), feed_last
    )
    feed_z = [z_swap(part, d) for d, part in ((1, feed_one), (2, feed_two), (3, feed_three))]
    final_near, final_far = final_part(at, after(hidden, feed_own), proj_pieces)
    (qkv_half,) = blocks_call(add_halves_kernel, "qkv_half", [7], after(qkv_keep, final_far), *qkv_y)
    qkv_last = y_swap(qkv_half, 2)
    (feed_rows,) = blocks_call(
        feed_z_kernel, "feed_z", [8], after(feed_own, qkv_half), *feed_z, feed_rest
    )
    feed_rows = lax.all_gather(feed_rows, "x", axis=0)
    final_parts, final_sent, final_came = team_parts(final_near, after(final_far, qkv_half))
    qkv_own, qkv_one, qkv_two, qkv_three, qkv_rest, sums_total = blocks_call(
        qkv_y_kernel, "qkv_y", [1, 2, 2, 2, 2, 1], after(qkv_half, final_sent, grad_turned), qkv_last
    )
    qkv_z = [z_swap(part, d) for d, part in ((1, qkv_one), (2, qkv_two), (3, qkv_three))]
    (qkv_rows,) = blocks_call(
        qkv_z_kernel, "qkv_z", [7], after(qkv_own, final_came), sums_total, *qkv_z, qkv_rest
    )
    qkv_rows = spread_x(qkv_rows, x_swap)
    (output_low,) = held_call(
        output_kernel,
        "output_rows",
        [like((WIDTH, ROWS))],
        at,
        middle,
        after(vectors_all, qkv_rows[0]),
        *final_parts,
        rows=ROWS,
    )
    output = jnp.transpose(turn(output_low))
    grad_fc, grad_proj = whole_call(
        place_feed_kernel,
        "place_feed",
        [like((SHARD, 8 * FF_PART), WIDE), like((FF_PART, WIDTH), WIDE)],
        at,
        feed_rows,
        c_swap(after(feed_rows, qkv_rows[1], qkv_rows[3])),
        limit=VMEM_LIMIT,
    )
    qkv_other = [c_swap(after(part, output, grad_fc)) for part in qkv_rows]
    vector_shapes = [like((SHARD,), WIDE)] * 6 + [like((FF_PART,), WIDE)]
    vector_shapes += [like((SHARD,), WIDE)] * 2
    grad_qkv, grad_out, *vector_grads = whole_call(
        place_qkv_kernel,
        "place_qkv",
        [like((SHARD, 3 * WIDTH), WIDE), like((SHARD, WIDTH), WIDE)] + vector_shapes,
        at,
        *qkv_rows,
        *qkv_other,
        scratch=[
            pltpu.VMEM((2, 4, 7) + SUMS, LOW),
            pltpu.VMEM(SUMS, WIDE),
            pltpu.VMEM((1, 8 * SPAN), WIDE),
        ],
        limit=VMEM_LIMIT,
    )

    g_gain_one, g_bias_one, g_gain_two, g_bias_two, g_out_b, g_proj_b = vector_grads[:6]
    g_fc_b, g_query_b, g_value_b = vector_grads[6:]

    return (
        output,
        input_grad,
        g_gain_one,
        g_bias_one,
        grad_qkv,
        g_query_b,
        g_value_b,
        grad_out,
        g_out_b,
        g_gain_two,
        g_bias_two,
        grad_fc,
        g_fc_b,
        grad_proj,
        g_proj_b,
    )


def solution(mesh):
    fine = Mesh(mesh.devices.reshape(2, 4, 2, 2, 4), ("yh", "x", "c", "yl", "z"))
    group, owner = ("yh", "x", "c"), ("yl", "z")
    everyone = group + owner
    vector, matrix = P(owner), P(owner, None)
    rows = P(everyone, None)
    return jax.shard_map(
        local,
        mesh=fine,
        in_specs=(
            rows,
            P(group, None),
            vector,
            vector,
            matrix,
            vector,
            vector,
            matrix,
            vector,
            vector,
            vector,
            matrix,
            vector,
            matrix,
            vector,
            rows,
        ),
        out_specs=(
            rows,
            rows,
            vector,
            vector,
            matrix,
            vector,
            vector,
            matrix,
            vector,
            vector,
            vector,
            matrix,
            vector,
            matrix,
            vector,
        ),
        check_vma=False,
    )
```

```python
import jax
import jax.numpy as jnp
from jax import lax
from jax.experimental import pallas as pl
from jax.experimental.pallas import tpu as pltpu
from jax.sharding import Mesh
from jax.sharding import PartitionSpec as P

HEADS = 25
HEAD_DIM = 64
EPSILON = 1e-05
LOW = jnp.bfloat16
WIDE = jnp.float32

TEAM_HEADS = 4
SPAN = TEAM_HEADS * HEAD_DIM
SHARD = 200
BLOCK = 256
CARRY = 208
WIDTH = 1600
LANES = 1664
ROWS = 128
FF_PART = 800
PIECE = 56
PIECE_STEP = 48
VMEM_LIMIT = 60 * 1024 * 1024
SMALL_LIMIT = 24 * 1024 * 1024


def after(value, *others):
    if not jax.tree.leaves(others):
        return value
    return lax.optimization_barrier((value, others))[0]


def z_swap(value, step):
    return lax.ppermute(value, "z", [(i, i ^ step) for i in range(4)])


def x_swap(value, step):
    return lax.ppermute(value, "x", [(i, i ^ step) for i in range(4)])


def y_swap(value, step):
    return lax.ppermute(value, ("yh", "yl"), [(i, i ^ step) for i in range(4)])


def c_swap(value):
    return lax.ppermute(value, "c", [(0, 1), (1, 0)])


def team_swap(value, slot):
    return lax.ppermute(value, ("c", "z"), [(i, i ^ slot) for i in range(8)])


def turn(value):
    return lax.ppermute(value, ("c", "yl"), [(0, 0), (1, 2), (2, 1), (3, 3)])


def y_swap_some(value, step, sender_diagonal):
    pairs = []
    for yh in range(2):
        for c in range(2):
            for yl in range(2):
                if (c == yl) == sender_diagonal:
                    y = (yh * 2 + yl) ^ step
                    pairs.append((yh * 4 + c * 2 + yl, (y // 2) * 4 + c * 2 + y % 2))
    return lax.ppermute(value, ("yh", "c", "yl"), pairs)


def x_swap_diagonal(value, step):
    pairs = []
    for x in range(4):
        for c in range(2):
            pairs.append((x * 4 + c * 3, (x ^ step) * 4 + c * 3))
    return lax.ppermute(value, ("x", "c", "yl"), pairs)


def pick(blocks, index):
    return lax.dynamic_index_in_dim(blocks, index, 0, keepdims=False)


DOWN = (((0,), (0,)), ((), ()))


ME, MEMBER, CORE, X, YL, Z = range(6)

def cost(microseconds):
    return pl.CostEstimate(flops=microseconds * 10**9, bytes_accessed=0, transcendentals=0)


SMEM = pl.BlockSpec(memory_space=pltpu.SMEM)
VMEM = pl.BlockSpec(memory_space=pltpu.VMEM)
ANY = pl.BlockSpec(memory_space=pltpu.HBM)


def like(shape, dtype=LOW):
    return jax.ShapeDtypeStruct(shape, dtype)


def whole_call(body, name, outs, *args, scratch=(), limit=SMALL_LIMIT):
    return pl.pallas_call(
        body,
        in_specs=[SMEM] + [VMEM] * (len(args) - 1),
        out_specs=[VMEM] * len(outs),
        out_shape=list(outs),
        scratch_shapes=list(scratch),
        compiler_params=pltpu.CompilerParams(vmem_limit_bytes=limit),
        cost_estimate=cost(0),
        name=name,
    )(*args)


def held_call(body, name, outs, at, *args, scratch=(), rows=None):
    count, made = len(args), len(outs)
    heights = [a.shape[0] if rows is None else min(rows, a.shape[0]) for a in args]

    def run(at_ref, *refs):
        sources, results, rest = refs[:count], refs[count : count + made], refs[count + made :]
        targets, others, sems = rest[:count], rest[count:-1], rest[-1]
        pairs = [(f.at[pl.ds(0, h)], t) for f, h, t in zip(sources, heights, targets)]
        for copy in load(pairs, sems):
            copy.wait()
        body(at_ref, *targets, *results, *others)

    return pl.pallas_call(
        run,
        in_specs=[SMEM] + [ANY] * count,
        out_specs=[VMEM] * made,
        out_shape=list(outs),
        scratch_shapes=[pltpu.VMEM((h,) + a.shape[1:], a.dtype) for a, h in zip(args, heights)]
        + list(scratch)
        + [pltpu.SemaphoreType.DMA((count,))],
        compiler_params=pltpu.CompilerParams(vmem_limit_bytes=VMEM_LIMIT),
        cost_estimate=cost(0),
        name=name,
    )(at, *args)


def whole_call_any(body, name, outs, args, others, scratch=()):
    return pl.pallas_call(
        body,
        in_specs=[SMEM] + [VMEM] * (len(args) - 1) + [ANY] * len(others),
        out_specs=[VMEM] * len(outs),
        out_shape=list(outs),
        scratch_shapes=list(scratch),
        compiler_params=pltpu.CompilerParams(vmem_limit_bytes=VMEM_LIMIT),
        cost_estimate=cost(0),
        name=name,
    )(*args, *others)


def block_at(index):
    return pl.ds(pl.multiple_of(index * BLOCK, BLOCK), BLOCK)


def to_blocks(source, mine, write):
    lane = lax.broadcasted_iota(jnp.int32, (source.shape[0], BLOCK), 1)
    for s in range(8):
        block = source[:, SHARD * s : SHARD * s + BLOCK]
        write(s ^ mine, jnp.where(lane < SHARD, block, jnp.zeros_like(block)))


def from_blocks(source, mine, target):
    for s in range(8):
        block = source[:, block_at(s ^ mine)]
        target[:, SHARD * s : SHARD * s + SHARD] = block[:, :SHARD].astype(target.dtype)


def prepare_qkv_kernel(at, weight, *refs):
    held, outs, vectors, sems = refs[:9], refs[9:13], refs[13:22], refs[22]
    copies = load(list(zip(held, vectors)), sems)
    for copy in copies:
        copy.wait()
    lane = lax.broadcasted_iota(jnp.int32, (SHARD, SPAN), 1)
    for d, out in enumerate(outs):
        j = at[CORE] * 4 + (at[Z] ^ d)
        valid = lane < WIDTH - SPAN * j
        none = jnp.zeros((SHARD, SPAN), LOW)
        query = weight[:, pl.ds(pl.multiple_of(SPAN * j, SPAN), SPAN)]
        out[:SHARD, :SPAN] = jnp.where(valid, query, none)
        key = weight[:, pl.ds(pl.multiple_of(WIDTH - 64 + SPAN * j, SPAN), SPAN + 128)]
        out[:SHARD, SPAN : 2 * SPAN] = jnp.where(valid, key[:, 64 : 64 + SPAN], none)

        @pl.when(j < 6)
        def _():
            start = pl.multiple_of(2 * WIDTH + SPAN * j, 128)
            out[:SHARD, 2 * SPAN :] = weight[:, pl.ds(start, SPAN)]

        @pl.when(j >= 6)
        def _():
            out[:SHARD, 2 * SPAN :] = none

        @pl.when(j == 6)
        def _():
            out[:SHARD, 2 * SPAN : 2 * SPAN + 64] = weight[:, 3 * WIDTH - 64 :]

        out[SHARD:, :] = jnp.zeros((CARRY - SHARD, 3 * SPAN), LOW)
        for i, vector in enumerate(vectors[:8]):
            out[SHARD + i : SHARD + i + 1, :SHARD] = vector[...].reshape(1, SHARD)
        for i in range(4):
            part = vectors[8][SHARD * i : SHARD * (i + 1)]
            out[SHARD + i : SHARD + i + 1, BLOCK : BLOCK + SHARD] = part.reshape(1, SHARD)


def prepare_rest_kernel(at, fc, outer, out_half, *outs):
    pad = jnp.zeros((CARRY - SHARD, FF_PART), LOW)
    for half in range(2):

        @pl.when(at[CORE] == half)
        def _():
            out_half[:SHARD, :] = outer[:, FF_PART * half : FF_PART * (half + 1)]

    out_half[SHARD:, :] = pad
    for r in range(4):
        start, shift = FF_PART * r // 128 * 128, FF_PART * r % 128
        start = pl.multiple_of(at[CORE] * (4 * FF_PART) + start, 128)
        part = fc[:, pl.ds(start, 896)][:, shift : shift + FF_PART]
        for d, out in enumerate(outs):

            @pl.when((at[Z] ^ d) == r)
            def _():
                out[:SHARD, :] = part
                out[SHARD:, :] = pad


def normalize(inputs):
    average = jnp.mean(inputs, axis=-1, keepdims=True)
    centred = inputs - average
    spread = jnp.mean(centred * centred, axis=-1, keepdims=True)
    inverse = lax.rsqrt(spread + EPSILON)
    return centred * inverse, inverse


def norm_back(d_normed, hat, inverse, gain):
    e = d_normed * gain
    return inverse * (
        e
        - jnp.mean(e, axis=-1, keepdims=True)
        - hat * jnp.mean(e * hat, axis=-1, keepdims=True)
    )


def load(pairs, sems):
    copies = [pltpu.make_async_copy(f, t, sems.at[i]) for i, (f, t) in enumerate(pairs)]
    for copy in copies:
        copy.start()
    return copies


def weight_pairs(pieces, target):
    pairs, k = [], 0
    for piece in pieces:
        for one in [piece] if len(piece.shape) == 2 else [piece.at[0], piece.at[1]]:
            pairs.append((one, target.at[k, pl.ds(0, CARRY)]))
            k += 1
    return pairs


def clear_pad(target):
    target[:, CARRY:, :] = jnp.zeros((8, BLOCK - CARRY, target.shape[2]), LOW)


def first_kernel(at, *refs):
    token_refs, weight_refs, refs = refs[:8], refs[8:12], refs[12:]
    normed, qkv, vectors, fc_bias, tokens, weight, wide, blocks, spread, *sems = refs
    step = pl.program_id(0)

    def token_copy(k):
        target = tokens.at[k ^ at[MEMBER]]
        return pltpu.make_async_copy(token_refs[k], target, sems[1].at[k])

    @pl.when(step == 0)
    def _():
        for k in range(8):
            token_copy(k).start()
        copies = load(weight_pairs(weight_refs, weight), sems[0])
        clear_pad(weight)
        spread[...] = jnp.zeros_like(spread)
        wide[:, WIDTH:] = jnp.zeros((wide.shape[0], wide.shape[1] - WIDTH), LOW)
        for copy in copies:
            copy.wait()
        for k in range(8):
            block = weight[k ^ at[ME], SHARD:CARRY, :BLOCK].astype(WIDE)
            spread[:, SHARD * k : SHARD * (k + 1)] = block[:, :SHARD]
        vectors[...] = spread[:, :WIDTH]
        rows = weight[(at[CORE] ^ at[YL]) * 4, SHARD:CARRY, BLOCK : 2 * BLOCK].astype(WIDE)
        for i in range(4):
            fc_bias[:, SHARD * i : SHARD * (i + 1)] = rows[i : i + 1, :SHARD]
        for k in range(8):
            token_copy(k).wait()

    rows = tokens[pl.ds(step * 2, 2)].reshape(2 * ROWS, WIDTH)
    hat, _ = normalize(rows.astype(WIDE))
    low = (hat * spread[0:1, :WIDTH] + spread[1:2, :WIDTH]).astype(LOW)
    normed[...] = low
    wide[:, :WIDTH] = low

    def write(k, block):
        blocks[:, block_at(k)] = block

    to_blocks(wide, at[ME], write)
    heads = pl.ds(pl.multiple_of(SPAN * at[MEMBER], SPAN), SPAN)
    total = jnp.dot(
        blocks[...], weight[...].reshape(8 * BLOCK, 3 * SPAN), preferred_element_type=WIDE
    )
    qkv[:, :SPAN] = (total[:, :SPAN] + spread[2:3, heads]).astype(LOW)
    qkv[:, SPAN : 2 * SPAN] = total[:, SPAN : 2 * SPAN].astype(LOW)
    qkv[:, 2 * SPAN :] = (total[:, 2 * SPAN :] + spread[3:4, heads]).astype(LOW)


Q_ROWS = 256


def first(at, tokens, weight):
    rows = 8 * ROWS
    still = lambda i: (0, 0)
    down = lambda i: (i, 0)
    return pl.pallas_call(
        first_kernel,
        grid=(rows // Q_ROWS,),
        in_specs=[SMEM] + [ANY] * 12,
        out_specs=[
            pl.BlockSpec((Q_ROWS, WIDTH), down),
            pl.BlockSpec((Q_ROWS, 3 * SPAN), down),
            pl.BlockSpec((8, WIDTH), still),
            pl.BlockSpec((1, FF_PART), still),
        ],
        out_shape=[
            like((rows, WIDTH)),
            like((rows, 3 * SPAN)),
            like((8, WIDTH), WIDE),
            like((1, FF_PART), WIDE),
        ],
        scratch_shapes=[
            pltpu.VMEM((8, ROWS, WIDTH), LOW),
            pltpu.VMEM((8, BLOCK, 3 * SPAN), LOW),
            pltpu.VMEM((Q_ROWS, WIDTH + 192), LOW),
            pltpu.VMEM((Q_ROWS, 8 * BLOCK), LOW),
            pltpu.VMEM((8, 8 * BLOCK), WIDE),
            pltpu.SemaphoreType.DMA((8,)),
            pltpu.SemaphoreType.DMA((8,)),
        ],
        compiler_params=pltpu.CompilerParams(vmem_limit_bytes=VMEM_LIMIT),
        cost_estimate=cost(0),
        name="first_norm_qkv",
    )(at, *tokens, *weight)


def visible(lengths, first_row, rows, keys):
    row = first_row + lax.broadcasted_iota(jnp.int32, (rows, 1), 0)
    key = lax.broadcasted_iota(jnp.int32, (1, keys), 1)
    start = jnp.zeros_like(row)
    bound = 0
    for i in range(3):
        bound = bound + lengths[0, i]
        start = jnp.where(row >= bound, bound, start)
    return (key <= row) & (key >= start)


ACROSS = (((1,), (1,)), ((), ()))


def by_block(body):
    for i in range(8 * ROWS // Q_ROWS):
        pl.when(pl.program_id(0) == i)(lambda i=i: body(i))


def slot_rows(at, chunk):
    return pl.ds(pl.multiple_of((chunk ^ at[MEMBER]) * ROWS, ROWS), ROWS)


def attend_kernel(at, lengths, q_ref, k_ref, v_ref, mixed_ref, logsum_ref):
    def block(i):
        keys = Q_ROWS * (i + 1)
        q, k, v = q_ref[...], k_ref[:keys, :], v_ref[:keys, :]
        allowed = visible(lengths, i * Q_ROWS, Q_ROWS, keys)
        lane = lax.broadcasted_iota(jnp.int32, q.shape, 1) // HEAD_DIM
        slim = lax.broadcasted_iota(jnp.int32, logsum_ref.shape, 1)
        mixed = jnp.zeros(q.shape, WIDE)
        logsums = jnp.zeros(logsum_ref.shape, WIDE)
        for head in range(TEAM_HEADS):
            own = lane == head
            q_own = jnp.where(own, q, jnp.zeros_like(q))
            scores = lax.dot_general(q_own, k, ACROSS, preferred_element_type=WIDE)
            scores = jnp.where(allowed, scores * (HEAD_DIM**-0.5), -1e30)
            top = jnp.max(scores, axis=-1, keepdims=True)
            powers = jnp.exp(scores - top)
            total = jnp.sum(powers, axis=-1, keepdims=True)
            probs = (powers * (1.0 / total)).astype(LOW)
            mixed = jnp.where(own, jnp.dot(probs, v, preferred_element_type=WIDE), mixed)
            logsums = jnp.where(slim == head, top + jnp.log(total), logsums)
        low = mixed.astype(LOW)
        for half in range(Q_ROWS // ROWS):
            rows = slot_rows(at, i * (Q_ROWS // ROWS) + half)
            mixed_ref[rows, :] = low[ROWS * half : ROWS * (half + 1)]
        logsum_ref[...] = logsums

    by_block(block)


def attend_back_kernel(
    at, lengths, q_ref, k_ref, v_ref, logsum_ref, dmix_ref, out_ref, dk_total, dv_total
):
    scale = HEAD_DIM**-0.5

    def block(i):
        keys = Q_ROWS * (i + 1)
        if i == 0:
            dk_total[...] = jnp.zeros_like(dk_total)
            dv_total[...] = jnp.zeros_like(dv_total)
        q, k, v = q_ref[...], k_ref[:keys, :], v_ref[:keys, :]
        count = Q_ROWS // ROWS
        dmix = jnp.concatenate([dmix_ref[slot_rows(at, i * count + n), :] for n in range(count)])
        allowed = visible(lengths, i * Q_ROWS, Q_ROWS, keys)
        lane = lax.broadcasted_iota(jnp.int32, q.shape, 1) // HEAD_DIM
        dq = jnp.zeros(q.shape, WIDE)
        for head in range(TEAM_HEADS):
            own = lane == head
            q_own = jnp.where(own, q, jnp.zeros_like(q))
            dmix_own = jnp.where(own, dmix, jnp.zeros_like(dmix))
            scores = lax.dot_general(q_own, k, ACROSS, preferred_element_type=WIDE) * scale
            scores = jnp.where(allowed, scores, -1e30)
            probs = jnp.exp(scores - logsum_ref[:, head : head + 1])
            d_probs = lax.dot_general(dmix_own, v, ACROSS, preferred_element_type=WIDE)
            term = jnp.sum(probs * d_probs, axis=-1, keepdims=True)
            d_scores = (probs * (d_probs - term)).astype(LOW)
            dq = jnp.where(own, jnp.dot(d_scores, k, preferred_element_type=WIDE), dq)
            dk_total[:keys, :] += lax.dot_general(
                d_scores, q_own, DOWN, preferred_element_type=WIDE
            )
            dv_total[:keys, :] += lax.dot_general(
                probs.astype(LOW), dmix_own, DOWN, preferred_element_type=WIDE
            )
        out_ref[Q_ROWS * i : Q_ROWS * (i + 1), :SPAN] = (dq * scale).astype(LOW)
        if i == 8 * ROWS // Q_ROWS - 1:
            out_ref[:, SPAN : 2 * SPAN] = (dk_total[...] * scale).astype(LOW)
            out_ref[:, 2 * SPAN :] = dv_total[...].astype(LOW)

    by_block(block)


def attend_specs(rows):
    return [
        SMEM,
        SMEM,
        pl.BlockSpec((Q_ROWS, SPAN), lambda i: (i, 0)),
        pl.BlockSpec((rows, SPAN), lambda i: (0, 1)),
        pl.BlockSpec((rows, SPAN), lambda i: (0, 2)),
    ]


def attend(places, qkv):
    rows = qkv.shape[0]
    return pl.pallas_call(
        attend_kernel,
        grid=(rows // Q_ROWS,),
        in_specs=attend_specs(rows),
        out_specs=[
            pl.BlockSpec((rows, SPAN), lambda i: (0, 0)),
            pl.BlockSpec((Q_ROWS, 128), lambda i: (i, 0)),
        ],
        out_shape=[
            jax.ShapeDtypeStruct((rows, SPAN), LOW),
            jax.ShapeDtypeStruct((rows, 128), WIDE),
        ],
        compiler_params=pltpu.CompilerParams(vmem_limit_bytes=VMEM_LIMIT),
        cost_estimate=cost(0),
        name="attend",
    )(*places, qkv, qkv, qkv)


def attend_back(places, qkv, logsum, dmix):
    rows = qkv.shape[0]
    whole = lambda i: (0, 0)
    return pl.pallas_call(
        attend_back_kernel,
        grid=(rows // Q_ROWS,),
        in_specs=attend_specs(rows)
        + [pl.BlockSpec((Q_ROWS, 128), lambda i: (i, 0)), pl.BlockSpec((rows, SPAN), whole)],
        out_specs=pl.BlockSpec((rows, 3 * SPAN), whole),
        out_shape=like((rows, 3 * SPAN)),
        scratch_shapes=[pltpu.VMEM((rows, SPAN), WIDE)] * 2,
        compiler_params=pltpu.CompilerParams(vmem_limit_bytes=VMEM_LIMIT),
        cost_estimate=cost(0),
        name="attend_back",
    )(*places, qkv, qkv, qkv, logsum, dmix)


def middle_kernel(at, tokens, vectors, *refs):
    pieces, mine_refs, other_refs, refs = refs[:4], refs[4:8], refs[8:12], refs[12:]
    middle, normed, mixed_out, mixed, blocks, wide, mine, other, *sems = refs
    copies = load(weight_pairs(mine_refs, mine), sems[0])
    copies += load(weight_pairs(other_refs, other), sems[1])
    clear_pad(mine)
    clear_pad(other)
    for d, piece in enumerate(pieces):
        mixed[:, block_at(d ^ at[MEMBER])] = piece[:, :SPAN]
        mixed[:, block_at((4 + d) ^ at[MEMBER])] = piece[:, SPAN:]

    def write_blocks(k, block):
        blocks[:, block_at(k)] = block

    to_blocks(mixed, at[ME], write_blocks)
    mixed_out[...] = mixed[:, :WIDTH]
    for copy in copies[:8]:
        copy.wait()
    flat = (8 * BLOCK, FF_PART)
    a = jnp.dot(blocks[...], mine[...].reshape(flat), preferred_element_type=WIDE)
    for copy in copies[8:]:
        copy.wait()
    b = jnp.dot(blocks[...], other[...].reshape(flat), preferred_element_type=WIDE)
    wide[:, :FF_PART] = jnp.where(at[CORE] == 0, a, b)
    wide[:, FF_PART:] = jnp.where(at[CORE] == 0, b, a)
    total = tokens[...].astype(WIDE) + wide[...] + vectors[4:5, :]
    middle[...] = total
    hat, _ = normalize(total)
    normed[...] = (hat * vectors[5:6, :] + vectors[6:7, :]).astype(LOW)


OUT_WEIGHT_SCRATCH = [
    pltpu.VMEM((8, BLOCK, FF_PART), LOW),
    pltpu.VMEM((8, BLOCK, FF_PART), LOW),
    pltpu.SemaphoreType.DMA((8,)),
    pltpu.SemaphoreType.DMA((8,)),
]


def proj_pairs(own, first_half, second_half, target):
    rows = FF_PART // 2
    return (
        [(own.at[pl.ds(0, rows)], target.at[pl.ds(0, rows)]), (own.at[pl.ds(rows, rows)], target.at[pl.ds(rows, rows)])],
        [(first_half, target.at[pl.ds(0, rows)]), (second_half, target.at[pl.ds(rows, rows)])],
    )


def load_proj(at, refs, target, sems):
    own, got = proj_pairs(*refs, target)

    @pl.when(at[CORE] == at[YL])
    def _():
        for copy in load(own, sems):
            copy.wait()

    @pl.when(at[CORE] != at[YL])
    def _():
        for copy in load(got, sems):
            copy.wait()


def halves(i):
    return jnp.minimum(i, 1), 0


def late_halves(i):
    return jnp.maximum(i - 2, 0), 0


def write_half(step, near, far, value):
    @pl.when(step < 2)
    def _():
        near[:, :WIDTH] = value
        near[:, WIDTH:] = jnp.zeros((value.shape[0], LANES - WIDTH), LOW)

    @pl.when(step >= 2)
    def _():
        far[:, :WIDTH] = value
        far[:, WIDTH:] = jnp.zeros((value.shape[0], LANES - WIDTH), LOW)


def hidden_back_kernel(at, *refs):
    cot_refs, proj_refs, (d_hidden, cot, proj, *sems) = refs[:8], refs[8:11], refs[11:]
    step = pl.program_id(0)

    def cot_copy(k):
        return pltpu.make_async_copy(cot_refs[k], cot.at[k], sems[0].at[k])

    @pl.when(step == 0)
    def _():
        for k in range(8):
            cot_copy(k).start()
        load_proj(at, proj_refs, proj, sems[1])

    for k in range(8):

        @pl.when(step == k // 2)
        def _():
            cot_copy(k).wait()

    rows = cot[pl.ds(step * 2, 2)].reshape(2 * ROWS, WIDTH)
    d_hidden[...] = lax.dot_general(rows, proj[...], ACROSS, preferred_element_type=WIDE)


def hidden_back(at, cot, proj):
    rows = 8 * ROWS
    return pl.pallas_call(
        hidden_back_kernel,
        grid=(rows // Q_ROWS,),
        in_specs=[SMEM] + [ANY] * 11,
        out_specs=pl.BlockSpec((Q_ROWS, FF_PART), lambda i: (i, 0)),
        out_shape=like((rows, FF_PART), WIDE),
        scratch_shapes=[
            pltpu.VMEM((8, ROWS, WIDTH), LOW),
            pltpu.VMEM((FF_PART, WIDTH), LOW),
            pltpu.SemaphoreType.DMA((8,)),
            pltpu.SemaphoreType.DMA((2,)),
        ],
        compiler_params=pltpu.CompilerParams(vmem_limit_bytes=VMEM_LIMIT),
        cost_estimate=cost(0),
        name="hidden_back",
    )(at, *cot, *proj)


def feed_kernel(at, bias, d_hidden, *refs):
    normed_refs, fc_refs, refs = refs[:8], refs[8:12], refs[12:]
    hidden, d_in, near, far, bias_sum, normed, fc, wide, blocks, tall, back, *sems = refs
    step = pl.program_id(0)

    def normed_copy(k):
        return pltpu.make_async_copy(normed_refs[k], normed.at[k], sems[0].at[k])

    @pl.when(step == 0)
    def _():
        for k in range(2):
            normed_copy(k).start()
        copies = load(weight_pairs(fc_refs, fc), sems[1])
        clear_pad(fc)
        bias_sum[...] = jnp.zeros_like(bias_sum)
        wide[:, WIDTH:] = jnp.zeros((2 * ROWS, wide.shape[1] - WIDTH), LOW)
        for copy in copies:
            copy.wait()

    for k in range(8):

        @pl.when(step == k // 2)
        def _():
            normed_copy(k).wait()

        @pl.when(step + 1 == k // 2)
        def _():
            normed_copy(k).start()

    wide[:, :WIDTH] = normed[pl.ds(step * 2, 2)].reshape(2 * ROWS, WIDTH)

    def write(k, block):
        blocks[:, block_at(k)] = block

    to_blocks(wide, at[ME], write)
    weight = fc[...].reshape(8 * BLOCK, FF_PART)
    u = jnp.dot(blocks[...], weight, preferred_element_type=WIDE) + bias[...]
    factor = (2.0 / jnp.pi) ** 0.5
    square = u * u
    bent = jnp.tanh(factor * (u + 0.044715 * (square * u)))
    half = 0.5 * (1.0 + bent)
    hidden[...] = (u * half).astype(LOW)
    slope = half + (0.5 * factor) * u * (1.0 - bent * bent) * (1.0 + (3 * 0.044715) * square)
    low = (d_hidden[...] * slope).astype(LOW)
    d_in[...] = low
    bias_sum[...] += jnp.sum(low.astype(WIDE), axis=0, keepdims=True)
    tall[...] = lax.dot_general(low, weight, ACROSS, preferred_element_type=WIDE).astype(LOW)
    from_blocks(tall, at[ME], back)
    write_half(step, near, far, back[...])


def feed(at, normed, d_hidden, fc, bias):
    rows = 8 * ROWS
    still = lambda i: (0, 0)
    down = lambda i: (i, 0)
    return pl.pallas_call(
        feed_kernel,
        grid=(rows // Q_ROWS,),
        in_specs=[
            SMEM,
            pl.BlockSpec((1, FF_PART), still),
            pl.BlockSpec((Q_ROWS, FF_PART), down),
        ]
        + [ANY] * 12,
        out_specs=[
            pl.BlockSpec((Q_ROWS, FF_PART), down),
            pl.BlockSpec((Q_ROWS, FF_PART), down),
            pl.BlockSpec((Q_ROWS, LANES), halves),
            pl.BlockSpec((Q_ROWS, LANES), late_halves),
            pl.BlockSpec((1, FF_PART), still),
        ],
        out_shape=[
            like((rows, FF_PART)),
            like((rows, FF_PART)),
            like((rows // 2, LANES)),
            like((rows // 2, LANES)),
            like((1, FF_PART), WIDE),
        ],
        scratch_shapes=[
            pltpu.VMEM((8, ROWS, WIDTH), LOW),
            pltpu.VMEM((8, BLOCK, FF_PART), LOW),
            pltpu.VMEM((Q_ROWS, WIDTH + 192), LOW),
            pltpu.VMEM((Q_ROWS, 8 * BLOCK), LOW),
            pltpu.VMEM((Q_ROWS, 8 * BLOCK), LOW),
            pltpu.VMEM((Q_ROWS, WIDTH), LOW),
            pltpu.SemaphoreType.DMA((8,)),
            pltpu.SemaphoreType.DMA((8,)),
        ],
        compiler_params=pltpu.CompilerParams(vmem_limit_bytes=VMEM_LIMIT),
        cost_estimate=cost(0),
        name="feed_forward_and_back",
    )(at, bias, d_hidden, *normed, *fc)


def final_kernel(at, hidden, *refs):
    proj_refs, (near, far, proj, sems) = refs[:3], refs[3:]
    step = pl.program_id(0)

    @pl.when(step == 0)
    def _():
        load_proj(at, proj_refs, proj, sems)

    total = jnp.dot(hidden[...], proj[...], preferred_element_type=WIDE).astype(LOW)
    write_half(step, near, far, total)


def final_part(at, hidden, proj):
    rows = hidden.shape[0]
    return pl.pallas_call(
        final_kernel,
        grid=(rows // Q_ROWS,),
        in_specs=[SMEM, pl.BlockSpec((Q_ROWS, FF_PART), lambda i: (i, 0))] + [ANY] * 3,
        out_specs=[
            pl.BlockSpec((Q_ROWS, LANES), halves),
            pl.BlockSpec((Q_ROWS, LANES), late_halves),
        ],
        out_shape=[like((rows // 2, LANES))] * 2,
        scratch_shapes=[pltpu.VMEM((FF_PART, WIDTH), LOW), pltpu.SemaphoreType.DMA((2,))],
        compiler_params=pltpu.CompilerParams(vmem_limit_bytes=VMEM_LIMIT),
        cost_estimate=cost(0),
        name="feed_forward_out",
    )(at, hidden, *proj)


def padded_rows():
    return pl.BlockSpec((ROWS, LANES), lambda i: (0, 0))


def team_total(refs):
    total = refs[0][:, :WIDTH].astype(WIDE)
    for ref in refs[1:]:
        total = total + ref[:, :WIDTH].astype(WIDE)
    return total


def row_sum(value):
    return jnp.sum(value, axis=0, keepdims=True)


def output_kernel(at, middle, vectors, near, got, one, two, three, out):
    total = middle[...] + vectors[7:8, :]
    total = total + team_total([near, got, one, two, three])
    out[...] = jnp.transpose(total).astype(LOW)


def out_grad_kernel(at, left, left_other, right, right_other, *refs):
    outs, total = refs[:4], refs[4]
    first_core = at[CORE] == 0

    def half(ref):
        value = ref[...]
        return jnp.where(first_core, value[:, :FF_PART], value[:, FF_PART:])

    total[:FF_PART, :] = lax.dot_general(
        jnp.concatenate([half(left), half(left_other)]),
        jnp.concatenate([right[...], right_other[...]]),
        DOWN,
        preferred_element_type=WIDE,
    )
    for d, out in enumerate(outs):
        start = pl.multiple_of((at[Z] ^ d) * SHARD, 8)
        out[...] = total[pl.ds(start, CARRY), :].astype(LOW)


def out_grad(at, left, left_other, right, right_other):
    return whole_call(
        out_grad_kernel,
        "out_grad",
        [like((CARRY, WIDTH))] * 4,
        at,
        left,
        left_other,
        right,
        right_other,
        scratch=[pltpu.VMEM((FF_PART + CARRY - SHARD, WIDTH), WIDE)],
        limit=VMEM_LIMIT,
    )


def out_sum_kernel(at, own, one, two, three, out, total):
    total[...] = team_total([own, one, two, three])
    for q in range(4):
        piece = total[PIECE_STEP * q : PIECE_STEP * q + PIECE, :].astype(LOW)
        out[2 * q] = piece[:, :FF_PART]
        out[2 * q + 1] = piece[:, FF_PART:]


def second_back_kernel(at, middle, cot, vectors, near, got, *refs):
    parts, mine_refs, other_refs, refs = refs[:3], refs[3:7], refs[7:11], refs[11:]
    (d_middle, d_branch, sums), pieces, refs = refs[:3], refs[3:7], refs[7:]
    wide, tall, narrow, mine, other, *sems = refs
    copies = load(weight_pairs(mine_refs, mine), sems[0])
    copies += load(weight_pairs(other_refs, other), sems[1])
    clear_pad(mine)
    clear_pad(other)
    d_second = team_total([near, got, *parts])
    hat, inverse = normalize(middle[...])
    d_cot = cot[...].astype(WIDE)
    total = d_cot + norm_back(d_second, hat, inverse, vectors[5:6, :])
    d_middle[...] = total
    low = total.astype(LOW)
    d_branch[...] = low
    sums[0:1, :] = row_sum(d_second * hat)
    sums[1:2, :] = row_sum(d_second)
    sums[2:3, :] = row_sum(low.astype(WIDE))
    sums[3:4, :] = row_sum(d_cot)
    sums[4:8, :] = jnp.zeros((4, WIDTH), WIDE)
    wide[...] = low
    left, right = wide[:, :FF_PART], wide[:, FF_PART:]
    first_core = at[CORE] == 0
    flat = (8 * BLOCK, FF_PART)
    across = (((1,), (1,)), ((), ()))
    for copy in copies[:8]:
        copy.wait()
    part = lax.dot_general(
        jnp.where(first_core, left, right),
        mine[...].reshape(flat),
        across,
        preferred_element_type=WIDE,
    )
    for copy in copies[8:]:
        copy.wait()
    tall[...] = part + lax.dot_general(
        jnp.where(first_core, right, left),
        other[...].reshape(flat),
        across,
        preferred_element_type=WIDE,
    )
    narrow[:, WIDTH:] = jnp.zeros((ROWS, 8 * SPAN - WIDTH), LOW)
    from_blocks(tall, at[ME], narrow)
    for d, piece in enumerate(pieces):
        piece[:, :SPAN] = narrow[:, block_at(d ^ at[MEMBER])]
        piece[:, SPAN:] = narrow[:, block_at((4 + d) ^ at[MEMBER])]


def second_back(at, middle, cot, vectors, near, got, parts, mine, other):
    part = pl.BlockSpec((ROWS, WIDTH), lambda i: (0, 0))
    return pl.pallas_call(
        second_back_kernel,
        grid=(1,),
        in_specs=[SMEM, part, part, pl.BlockSpec((8, WIDTH), lambda i: (0, 0))]
        + [padded_rows()] * 5
        + [ANY] * 8,
        out_specs=[VMEM] * 7,
        out_shape=[like((ROWS, WIDTH), WIDE), like((ROWS, WIDTH)), like((8, WIDTH), WIDE)]
        + [like((ROWS, 2 * SPAN))] * 4,
        scratch_shapes=[
            pltpu.VMEM((ROWS, WIDTH), LOW),
            pltpu.VMEM((ROWS, 8 * BLOCK), WIDE),
            pltpu.VMEM((ROWS, 8 * SPAN), LOW),
        ]
        + OUT_WEIGHT_SCRATCH,
        compiler_params=pltpu.CompilerParams(vmem_limit_bytes=VMEM_LIMIT),
        cost_estimate=cost(0),
        name="second_norm_and_out_back",
    )(at, middle, cot, vectors, near, got, *parts, *mine, *other)


def first_back_kernel(at, d_qkv, *refs):
    weight_refs, (near, far, sums, weight, tall, back, sems) = refs[:4], refs[4:]
    step = pl.program_id(0)

    @pl.when(step == 0)
    def _():
        copies = load(weight_pairs(weight_refs, weight), sems)
        clear_pad(weight)
        sums[...] = row_sum(d_qkv[...].astype(WIDE))
        for copy in copies:
            copy.wait()

    rows = jnp.concatenate([d_qkv[slot_rows(at, 2 * step + n), :] for n in range(2)])
    tall[...] = lax.dot_general(
        rows, weight[...].reshape(8 * BLOCK, 3 * SPAN), ACROSS, preferred_element_type=WIDE
    ).astype(LOW)
    from_blocks(tall, at[ME], back)
    write_half(step, near, far, back[...])


def first_back(at, d_qkv, weight):
    rows = d_qkv.shape[0]
    whole = lambda i: (0, 0)
    return pl.pallas_call(
        first_back_kernel,
        grid=(rows // Q_ROWS,),
        in_specs=[SMEM, pl.BlockSpec((rows, 3 * SPAN), whole)] + [ANY] * 4,
        out_specs=[
            pl.BlockSpec((Q_ROWS, LANES), halves),
            pl.BlockSpec((Q_ROWS, LANES), late_halves),
            pl.BlockSpec((1, 3 * SPAN), whole),
        ],
        out_shape=[
            like((rows // 2, LANES)),
            like((rows // 2, LANES)),
            like((1, 3 * SPAN), WIDE),
        ],
        scratch_shapes=[
            pltpu.VMEM((8, BLOCK, 3 * SPAN), LOW),
            pltpu.VMEM((Q_ROWS, 8 * BLOCK), LOW),
            pltpu.VMEM((Q_ROWS, WIDTH), LOW),
            pltpu.SemaphoreType.DMA((8,)),
        ],
        compiler_params=pltpu.CompilerParams(vmem_limit_bytes=VMEM_LIMIT),
        cost_estimate=cost(0),
        name="qkv_back",
    )(at, d_qkv, *weight)


SUMS = (PIECE, FF_PART)


def input_kernel(at, tokens, d_middle, vectors, second_sums, fc_sum, qkv_sum, *refs):
    parts, (grad, sums, held) = refs[:5], refs[5:]
    d_first = team_total(parts)
    hat, inverse = normalize(tokens[...].astype(WIDE))
    total = d_middle[...] + norm_back(d_first, hat, inverse, vectors[0:1, :])
    grad[...] = jnp.transpose(total).astype(LOW)
    held[...] = jnp.zeros(SUMS, WIDE)
    rows = [row_sum(d_first * hat), row_sum(d_first)] + [second_sums[i : i + 1, :] for i in range(4)]
    for i, row in enumerate(rows):
        held[2 * i : 2 * i + 1, :] = row[:, :FF_PART]
        held[2 * i + 1 : 2 * i + 2, :] = row[:, FF_PART:]
    held[pl.ds(16 + at[MEMBER], 1), :] = fc_sum[...]
    held[pl.ds(24 + at[MEMBER], 1), :SPAN] = qkv_sum[:, :SPAN]
    held[pl.ds(32 + at[MEMBER], 1), :SPAN] = qkv_sum[:, 2 * SPAN :]
    sums[0] = held[...].astype(LOW)


def input_back(at, tokens, d_middle, vectors, second_sums, fc_sum, qkv_sum, parts):
    still = lambda i: (0, 0)
    part = pl.BlockSpec((ROWS, WIDTH), still)
    rows = pl.BlockSpec((8, WIDTH), still)
    return pl.pallas_call(
        input_kernel,
        grid=(1,),
        in_specs=[
            SMEM,
            part,
            part,
            rows,
            rows,
            pl.BlockSpec((1, FF_PART), still),
            pl.BlockSpec((1, 3 * SPAN), still),
        ]
        + [padded_rows()] * 5,
        out_specs=[
            pl.BlockSpec((WIDTH, ROWS), still),
            pl.BlockSpec((1,) + SUMS, lambda i: (0, 0, 0)),
        ],
        out_shape=[like((WIDTH, ROWS)), like((1,) + SUMS)],
        scratch_shapes=[pltpu.VMEM(SUMS, WIDE)],
        compiler_params=pltpu.CompilerParams(vmem_limit_bytes=SMALL_LIMIT),
        cost_estimate=cost(0),
        name="first_norm_back",
    )(at, tokens, d_middle, vectors, second_sums, fc_sum, qkv_sum, *parts)


def feed_grad_kernel(at, hidden, d_in, *refs):
    cot_refs, normed_refs, (out, normed, cot, total, tall, *sems) = refs[:8], refs[8:16], refs[16:]
    pairs = [(normed_refs[k], normed.at[k]) for k in range(8)]
    first_copies = load(pairs, sems[0])
    pairs = [(cot_refs[k], cot.at[k]) for k in range(8)]
    second_copies = load(pairs, sems[1])
    for copy in first_copies:
        copy.wait()
    total[...] = lax.dot_general(
        normed[...].reshape(8 * ROWS, WIDTH), d_in[...], DOWN, preferred_element_type=WIDE
    )
    for k in range(8):
        for q in range(4):
            start = pl.multiple_of((k ^ at[ME]) * SHARD + PIECE_STEP * q, 8)
            out[16 * q + k] = total[pl.ds(start, PIECE), :].astype(LOW)
    for copy in second_copies:
        copy.wait()
    tall[...] = lax.dot_general(
        hidden[...], cot[...].reshape(8 * ROWS, WIDTH), DOWN, preferred_element_type=WIDE
    )
    for q in range(4):
        for half in range(2):
            lanes = slice(FF_PART * half, FF_PART * (half + 1))
            for k in range(4):
                start = SHARD * q + PIECE_STEP * k
                out[16 * q + 8 + 4 * half + k] = tall[start : start + PIECE, lanes].astype(LOW)


def feed_grad(at, normed, d_in, hidden, cot):
    rows = 8 * ROWS
    return pl.pallas_call(
        feed_grad_kernel,
        in_specs=[SMEM, VMEM, VMEM] + [ANY] * 16,
        out_specs=VMEM,
        out_shape=like((64, PIECE, FF_PART)),
        scratch_shapes=[
            pltpu.VMEM((8, ROWS, WIDTH), LOW),
            pltpu.VMEM((8, ROWS, WIDTH), LOW),
            pltpu.VMEM((WIDTH, FF_PART), WIDE),
            pltpu.VMEM((FF_PART, WIDTH), WIDE),
            pltpu.SemaphoreType.DMA((8,)),
            pltpu.SemaphoreType.DMA((8,)),
        ],
        compiler_params=pltpu.CompilerParams(vmem_limit_bytes=VMEM_LIMIT),
        cost_estimate=cost(0),
        name="feed_forward_grad",
    )(at, hidden, d_in, *cot, *normed)


def qkv_grad_kernel(at, normed, d_qkv, *refs):
    outs, total = refs[:4], refs[4]
    total[:, 3 * SPAN :] = jnp.zeros((WIDTH, FF_PART - 3 * SPAN), WIDE)
    total[:, : 3 * SPAN] = lax.dot_general(
        normed[...], d_qkv[...], DOWN, preferred_element_type=WIDE
    )
    for d, out in enumerate(outs):
        place = pl.multiple_of((at[X] ^ d) * PIECE_STEP, 8)
        for k in range(8):
            start = pl.multiple_of((k ^ at[ME]) * SHARD + place, 8)
            out[k] = total[pl.ds(start, PIECE), :].astype(LOW)


def added(refs, k):
    total = refs[0][k].astype(WIDE)
    for ref in refs[1:]:
        total = total + ref[k].astype(WIDE)
    return total.astype(LOW)


def feed_mid_kernel(at, total, half_got, keep, give_fc, give_proj):
    own = at[CORE] == at[YL]
    keep[:4] = total[:4]
    give_fc[...] = total[4:8]
    mine, other = total[pl.ds(8 + 4 * at[CORE], 4)], half_got[...]
    keep[4:] = jnp.where(own, mine, other)
    give_proj[...] = jnp.where(own, other, mine)


def add_halves_kernel(at, keep, first_half, second_half, out):
    count = first_half.shape[0]
    for k in range(keep.shape[0]):
        half = (first_half, k) if k < count else (second_half, k - count)
        out[k] = (keep[k].astype(WIDE) + half[0][half[1]].astype(WIDE)).astype(LOW)


def split_sum_kernel(at, one, two, *outs):
    place = 0
    for out in outs:
        for k in range(out.shape[0]):
            out[k] = added((one, two), place)
            place += 1


def qkv_x_kernel(at, *refs):
    parts, out_total, sums, (keep, give_one, give_two) = refs[:4], refs[4], refs[5], refs[6:]
    for k in range(3):
        keep[k] = added(parts, k)
        give_one[k] = added(parts, 4 + k)
    keep[3] = sums[0]
    give_one[3] = sums[0]
    keep[4] = added(parts, 3)
    give_two[0] = added(parts, 7)
    for k in range(2):
        keep[5 + k] = out_total[k]
        give_two[1 + k] = out_total[k]


def qkv_y_kernel(at, half, last, own, one, two, three, rest, sums):
    pair = (half, last)
    own[0] = added(pair, 0)
    total = added(pair, 3)
    sums[0] = total
    for out, place in ((one, 1), (two, 2), (three, 4)):
        out[0] = added(pair, place)
        out[1] = total
    for k in range(2):
        rest[k] = added(pair, 5 + k)


def qkv_z_kernel(at, own, sums, one, two, three, rest, out):
    out[0] = own[0]
    total = sums[0].astype(WIDE)
    for k, got in enumerate((one, two, three)):
        out[1 + k] = got[0]
        total = total + got[1].astype(WIDE)
    out[4:6] = rest[...]
    out[6] = total.astype(LOW)


def feed_z_kernel(at, own, one, two, three, rest, out):
    for k, got in enumerate((own, one, two, three)):
        out[k] = got[0]
    out[4:] = rest[...]


def place_feed_kernel(at, mine, other, fc, proj):
    for c in range(2):
        for q in range(4):
            count = PIECE_STEP if q < 3 else PIECE

            def block(k):
                return jnp.where(at[CORE] == c, mine[q, k], other[q, k]).astype(WIDE)

            for z in range(4):
                j = c * 4 + z
                fc[PIECE_STEP * q : PIECE_STEP * q + count, FF_PART * j : FF_PART * (j + 1)] = block(
                    z ^ at[Z]
                )[:count]
            for k in range(4):
                rows = PIECE_STEP if k < 3 else PIECE
                row = SHARD * q + PIECE_STEP * k
                proj[row : row + rows, FF_PART * c : FF_PART * (c + 1)] = block(4 + k)[:rows]


def place_qkv_kernel(at, *refs):
    mine, other, (qkv, out), refs = refs[:4], refs[4:8], refs[8:10], refs[10:]
    vectors, held, scratch = refs[:9], refs[9], refs[10:]
    for k in range(4):
        held[0, k] = mine[k][...]
        held[1, k] = other[k][...]
    own = jnp.where(at[CORE] == at[YL], 0, 1)
    for q in range(4):
        count = PIECE_STEP if q < 3 else PIECE
        rows = slice(PIECE_STEP * q, PIECE_STEP * q + count)
        for c in range(2):
            for z in range(4):
                block = held[c ^ at[CORE], q ^ at[X], z ^ at[Z]].astype(WIDE)
                for start, stop, target in qkv_columns(c * 4 + z):
                    qkv[rows, target : target + stop - start] = block[:count, start:stop]
        for half in range(2):
            block = held[own, q ^ at[X], 4 + half].astype(WIDE)
            out[rows, FF_PART * half : FF_PART * (half + 1)] = block[:count]
    total = held[0, 0, 6].astype(WIDE)
    for core in range(2):
        for k in range(4):
            if core + k:
                total = total + held[core, k, 6].astype(WIDE)
    place_vectors(at, total, *vectors, *scratch)


def place_vectors(at, total, *refs):
    outs, (small, joined) = refs[:9], refs[9:]
    small[...] = total
    for i in range(6):
        row = small[pl.ds(2 * i + at[ME] // 4, 1), :]
        for k in range(4):

            @pl.when(at[ME] % 4 == k)
            def _():
                outs[i][...] = row[:, SHARD * k : SHARD * (k + 1)].reshape(SHARD)

    outs[6][...] = small[pl.ds(16 + at[ME], 1), :].reshape(FF_PART)
    for n in range(2):
        for k in range(8):
            at_row = 24 + 8 * n + k
            joined[:, SPAN * k : SPAN * (k + 1)] = small[at_row : at_row + 1, :SPAN]
        for k in range(8):

            @pl.when(at[ME] == k)
            def _():
                outs[7 + n][...] = joined[:, SHARD * k : SHARD * (k + 1)].reshape(SHARD)


def qkv_columns(j):
    count = min(SPAN, WIDTH - SPAN * j)
    if count <= 0:
        return []
    return [(SPAN * p, SPAN * p + count, WIDTH * p + SPAN * j) for p in range(3)]


def gather_rows(block, *gates, late=()):
    beside = c_swap(block)
    sent = after(block, *gates)
    near = {d: z_swap(sent, d) for d in (1, 3, 2)}
    far = {d: c_swap(after(near[d], *late)) for d in (1, 3, 2)}
    return [block, near[1], near[2], near[3], beside, far[1], far[2], far[3]], list(near.values())


def team_parts(near, far, c_gates=(), z_gates=()):
    got = c_swap(after(far, *c_gates))
    pair = [add([v[ROWS * d : ROWS * (d + 1)] for v in (near, got)]) for d in (1, 2, 3)]
    sent = after(pair, *z_gates)
    came = [z_swap(sent[d - 1], d) for d in (1, 3, 2)]
    return [near, got] + came, sent, came


def z_blocks(own, sends, *gates):
    sends = after(sends, *gates)
    near = {d: z_swap(sends[d], d) for d in (1, 3, 2)}
    near[0] = own
    return near


def far_blocks(near, *gates):
    near = after(near, *gates)
    one, two = jnp.stack([near[0], near[1]]), jnp.stack([near[2], near[3]])
    return [one, two, y_swap(one, 1), y_swap(two, 3)]


def spread_x(value, swap):
    got = [swap(value, d) for d in (1, 3)]
    two = swap(after(value, got), 2)
    return [value, got[0], two, got[1]]


def add(values):
    total = values[0].astype(WIDE)
    for value in values[1:]:
        total = total + value.astype(WIDE)
    return total.astype(LOW)


def local(
    tokens,
    lengths,
    ln1_gain,
    ln1_bias,
    qkv_weight,
    q_bias,
    v_bias,
    out_weight,
    out_bias,
    ln2_gain,
    ln2_bias,
    fc_weight,
    fc_bias,
    proj_weight,
    proj_bias,
    cotangent,
):
    c, x, yl, z = (lax.axis_index(a) for a in ("c", "x", "yl", "z"))
    me, member = yl * 4 + z, c * 4 + z
    at = jnp.stack([me, member, c, x, yl, z]).astype(jnp.int32)

    vectors = [ln1_gain, ln1_bias, q_bias, v_bias, out_bias, ln2_gain, ln2_bias, proj_bias, fc_bias]
    own_tokens = turn(tokens)
    qkv_sends = whole_call_any(
        prepare_qkv_kernel,
        "prepare_qkv",
        [like((CARRY, 3 * SPAN))] * 4,
        [at, qkv_weight],
        vectors,
        scratch=[pltpu.VMEM(v.shape, LOW) for v in vectors] + [pltpu.SemaphoreType.DMA((9,))],
    )
    half = proj_weight.shape[0] // 2
    proj_sends = proj_weight[:half], proj_weight[half:]

    out_half, *fc_sends = whole_call(
        prepare_rest_kernel,
        "prepare_rest",
        [like((CARRY, FF_PART))] * 5,
        at,
        after(fc_weight, qkv_sends),
        out_weight,
    )
    all_tokens, tokens_came = gather_rows(own_tokens)
    qkv_near = z_blocks(qkv_sends[0], qkv_sends, own_tokens)
    other_lengths = c_swap(after(lengths, tokens_came[0]))
    places = at, jnp.where(c == yl, lengths, other_lengths)
    weight_qkv = far_blocks(qkv_near, out_half, fc_sends, places, proj_sends)
    own_cotangent = turn(after(cotangent, own_tokens))
    out_near = z_blocks(out_half, [out_half] * 4, qkv_near, all_tokens, own_cotangent)
    proj_sent = after(proj_sends, weight_qkv, out_near)
    proj_pieces = [
        proj_weight,
        y_swap_some(proj_sent[0], 1, True),
        y_swap_some(proj_sent[1], 3, True),
    ]

    normed_first, qkv, vectors_all, fc_bias_own = first(at, all_tokens, after(weight_qkv, out_near))
    all_cotangent, cotangent_came = gather_rows(own_cotangent, out_near, late=(qkv,))
    qkv = after(qkv, cotangent_came, proj_pieces)
    out_mine = far_blocks(out_near, qkv)
    fc_near = z_blocks(fc_sends[0], fc_sends, qkv)
    mixed_heads, logsum = attend(places, qkv)
    mixed_heads = after(mixed_heads, out_mine, fc_near)
    out_other = [c_swap(after(piece, mixed_heads)) for piece in out_mine]

    mixed_near = mixed_heads[: 4 * ROWS]
    mixed_got = after(c_swap(mixed_heads[4 * ROWS :]), out_other)
    mixed_sent = [
        jnp.concatenate([v[ROWS * d : ROWS * (d + 1)] for v in (mixed_near, mixed_got)], axis=1)
        for d in range(4)
    ]
    mixed_pieces = [mixed_sent[0]] + [z_swap(mixed_sent[d], d) for d in (1, 2, 3)]
    middle, normed_second, mixed = whole_call_any(
        middle_kernel,
        "out_and_second_norm",
        [like((ROWS, WIDTH), WIDE), like((ROWS, WIDTH)), like((ROWS, WIDTH))],
        [at, own_tokens, vectors_all] + mixed_pieces,
        out_mine + out_other,
        scratch=[
            pltpu.VMEM((ROWS, 8 * SPAN), LOW),
            pltpu.VMEM((ROWS, 8 * BLOCK), LOW),
            pltpu.VMEM((ROWS, WIDTH), WIDE),
        ]
        + OUT_WEIGHT_SCRATCH,
    )

    d_hidden = hidden_back(at, after(all_cotangent, normed_second), proj_pieces)
    all_second, second_came = gather_rows(normed_second, late=(d_hidden,))
    weight_fc = far_blocks(fc_near, normed_second)
    mixed_other = c_swap(after(mixed, second_came))
    hidden, d_hidden_in, d_second_near, d_second_far, fc_bias_sum = feed(
        at, all_second, d_hidden, weight_fc, fc_bias_own
    )
    d_second_parts, d_second_sent, d_second_came = team_parts(d_second_near, d_second_far)

    hidden_late = after(hidden, d_second_sent)
    feed_pieces = feed_grad(at, all_second, d_hidden_in, hidden_late, all_cotangent)
    feed_total = lax.psum_scatter(
        after(feed_pieces, d_second_came), "x", scatter_dimension=0, tiled=True
    )

    d_middle, d_branch, second_sums, *d_mixed = second_back(
        at,
        middle,
        own_cotangent,
        after(vectors_all, feed_pieces),
        d_second_parts[0],
        d_second_parts[1],
        d_second_parts[2:],
        out_mine,
        out_other,
    )
    d_got = [d_mixed[0]] + [z_swap(d_mixed[d], d) for d in (1, 2, 3)]
    out_sent = out_grad(at, mixed, mixed_other, d_branch, c_swap(d_branch))
    d_keep = jnp.concatenate([v[:, :SPAN] for v in d_got])
    d_give = jnp.concatenate([v[:, SPAN:] for v in d_got])
    d_mixed_heads = jnp.concatenate([d_keep, c_swap(after(d_give, out_sent))])
    out_late = after(out_sent, d_give)
    out_came = [z_swap(out_late[d], d) for d in (1, 3)]
    d_qkv = attend_back(places, qkv, logsum, d_mixed_heads)
    d_qkv = after(d_qkv, out_came)
    out_came.append(z_swap(after(out_late[2], out_came), 2))

    def blocks_call(body, name, counts, *args):
        outs = [like((count, PIECE, FF_PART)) for count in counts]
        return whole_call(body, name, outs, at, *args)

    qkv_pieces = whole_call(
        qkv_grad_kernel,
        "qkv_grad",
        [like((8, PIECE, FF_PART))] * 4,
        at,
        normed_first,
        d_qkv,
        scratch=[pltpu.VMEM((WIDTH, FF_PART), WIDE)],
        limit=VMEM_LIMIT,
    )
    qkv_got = [x_swap(qkv_pieces[d], d) for d in (1, 3)]
    d_first_near, d_first_far, qkv_sums = first_back(at, after(d_qkv, qkv_pieces), weight_qkv)
    qkv_got.append(x_swap(after(qkv_pieces[2], qkv_got), 2))
    d_first_parts, d_first_sent, d_first_came = team_parts(
        d_first_near, d_first_far, (qkv_got[:2], out_came)
    )
    (out_pieces,) = held_call(
        out_sum_kernel,
        "out_sum",
        [like((8, PIECE, FF_PART))],
        at,
        out_sent[0],
        *out_came,
        scratch=[pltpu.VMEM((CARRY, WIDTH), WIDE)],
    )
    out_total = lax.psum_scatter(out_pieces, "x", scatter_dimension=0, tiled=True)
    feed_total = after(feed_total, d_first_sent)
    half_got = c_swap(lax.dynamic_slice_in_dim(feed_total, 12 - 4 * c, 4, 0))
    feed_keep, give_fc, give_proj = blocks_call(
        feed_mid_kernel, "feed_mid", [8, 4, 4], feed_total, half_got
    )
    feed_y = [y_swap(give_fc, 1), y_swap(give_proj, 3)]
    (feed_half,) = blocks_call(
        add_halves_kernel, "feed_half", [8], after(feed_keep, d_first_came), *feed_y
    )
    feed_last = y_swap(feed_half, 2)
    grad_low, sums = input_back(
        at,
        own_tokens,
        d_middle,
        after(vectors_all, feed_half),
        second_sums,
        fc_bias_sum,
        qkv_sums,
        d_first_parts,
    )
    grad_turned = turn(grad_low)
    input_grad = jnp.transpose(grad_turned.astype(WIDE))

    qkv_keep, give_one, give_two = held_call(
        qkv_x_kernel,
        "qkv_x",
        [like((count, PIECE, FF_PART)) for count in (7, 4, 3)],
        at,
        qkv_pieces[0],
        *qkv_got,
        out_total,
        sums,
    )
    qkv_y = [y_swap(give_one, 1), y_swap(give_two, 3)]
    feed_own, feed_one, feed_two, feed_three, feed_rest = blocks_call(
        split_sum_kernel, "feed_y", [1, 1, 1, 1, 4], after(feed_half, give_one), feed_last
    )
    feed_z = [z_swap(part, d) for d, part in ((1, feed_one), (2, feed_two), (3, feed_three))]
    final_near, final_far = final_part(at, after(hidden, feed_own), proj_pieces)
    (qkv_half,) = blocks_call(add_halves_kernel, "qkv_half", [7], after(qkv_keep, final_far), *qkv_y)
    qkv_last = y_swap(qkv_half, 2)
    (feed_rows,) = blocks_call(
        feed_z_kernel, "feed_z", [8], after(feed_own, qkv_half), *feed_z, feed_rest
    )
    feed_rows = lax.all_gather(feed_rows, "x", axis=0)
    final_parts, final_sent, final_came = team_parts(final_near, after(final_far, qkv_half))
    qkv_own, qkv_one, qkv_two, qkv_three, qkv_rest, sums_total = blocks_call(
        qkv_y_kernel, "qkv_y", [1, 2, 2, 2, 2, 1], after(qkv_half, final_sent, grad_turned), qkv_last
    )
    qkv_z = [z_swap(part, d) for d, part in ((1, qkv_one), (2, qkv_two), (3, qkv_three))]
    (qkv_rows,) = blocks_call(
        qkv_z_kernel, "qkv_z", [7], after(qkv_own, final_came), sums_total, *qkv_z, qkv_rest
    )
    qkv_rows = spread_x(qkv_rows, x_swap)
    (output_low,) = held_call(
        output_kernel,
        "output_rows",
        [like((WIDTH, ROWS))],
        at,
        middle,
        after(vectors_all, qkv_rows[0]),
        *final_parts,
        rows=ROWS,
    )
    output = jnp.transpose(turn(output_low))
    grad_fc, grad_proj = whole_call(
        place_feed_kernel,
        "place_feed",
        [like((SHARD, 8 * FF_PART), WIDE), like((FF_PART, WIDTH), WIDE)],
        at,
        feed_rows,
        c_swap(after(feed_rows, qkv_rows[1], qkv_rows[3])),
        limit=VMEM_LIMIT,
    )
    qkv_other = [c_swap(after(part, output, grad_fc)) for part in qkv_rows]
    vector_shapes = [like((SHARD,), WIDE)] * 6 + [like((FF_PART,), WIDE)]
    vector_shapes += [like((SHARD,), WIDE)] * 2
    grad_qkv, grad_out, *vector_grads = whole_call(
        place_qkv_kernel,
        "place_qkv",
        [like((SHARD, 3 * WIDTH), WIDE), like((SHARD, WIDTH), WIDE)] + vector_shapes,
        at,
        *qkv_rows,
        *qkv_other,
        scratch=[
            pltpu.VMEM((2, 4, 7) + SUMS, LOW),
            pltpu.VMEM(SUMS, WIDE),
            pltpu.VMEM((1, 8 * SPAN), WIDE),
        ],
        limit=VMEM_LIMIT,
    )

    g_gain_one, g_bias_one, g_gain_two, g_bias_two, g_out_b, g_proj_b = vector_grads[:6]
    g_fc_b, g_query_b, g_value_b = vector_grads[6:]

    return (
        output,
        input_grad,
        g_gain_one,
        g_bias_one,
        grad_qkv,
        g_query_b,
        g_value_b,
        grad_out,
        g_out_b,
        g_gain_two,
        g_bias_two,
        grad_fc,
        g_fc_b,
        grad_proj,
        g_proj_b,
    )


def solution(mesh):
    fine = Mesh(mesh.devices.reshape(2, 4, 2, 2, 4), ("yh", "x", "c", "yl", "z"))
    group, owner = ("yh", "x", "c"), ("yl", "z")
    everyone = group + owner
    vector, matrix = P(owner), P(owner, None)
    rows = P(everyone, None)
    return jax.shard_map(
        local,
        mesh=fine,
        in_specs=(
            rows,
            P(group, None),
            vector,
            vector,
            matrix,
            vector,
            vector,
            matrix,
            vector,
            vector,
            vector,
            matrix,
            vector,
            matrix,
            vector,
            rows,
        ),
        out_specs=(
            rows,
            rows,
            vector,
            vector,
            matrix,
            vector,
            vector,
            matrix,
            vector,
            vector,
            vector,
            matrix,
            vector,
            matrix,
            vector,
        ),
        check_vma=False,
    )
```

```python
import jax
import jax.numpy as jnp
from jax import lax
from jax.experimental import pallas as pl
from jax.experimental.pallas import tpu as pltpu
from jax.sharding import Mesh
from jax.sharding import PartitionSpec as P

HEADS = 25
HEAD_DIM = 64
EPSILON = 1e-05
LOW = jnp.bfloat16
WIDE = jnp.float32

TEAM_HEADS = 4
SPAN = TEAM_HEADS * HEAD_DIM
SHARD = 200
BLOCK = 256
CARRY = 208
WIDTH = 1600
LANES = 1664
ROWS = 128
FF_PART = 800
PIECE = 56
PIECE_STEP = 48
VMEM_LIMIT = 60 * 1024 * 1024
SMALL_LIMIT = 24 * 1024 * 1024


def after(value, *others):
    if not jax.tree.leaves(others):
        return value
    return lax.optimization_barrier((value, others))[0]


def z_swap(value, step):
    return lax.ppermute(value, "z", [(i, i ^ step) for i in range(4)])


def x_swap(value, step):
    return lax.ppermute(value, "x", [(i, i ^ step) for i in range(4)])


def y_swap(value, step):
    return lax.ppermute(value, ("yh", "yl"), [(i, i ^ step) for i in range(4)])


def c_swap(value):
    return lax.ppermute(value, "c", [(0, 1), (1, 0)])


def team_swap(value, slot):
    return lax.ppermute(value, ("c", "z"), [(i, i ^ slot) for i in range(8)])


def turn(value):
    return lax.ppermute(value, ("c", "yl"), [(0, 0), (1, 2), (2, 1), (3, 3)])


def y_swap_some(value, step, sender_diagonal):
    pairs = []
    for yh in range(2):
        for c in range(2):
            for yl in range(2):
                if (c == yl) == sender_diagonal:
                    y = (yh * 2 + yl) ^ step
                    pairs.append((yh * 4 + c * 2 + yl, (y // 2) * 4 + c * 2 + y % 2))
    return lax.ppermute(value, ("yh", "c", "yl"), pairs)


def x_swap_diagonal(value, step):
    pairs = []
    for x in range(4):
        for c in range(2):
            pairs.append((x * 4 + c * 3, (x ^ step) * 4 + c * 3))
    return lax.ppermute(value, ("x", "c", "yl"), pairs)


def pick(blocks, index):
    return lax.dynamic_index_in_dim(blocks, index, 0, keepdims=False)


DOWN = (((0,), (0,)), ((), ()))


ME, MEMBER, CORE, X, YL, Z = range(6)

def cost(microseconds):
    return pl.CostEstimate(flops=microseconds * 10**9, bytes_accessed=0, transcendentals=0)


SMEM = pl.BlockSpec(memory_space=pltpu.SMEM)
VMEM = pl.BlockSpec(memory_space=pltpu.VMEM)
ANY = pl.BlockSpec(memory_space=pltpu.HBM)


def like(shape, dtype=LOW):
    return jax.ShapeDtypeStruct(shape, dtype)


def whole_call(body, name, outs, *args, scratch=(), limit=SMALL_LIMIT):
    return pl.pallas_call(
        body,
        in_specs=[SMEM] + [VMEM] * (len(args) - 1),
        out_specs=[VMEM] * len(outs),
        out_shape=list(outs),
        scratch_shapes=list(scratch),
        compiler_params=pltpu.CompilerParams(vmem_limit_bytes=limit),
        cost_estimate=cost(0),
        name=name,
    )(*args)


def held_call(body, name, outs, at, *args, scratch=(), rows=None):
    count, made = len(args), len(outs)
    heights = [a.shape[0] if rows is None else min(rows, a.shape[0]) for a in args]

    def run(at_ref, *refs):
        sources, results, rest = refs[:count], refs[count : count + made], refs[count + made :]
        targets, others, sems = rest[:count], rest[count:-1], rest[-1]
        pairs = [(f.at[pl.ds(0, h)], t) for f, h, t in zip(sources, heights, targets)]
        for copy in load(pairs, sems):
            copy.wait()
        body(at_ref, *targets, *results, *others)

    return pl.pallas_call(
        run,
        in_specs=[SMEM] + [ANY] * count,
        out_specs=[VMEM] * made,
        out_shape=list(outs),
        scratch_shapes=[pltpu.VMEM((h,) + a.shape[1:], a.dtype) for a, h in zip(args, heights)]
        + list(scratch)
        + [pltpu.SemaphoreType.DMA((count,))],
        compiler_params=pltpu.CompilerParams(vmem_limit_bytes=VMEM_LIMIT),
        cost_estimate=cost(0),
        name=name,
    )(at, *args)


def whole_call_any(body, name, outs, args, others, scratch=()):
    return pl.pallas_call(
        body,
        in_specs=[SMEM] + [VMEM] * (len(args) - 1) + [ANY] * len(others),
        out_specs=[VMEM] * len(outs),
        out_shape=list(outs),
        scratch_shapes=list(scratch),
        compiler_params=pltpu.CompilerParams(vmem_limit_bytes=VMEM_LIMIT),
        cost_estimate=cost(0),
        name=name,
    )(*args, *others)


def block_at(index):
    return pl.ds(pl.multiple_of(index * BLOCK, BLOCK), BLOCK)


def to_blocks(source, mine, write):
    lane = lax.broadcasted_iota(jnp.int32, (source.shape[0], BLOCK), 1)
    for s in range(8):
        block = source[:, SHARD * s : SHARD * s + BLOCK]
        write(s ^ mine, jnp.where(lane < SHARD, block, jnp.zeros_like(block)))


def from_blocks(source, mine, target):
    for s in range(8):
        block = source[:, block_at(s ^ mine)]
        target[:, SHARD * s : SHARD * s + SHARD] = block[:, :SHARD].astype(target.dtype)


def prepare_qkv_kernel(at, weight, *refs):
    held, outs, vectors, sems = refs[:9], refs[9:13], refs[13:22], refs[22]
    copies = load(list(zip(held, vectors)), sems)
    for copy in copies:
        copy.wait()
    lane = lax.broadcasted_iota(jnp.int32, (SHARD, SPAN), 1)
    for d, out in enumerate(outs):
        j = at[CORE] * 4 + (at[Z] ^ d)
        valid = lane < WIDTH - SPAN * j
        none = jnp.zeros((SHARD, SPAN), LOW)
        query = weight[:, pl.ds(pl.multiple_of(SPAN * j, SPAN), SPAN)]
        out[:SHARD, :SPAN] = jnp.where(valid, query, none)
        key = weight[:, pl.ds(pl.multiple_of(WIDTH - 64 + SPAN * j, SPAN), SPAN + 128)]
        out[:SHARD, SPAN : 2 * SPAN] = jnp.where(valid, key[:, 64 : 64 + SPAN], none)

        @pl.when(j < 6)
        def _():
            start = pl.multiple_of(2 * WIDTH + SPAN * j, 128)
            out[:SHARD, 2 * SPAN :] = weight[:, pl.ds(start, SPAN)]

        @pl.when(j >= 6)
        def _():
            out[:SHARD, 2 * SPAN :] = none

        @pl.when(j == 6)
        def _():
            out[:SHARD, 2 * SPAN : 2 * SPAN + 64] = weight[:, 3 * WIDTH - 64 :]

        out[SHARD:, :] = jnp.zeros((CARRY - SHARD, 3 * SPAN), LOW)
        for i, vector in enumerate(vectors[:8]):
            out[SHARD + i : SHARD + i + 1, :SHARD] = vector[...].reshape(1, SHARD)
        for i in range(4):
            part = vectors[8][SHARD * i : SHARD * (i + 1)]
            out[SHARD + i : SHARD + i + 1, BLOCK : BLOCK + SHARD] = part.reshape(1, SHARD)


def prepare_rest_kernel(at, fc, outer, out_half, *outs):
    pad = jnp.zeros((CARRY - SHARD, FF_PART), LOW)
    for half in range(2):

        @pl.when(at[CORE] == half)
        def _():
            out_half[:SHARD, :] = outer[:, FF_PART * half : FF_PART * (half + 1)]

    out_half[SHARD:, :] = pad
    for r in range(4):
        start, shift = FF_PART * r // 128 * 128, FF_PART * r % 128
        start = pl.multiple_of(at[CORE] * (4 * FF_PART) + start, 128)
        part = fc[:, pl.ds(start, 896)][:, shift : shift + FF_PART]
        for d, out in enumerate(outs):

            @pl.when((at[Z] ^ d) == r)
            def _():
                out[:SHARD, :] = part
                out[SHARD:, :] = pad


def normalize(inputs):
    average = jnp.mean(inputs, axis=-1, keepdims=True)
    centred = inputs - average
    spread = jnp.mean(centred * centred, axis=-1, keepdims=True)
    inverse = lax.rsqrt(spread + EPSILON)
    return centred * inverse, inverse


def norm_back(d_normed, hat, inverse, gain):
    e = d_normed * gain
    return inverse * (
        e
        - jnp.mean(e, axis=-1, keepdims=True)
        - hat * jnp.mean(e * hat, axis=-1, keepdims=True)
    )


def load(pairs, sems):
    copies = [pltpu.make_async_copy(f, t, sems.at[i]) for i, (f, t) in enumerate(pairs)]
    for copy in copies:
        copy.start()
    return copies


def weight_pairs(pieces, target):
    pairs, k = [], 0
    for piece in pieces:
        for one in [piece] if len(piece.shape) == 2 else [piece.at[0], piece.at[1]]:
            pairs.append((one, target.at[k, pl.ds(0, CARRY)]))
            k += 1
    return pairs


def clear_pad(target):
    target[:, CARRY:, :] = jnp.zeros((8, BLOCK - CARRY, target.shape[2]), LOW)


def first_kernel(at, *refs):
    token_refs, weight_refs, refs = refs[:8], refs[8:12], refs[12:]
    normed, qkv, vectors, fc_bias, tokens, weight, wide, blocks, spread, *sems = refs
    step = pl.program_id(0)

    def token_copy(k):
        target = tokens.at[k ^ at[MEMBER]]
        return pltpu.make_async_copy(token_refs[k], target, sems[1].at[k])

    @pl.when(step == 0)
    def _():
        for k in range(8):
            token_copy(k).start()
        copies = load(weight_pairs(weight_refs, weight), sems[0])
        clear_pad(weight)
        spread[...] = jnp.zeros_like(spread)
        wide[:, WIDTH:] = jnp.zeros((wide.shape[0], wide.shape[1] - WIDTH), LOW)
        for copy in copies:
            copy.wait()
        for k in range(8):
            block = weight[k ^ at[ME], SHARD:CARRY, :BLOCK].astype(WIDE)
            spread[:, SHARD * k : SHARD * (k + 1)] = block[:, :SHARD]
        vectors[...] = spread[:, :WIDTH]
        rows = weight[(at[CORE] ^ at[YL]) * 4, SHARD:CARRY, BLOCK : 2 * BLOCK].astype(WIDE)
        for i in range(4):
            fc_bias[:, SHARD * i : SHARD * (i + 1)] = rows[i : i + 1, :SHARD]
        for k in range(8):
            token_copy(k).wait()

    rows = tokens[pl.ds(step * 2, 2)].reshape(2 * ROWS, WIDTH)
    hat, _ = normalize(rows.astype(WIDE))
    low = (hat * spread[0:1, :WIDTH] + spread[1:2, :WIDTH]).astype(LOW)
    normed[...] = low
    wide[:, :WIDTH] = low

    def write(k, block):
        blocks[:, block_at(k)] = block

    to_blocks(wide, at[ME], write)
    heads = pl.ds(pl.multiple_of(SPAN * at[MEMBER], SPAN), SPAN)
    total = jnp.dot(
        blocks[...], weight[...].reshape(8 * BLOCK, 3 * SPAN), preferred_element_type=WIDE
    )
    qkv[:, :SPAN] = (total[:, :SPAN] + spread[2:3, heads]).astype(LOW)
    qkv[:, SPAN : 2 * SPAN] = total[:, SPAN : 2 * SPAN].astype(LOW)
    qkv[:, 2 * SPAN :] = (total[:, 2 * SPAN :] + spread[3:4, heads]).astype(LOW)


Q_ROWS = 256


def first(at, tokens, weight):
    rows = 8 * ROWS
    still = lambda i: (0, 0)
    down = lambda i: (i, 0)
    return pl.pallas_call(
        first_kernel,
        grid=(rows // Q_ROWS,),
        in_specs=[SMEM] + [ANY] * 12,
        out_specs=[
            pl.BlockSpec((Q_ROWS, WIDTH), down),
            pl.BlockSpec((Q_ROWS, 3 * SPAN), down),
            pl.BlockSpec((8, WIDTH), still),
            pl.BlockSpec((1, FF_PART), still),
        ],
        out_shape=[
            like((rows, WIDTH)),
            like((rows, 3 * SPAN)),
            like((8, WIDTH), WIDE),
            like((1, FF_PART), WIDE),
        ],
        scratch_shapes=[
            pltpu.VMEM((8, ROWS, WIDTH), LOW),
            pltpu.VMEM((8, BLOCK, 3 * SPAN), LOW),
            pltpu.VMEM((Q_ROWS, WIDTH + 192), LOW),
            pltpu.VMEM((Q_ROWS, 8 * BLOCK), LOW),
            pltpu.VMEM((8, 8 * BLOCK), WIDE),
            pltpu.SemaphoreType.DMA((8,)),
            pltpu.SemaphoreType.DMA((8,)),
        ],
        compiler_params=pltpu.CompilerParams(vmem_limit_bytes=VMEM_LIMIT),
        cost_estimate=cost(0),
        name="first_norm_qkv",
    )(at, *tokens, *weight)


def visible(lengths, first_row, rows, keys):
    row = first_row + lax.broadcasted_iota(jnp.int32, (rows, 1), 0)
    key = lax.broadcasted_iota(jnp.int32, (1, keys), 1)
    start = jnp.zeros_like(row)
    bound = 0
    for i in range(3):
        bound = bound + lengths[0, i]
        start = jnp.where(row >= bound, bound, start)
    return (key <= row) & (key >= start)


ACROSS = (((1,), (1,)), ((), ()))


def by_block(body):
    for i in range(8 * ROWS // Q_ROWS):
        pl.when(pl.program_id(0) == i)(lambda i=i: body(i))


def slot_rows(at, chunk):
    return pl.ds(pl.multiple_of((chunk ^ at[MEMBER]) * ROWS, ROWS), ROWS)


def attend_kernel(at, lengths, q_ref, k_ref, v_ref, mixed_ref, logsum_ref):
    def block(i):
        keys = Q_ROWS * (i + 1)
        q, k, v = q_ref[...], k_ref[:keys, :], v_ref[:keys, :]
        allowed = visible(lengths, i * Q_ROWS, Q_ROWS, keys)
        lane = lax.broadcasted_iota(jnp.int32, q.shape, 1) // HEAD_DIM
        slim = lax.broadcasted_iota(jnp.int32, logsum_ref.shape, 1)
        mixed = jnp.zeros(q.shape, WIDE)
        logsums = jnp.zeros(logsum_ref.shape, WIDE)
        for head in range(TEAM_HEADS):
            own = lane == head
            q_own = jnp.where(own, q, jnp.zeros_like(q))
            scores = lax.dot_general(q_own, k, ACROSS, preferred_element_type=WIDE)
            scores = jnp.where(allowed, scores * (HEAD_DIM**-0.5), -1e30)
            top = jnp.max(scores, axis=-1, keepdims=True)
            powers = jnp.exp(scores - top)
            total = jnp.sum(powers, axis=-1, keepdims=True)
            probs = (powers * (1.0 / total)).astype(LOW)
            mixed = jnp.where(own, jnp.dot(probs, v, preferred_element_type=WIDE), mixed)
            logsums = jnp.where(slim == head, top + jnp.log(total), logsums)
        low = mixed.astype(LOW)
        for half in range(Q_ROWS // ROWS):
            rows = slot_rows(at, i * (Q_ROWS // ROWS) + half)
            mixed_ref[rows, :] = low[ROWS * half : ROWS * (half + 1)]
        logsum_ref[...] = logsums

    by_block(block)


def attend_back_kernel(
    at, lengths, q_ref, k_ref, v_ref, logsum_ref, dmix_ref, out_ref, dk_total, dv_total
):
    scale = HEAD_DIM**-0.5

    def block(i):
        keys = Q_ROWS * (i + 1)
        if i == 0:
            dk_total[...] = jnp.zeros_like(dk_total)
            dv_total[...] = jnp.zeros_like(dv_total)
        q, k, v = q_ref[...], k_ref[:keys, :], v_ref[:keys, :]
        count = Q_ROWS // ROWS
        dmix = jnp.concatenate([dmix_ref[slot_rows(at, i * count + n), :] for n in range(count)])
        allowed = visible(lengths, i * Q_ROWS, Q_ROWS, keys)
        lane = lax.broadcasted_iota(jnp.int32, q.shape, 1) // HEAD_DIM
        dq = jnp.zeros(q.shape, WIDE)
        for head in range(TEAM_HEADS):
            own = lane == head
            q_own = jnp.where(own, q, jnp.zeros_like(q))
            dmix_own = jnp.where(own, dmix, jnp.zeros_like(dmix))
            scores = lax.dot_general(q_own, k, ACROSS, preferred_element_type=WIDE) * scale
            scores = jnp.where(allowed, scores, -1e30)
            probs = jnp.exp(scores - logsum_ref[:, head : head + 1])
            d_probs = lax.dot_general(dmix_own, v, ACROSS, preferred_element_type=WIDE)
            term = jnp.sum(probs * d_probs, axis=-1, keepdims=True)
            d_scores = (probs * (d_probs - term)).astype(LOW)
            dq = jnp.where(own, jnp.dot(d_scores, k, preferred_element_type=WIDE), dq)
            dk_total[:keys, :] += lax.dot_general(
                d_scores, q_own, DOWN, preferred_element_type=WIDE
            )
            dv_total[:keys, :] += lax.dot_general(
                probs.astype(LOW), dmix_own, DOWN, preferred_element_type=WIDE
            )
        out_ref[Q_ROWS * i : Q_ROWS * (i + 1), :SPAN] = (dq * scale).astype(LOW)
        if i == 8 * ROWS // Q_ROWS - 1:
            out_ref[:, SPAN : 2 * SPAN] = (dk_total[...] * scale).astype(LOW)
            out_ref[:, 2 * SPAN :] = dv_total[...].astype(LOW)

    by_block(block)


def attend_specs(rows):
    return [
        SMEM,
        SMEM,
        pl.BlockSpec((Q_ROWS, SPAN), lambda i: (i, 0)),
        pl.BlockSpec((rows, SPAN), lambda i: (0, 1)),
        pl.BlockSpec((rows, SPAN), lambda i: (0, 2)),
    ]


def attend(places, qkv):
    rows = qkv.shape[0]
    return pl.pallas_call(
        attend_kernel,
        grid=(rows // Q_ROWS,),
        in_specs=attend_specs(rows),
        out_specs=[
            pl.BlockSpec((rows, SPAN), lambda i: (0, 0)),
            pl.BlockSpec((Q_ROWS, 128), lambda i: (i, 0)),
        ],
        out_shape=[
            jax.ShapeDtypeStruct((rows, SPAN), LOW),
            jax.ShapeDtypeStruct((rows, 128), WIDE),
        ],
        compiler_params=pltpu.CompilerParams(vmem_limit_bytes=VMEM_LIMIT),
        cost_estimate=cost(0),
        name="attend",
    )(*places, qkv, qkv, qkv)


def attend_back(places, qkv, logsum, dmix):
    rows = qkv.shape[0]
    whole = lambda i: (0, 0)
    return pl.pallas_call(
        attend_back_kernel,
        grid=(rows // Q_ROWS,),
        in_specs=attend_specs(rows)
        + [pl.BlockSpec((Q_ROWS, 128), lambda i: (i, 0)), pl.BlockSpec((rows, SPAN), whole)],
        out_specs=pl.BlockSpec((rows, 3 * SPAN), whole),
        out_shape=like((rows, 3 * SPAN)),
        scratch_shapes=[pltpu.VMEM((rows, SPAN), WIDE)] * 2,
        compiler_params=pltpu.CompilerParams(vmem_limit_bytes=VMEM_LIMIT),
        cost_estimate=cost(0),
        name="attend_back",
    )(*places, qkv, qkv, qkv, logsum, dmix)


def middle_kernel(at, tokens, vectors, *refs):
    pieces, mine_refs, other_refs, refs = refs[:4], refs[4:8], refs[8:12], refs[12:]
    middle, normed, mixed_out, mixed, blocks, wide, mine, other, *sems = refs
    copies = load(weight_pairs(mine_refs, mine), sems[0])
    copies += load(weight_pairs(other_refs, other), sems[1])
    clear_pad(mine)
    clear_pad(other)
    for d, piece in enumerate(pieces):
        mixed[:, block_at(d ^ at[MEMBER])] = piece[:, :SPAN]
        mixed[:, block_at((4 + d) ^ at[MEMBER])] = piece[:, SPAN:]

    def write_blocks(k, block):
        blocks[:, block_at(k)] = block

    to_blocks(mixed, at[ME], write_blocks)
    mixed_out[...] = mixed[:, :WIDTH]
    for copy in copies[:8]:
        copy.wait()
    flat = (8 * BLOCK, FF_PART)
    a = jnp.dot(blocks[...], mine[...].reshape(flat), preferred_element_type=WIDE)
    for copy in copies[8:]:
        copy.wait()
    b = jnp.dot(blocks[...], other[...].reshape(flat), preferred_element_type=WIDE)
    wide[:, :FF_PART] = jnp.where(at[CORE] == 0, a, b)
    wide[:, FF_PART:] = jnp.where(at[CORE] == 0, b, a)
    total = tokens[...].astype(WIDE) + wide[...] + vectors[4:5, :]
    middle[...] = total
    hat, _ = normalize(total)
    normed[...] = (hat * vectors[5:6, :] + vectors[6:7, :]).astype(LOW)


OUT_WEIGHT_SCRATCH = [
    pltpu.VMEM((8, BLOCK, FF_PART), LOW),
    pltpu.VMEM((8, BLOCK, FF_PART), LOW),
    pltpu.SemaphoreType.DMA((8,)),
    pltpu.SemaphoreType.DMA((8,)),
]


def proj_pairs(own, first_half, second_half, target):
    rows = FF_PART // 2
    return (
        [(own.at[pl.ds(0, rows)], target.at[pl.ds(0, rows)]), (own.at[pl.ds(rows, rows)], target.at[pl.ds(rows, rows)])],
        [(first_half, target.at[pl.ds(0, rows)]), (second_half, target.at[pl.ds(rows, rows)])],
    )


def load_proj(at, refs, target, sems):
    own, got = proj_pairs(*refs, target)

    @pl.when(at[CORE] == at[YL])
    def _():
        for copy in load(own, sems):
            copy.wait()

    @pl.when(at[CORE] != at[YL])
    def _():
        for copy in load(got, sems):
            copy.wait()


def halves(i):
    return jnp.minimum(i, 1), 0


def late_halves(i):
    return jnp.maximum(i - 2, 0), 0


def write_half(step, near, far, value):
    @pl.when(step < 2)
    def _():
        near[:, :WIDTH] = value
        near[:, WIDTH:] = jnp.zeros((value.shape[0], LANES - WIDTH), LOW)

    @pl.when(step >= 2)
    def _():
        far[:, :WIDTH] = value
        far[:, WIDTH:] = jnp.zeros((value.shape[0], LANES - WIDTH), LOW)


def hidden_back_kernel(at, *refs):
    cot_refs, proj_refs, (d_hidden, cot, proj, *sems) = refs[:8], refs[8:11], refs[11:]
    step = pl.program_id(0)

    def cot_copy(k):
        return pltpu.make_async_copy(cot_refs[k], cot.at[k], sems[0].at[k])

    @pl.when(step == 0)
    def _():
        for k in range(8):
            cot_copy(k).start()
        load_proj(at, proj_refs, proj, sems[1])

    for k in range(8):

        @pl.when(step == k // 2)
        def _():
            cot_copy(k).wait()

    rows = cot[pl.ds(step * 2, 2)].reshape(2 * ROWS, WIDTH)
    d_hidden[...] = lax.dot_general(rows, proj[...], ACROSS, preferred_element_type=WIDE)


def hidden_back(at, cot, proj):
    rows = 8 * ROWS
    return pl.pallas_call(
        hidden_back_kernel,
        grid=(rows // Q_ROWS,),
        in_specs=[SMEM] + [ANY] * 11,
        out_specs=pl.BlockSpec((Q_ROWS, FF_PART), lambda i: (i, 0)),
        out_shape=like((rows, FF_PART), WIDE),
        scratch_shapes=[
            pltpu.VMEM((8, ROWS, WIDTH), LOW),
            pltpu.VMEM((FF_PART, WIDTH), LOW),
            pltpu.SemaphoreType.DMA((8,)),
            pltpu.SemaphoreType.DMA((2,)),
        ],
        compiler_params=pltpu.CompilerParams(vmem_limit_bytes=VMEM_LIMIT),
        cost_estimate=cost(0),
        name="hidden_back",
    )(at, *cot, *proj)


def feed_kernel(at, bias, d_hidden, *refs):
    normed_refs, fc_refs, refs = refs[:8], refs[8:12], refs[12:]
    hidden, d_in, near, far, bias_sum, normed, fc, wide, blocks, tall, back, *sems = refs
    step = pl.program_id(0)

    def normed_copy(k):
        return pltpu.make_async_copy(normed_refs[k], normed.at[k], sems[0].at[k])

    @pl.when(step == 0)
    def _():
        for k in range(2):
            normed_copy(k).start()
        copies = load(weight_pairs(fc_refs, fc), sems[1])
        clear_pad(fc)
        bias_sum[...] = jnp.zeros_like(bias_sum)
        wide[:, WIDTH:] = jnp.zeros((2 * ROWS, wide.shape[1] - WIDTH), LOW)
        for copy in copies:
            copy.wait()

    for k in range(8):

        @pl.when(step == k // 2)
        def _():
            normed_copy(k).wait()

        @pl.when(step + 1 == k // 2)
        def _():
            normed_copy(k).start()

    wide[:, :WIDTH] = normed[pl.ds(step * 2, 2)].reshape(2 * ROWS, WIDTH)

    def write(k, block):
        blocks[:, block_at(k)] = block

    to_blocks(wide, at[ME], write)
    weight = fc[...].reshape(8 * BLOCK, FF_PART)
    u = jnp.dot(blocks[...], weight, preferred_element_type=WIDE) + bias[...]
    factor = (2.0 / jnp.pi) ** 0.5
    square = u * u
    bent = jnp.tanh(factor * (u + 0.044715 * (square * u)))
    half = 0.5 * (1.0 + bent)
    hidden[...] = (u * half).astype(LOW)
    slope = half + (0.5 * factor) * u * (1.0 - bent * bent) * (1.0 + (3 * 0.044715) * square)
    low = (d_hidden[...] * slope).astype(LOW)
    d_in[...] = low
    bias_sum[...] += jnp.sum(low.astype(WIDE), axis=0, keepdims=True)
    tall[...] = lax.dot_general(low, weight, ACROSS, preferred_element_type=WIDE).astype(LOW)
    from_blocks(tall, at[ME], back)
    write_half(step, near, far, back[...])


def feed(at, normed, d_hidden, fc, bias):
    rows = 8 * ROWS
    still = lambda i: (0, 0)
    down = lambda i: (i, 0)
    return pl.pallas_call(
        feed_kernel,
        grid=(rows // Q_ROWS,),
        in_specs=[
            SMEM,
            pl.BlockSpec((1, FF_PART), still),
            pl.BlockSpec((Q_ROWS, FF_PART), down),
        ]
        + [ANY] * 12,
        out_specs=[
            pl.BlockSpec((Q_ROWS, FF_PART), down),
            pl.BlockSpec((Q_ROWS, FF_PART), down),
            pl.BlockSpec((Q_ROWS, LANES), halves),
            pl.BlockSpec((Q_ROWS, LANES), late_halves),
            pl.BlockSpec((1, FF_PART), still),
        ],
        out_shape=[
            like((rows, FF_PART)),
            like((rows, FF_PART)),
            like((rows // 2, LANES)),
            like((rows // 2, LANES)),
            like((1, FF_PART), WIDE),
        ],
        scratch_shapes=[
            pltpu.VMEM((8, ROWS, WIDTH), LOW),
            pltpu.VMEM((8, BLOCK, FF_PART), LOW),
            pltpu.VMEM((Q_ROWS, WIDTH + 192), LOW),
            pltpu.VMEM((Q_ROWS, 8 * BLOCK), LOW),
            pltpu.VMEM((Q_ROWS, 8 * BLOCK), LOW),
            pltpu.VMEM((Q_ROWS, WIDTH), LOW),
            pltpu.SemaphoreType.DMA((8,)),
            pltpu.SemaphoreType.DMA((8,)),
        ],
        compiler_params=pltpu.CompilerParams(vmem_limit_bytes=VMEM_LIMIT),
        cost_estimate=cost(0),
        name="feed_forward_and_back",
    )(at, bias, d_hidden, *normed, *fc)


def final_kernel(at, hidden, *refs):
    proj_refs, (near, far, proj, sems) = refs[:3], refs[3:]
    step = pl.program_id(0)

    @pl.when(step == 0)
    def _():
        load_proj(at, proj_refs, proj, sems)

    total = jnp.dot(hidden[...], proj[...], preferred_element_type=WIDE).astype(LOW)
    write_half(step, near, far, total)


def final_part(at, hidden, proj):
    rows = hidden.shape[0]
    return pl.pallas_call(
        final_kernel,
        grid=(rows // Q_ROWS,),
        in_specs=[SMEM, pl.BlockSpec((Q_ROWS, FF_PART), lambda i: (i, 0))] + [ANY] * 3,
        out_specs=[
            pl.BlockSpec((Q_ROWS, LANES), halves),
            pl.BlockSpec((Q_ROWS, LANES), late_halves),
        ],
        out_shape=[like((rows // 2, LANES))] * 2,
        scratch_shapes=[pltpu.VMEM((FF_PART, WIDTH), LOW), pltpu.SemaphoreType.DMA((2,))],
        compiler_params=pltpu.CompilerParams(vmem_limit_bytes=VMEM_LIMIT),
        cost_estimate=cost(0),
        name="feed_forward_out",
    )(at, hidden, *proj)


def padded_rows():
    return pl.BlockSpec((ROWS, LANES), lambda i: (0, 0))


def team_total(refs):
    total = refs[0][:, :WIDTH].astype(WIDE)
    for ref in refs[1:]:
        total = total + ref[:, :WIDTH].astype(WIDE)
    return total


def row_sum(value):
    return jnp.sum(value, axis=0, keepdims=True)


def output_kernel(at, middle, vectors, near, got, one, two, three, out):
    total = middle[...] + vectors[7:8, :]
    total = total + team_total([near, got, one, two, three])
    out[...] = jnp.transpose(total).astype(LOW)


def out_grad_kernel(at, left, left_other, right, right_other, *refs):
    outs, total = refs[:4], refs[4]
    first_core = at[CORE] == 0

    def half(ref):
        value = ref[...]
        return jnp.where(first_core, value[:, :FF_PART], value[:, FF_PART:])

    total[:FF_PART, :] = lax.dot_general(
        jnp.concatenate([half(left), half(left_other)]),
        jnp.concatenate([right[...], right_other[...]]),
        DOWN,
        preferred_element_type=WIDE,
    )
    for d, out in enumerate(outs):
        start = pl.multiple_of((at[Z] ^ d) * SHARD, 8)
        out[...] = total[pl.ds(start, CARRY), :].astype(LOW)


def out_grad(at, left, left_other, right, right_other):
    return whole_call(
        out_grad_kernel,
        "out_grad",
        [like((CARRY, WIDTH))] * 4,
        at,
        left,
        left_other,
        right,
        right_other,
        scratch=[pltpu.VMEM((FF_PART + CARRY - SHARD, WIDTH), WIDE)],
        limit=VMEM_LIMIT,
    )


def out_sum_kernel(at, own, one, two, three, out, total):
    total[...] = team_total([own, one, two, three])
    for q in range(4):
        piece = total[PIECE_STEP * q : PIECE_STEP * q + PIECE, :].astype(LOW)
        out[2 * q] = piece[:, :FF_PART]
        out[2 * q + 1] = piece[:, FF_PART:]


def second_back_kernel(at, middle, cot, vectors, near, got, *refs):
    parts, mine_refs, other_refs, refs = refs[:3], refs[3:7], refs[7:11], refs[11:]
    (d_middle, d_branch, sums), pieces, refs = refs[:3], refs[3:7], refs[7:]
    wide, tall, narrow, mine, other, *sems = refs
    copies = load(weight_pairs(mine_refs, mine), sems[0])
    copies += load(weight_pairs(other_refs, other), sems[1])
    clear_pad(mine)
    clear_pad(other)
    d_second = team_total([near, got, *parts])
    hat, inverse = normalize(middle[...])
    d_cot = cot[...].astype(WIDE)
    total = d_cot + norm_back(d_second, hat, inverse, vectors[5:6, :])
    d_middle[...] = total
    low = total.astype(LOW)
    d_branch[...] = low
    sums[0:1, :] = row_sum(d_second * hat)
    sums[1:2, :] = row_sum(d_second)
    sums[2:3, :] = row_sum(low.astype(WIDE))
    sums[3:4, :] = row_sum(d_cot)
    sums[4:8, :] = jnp.zeros((4, WIDTH), WIDE)
    wide[...] = low
    left, right = wide[:, :FF_PART], wide[:, FF_PART:]
    first_core = at[CORE] == 0
    flat = (8 * BLOCK, FF_PART)
    across = (((1,), (1,)), ((), ()))
    for copy in copies[:8]:
        copy.wait()
    part = lax.dot_general(
        jnp.where(first_core, left, right),
        mine[...].reshape(flat),
        across,
        preferred_element_type=WIDE,
    )
    for copy in copies[8:]:
        copy.wait()
    tall[...] = part + lax.dot_general(
        jnp.where(first_core, right, left),
        other[...].reshape(flat),
        across,
        preferred_element_type=WIDE,
    )
    narrow[:, WIDTH:] = jnp.zeros((ROWS, 8 * SPAN - WIDTH), LOW)
    from_blocks(tall, at[ME], narrow)
    for d, piece in enumerate(pieces):
        piece[:, :SPAN] = narrow[:, block_at(d ^ at[MEMBER])]
        piece[:, SPAN:] = narrow[:, block_at((4 + d) ^ at[MEMBER])]


def second_back(at, middle, cot, vectors, near, got, parts, mine, other):
    part = pl.BlockSpec((ROWS, WIDTH), lambda i: (0, 0))
    return pl.pallas_call(
        second_back_kernel,
        grid=(1,),
        in_specs=[SMEM, part, part, pl.BlockSpec((8, WIDTH), lambda i: (0, 0))]
        + [padded_rows()] * 5
        + [ANY] * 8,
        out_specs=[VMEM] * 7,
        out_shape=[like((ROWS, WIDTH), WIDE), like((ROWS, WIDTH)), like((8, WIDTH), WIDE)]
        + [like((ROWS, 2 * SPAN))] * 4,
        scratch_shapes=[
            pltpu.VMEM((ROWS, WIDTH), LOW),
            pltpu.VMEM((ROWS, 8 * BLOCK), WIDE),
            pltpu.VMEM((ROWS, 8 * SPAN), LOW),
        ]
        + OUT_WEIGHT_SCRATCH,
        compiler_params=pltpu.CompilerParams(vmem_limit_bytes=VMEM_LIMIT),
        cost_estimate=cost(0),
        name="second_norm_and_out_back",
    )(at, middle, cot, vectors, near, got, *parts, *mine, *other)


def first_back_kernel(at, d_qkv, *refs):
    weight_refs, (near, far, sums, weight, tall, back, sems) = refs[:4], refs[4:]
    step = pl.program_id(0)

    @pl.when(step == 0)
    def _():
        copies = load(weight_pairs(weight_refs, weight), sems)
        clear_pad(weight)
        ones = jnp.ones((16, d_qkv.shape[0]), LOW)
        sums[...] = jnp.dot(ones, d_qkv[...], preferred_element_type=WIDE)[:1]
        for copy in copies:
            copy.wait()

    rows = jnp.concatenate([d_qkv[slot_rows(at, 2 * step + n), :] for n in range(2)])
    tall[...] = lax.dot_general(
        rows, weight[...].reshape(8 * BLOCK, 3 * SPAN), ACROSS, preferred_element_type=WIDE
    ).astype(LOW)
    from_blocks(tall, at[ME], back)
    write_half(step, near, far, back[...])


def first_back(at, d_qkv, weight):
    rows = d_qkv.shape[0]
    whole = lambda i: (0, 0)
    return pl.pallas_call(
        first_back_kernel,
        grid=(rows // Q_ROWS,),
        in_specs=[SMEM, pl.BlockSpec((rows, 3 * SPAN), whole)] + [ANY] * 4,
        out_specs=[
            pl.BlockSpec((Q_ROWS, LANES), halves),
            pl.BlockSpec((Q_ROWS, LANES), late_halves),
            pl.BlockSpec((1, 3 * SPAN), whole),
        ],
        out_shape=[
            like((rows // 2, LANES)),
            like((rows // 2, LANES)),
            like((1, 3 * SPAN), WIDE),
        ],
        scratch_shapes=[
            pltpu.VMEM((8, BLOCK, 3 * SPAN), LOW),
            pltpu.VMEM((Q_ROWS, 8 * BLOCK), LOW),
            pltpu.VMEM((Q_ROWS, WIDTH), LOW),
            pltpu.SemaphoreType.DMA((8,)),
        ],
        compiler_params=pltpu.CompilerParams(vmem_limit_bytes=VMEM_LIMIT),
        cost_estimate=cost(0),
        name="qkv_back",
    )(at, d_qkv, *weight)


SUMS = (PIECE, FF_PART)


def input_kernel(at, tokens, d_middle, vectors, second_sums, fc_sum, qkv_sum, *refs):
    parts, (grad, sums, held) = refs[:5], refs[5:]
    d_first = team_total(parts)
    hat, inverse = normalize(tokens[...].astype(WIDE))
    total = d_middle[...] + norm_back(d_first, hat, inverse, vectors[0:1, :])
    grad[...] = jnp.transpose(total).astype(LOW)
    held[...] = jnp.zeros(SUMS, WIDE)
    rows = [row_sum(d_first * hat), row_sum(d_first)] + [second_sums[i : i + 1, :] for i in range(4)]
    for i, row in enumerate(rows):
        held[2 * i : 2 * i + 1, :] = row[:, :FF_PART]
        held[2 * i + 1 : 2 * i + 2, :] = row[:, FF_PART:]
    held[pl.ds(16 + at[MEMBER], 1), :] = fc_sum[...]
    held[pl.ds(24 + at[MEMBER], 1), :SPAN] = qkv_sum[:, :SPAN]
    held[pl.ds(32 + at[MEMBER], 1), :SPAN] = qkv_sum[:, 2 * SPAN :]
    sums[0] = held[...].astype(LOW)


def input_back(at, tokens, d_middle, vectors, second_sums, fc_sum, qkv_sum, parts):
    still = lambda i: (0, 0)
    part = pl.BlockSpec((ROWS, WIDTH), still)
    rows = pl.BlockSpec((8, WIDTH), still)
    return pl.pallas_call(
        input_kernel,
        grid=(1,),
        in_specs=[
            SMEM,
            part,
            part,
            rows,
            rows,
            pl.BlockSpec((1, FF_PART), still),
            pl.BlockSpec((1, 3 * SPAN), still),
        ]
        + [padded_rows()] * 5,
        out_specs=[
            pl.BlockSpec((WIDTH, ROWS), still),
            pl.BlockSpec((1,) + SUMS, lambda i: (0, 0, 0)),
        ],
        out_shape=[like((WIDTH, ROWS)), like((1,) + SUMS)],
        scratch_shapes=[pltpu.VMEM(SUMS, WIDE)],
        compiler_params=pltpu.CompilerParams(vmem_limit_bytes=SMALL_LIMIT),
        cost_estimate=cost(0),
        name="first_norm_back",
    )(at, tokens, d_middle, vectors, second_sums, fc_sum, qkv_sum, *parts)


def feed_grad_kernel(at, hidden, d_in, *refs):
    cot_refs, normed_refs, (out, normed, cot, total, tall, *sems) = refs[:8], refs[8:16], refs[16:]
    pairs = [(normed_refs[k], normed.at[k]) for k in range(8)]
    first_copies = load(pairs, sems[0])
    pairs = [(cot_refs[k], cot.at[k]) for k in range(8)]
    second_copies = load(pairs, sems[1])
    for copy in first_copies:
        copy.wait()
    total[...] = lax.dot_general(
        normed[...].reshape(8 * ROWS, WIDTH), d_in[...], DOWN, preferred_element_type=WIDE
    )
    for k in range(8):
        for q in range(4):
            start = pl.multiple_of((k ^ at[ME]) * SHARD + PIECE_STEP * q, 8)
            out[16 * q + k] = total[pl.ds(start, PIECE), :].astype(LOW)
    for copy in second_copies:
        copy.wait()
    tall[...] = lax.dot_general(
        hidden[...], cot[...].reshape(8 * ROWS, WIDTH), DOWN, preferred_element_type=WIDE
    )
    for q in range(4):
        for half in range(2):
            lanes = slice(FF_PART * half, FF_PART * (half + 1))
            for k in range(4):
                start = SHARD * q + PIECE_STEP * k
                out[16 * q + 8 + 4 * half + k] = tall[start : start + PIECE, lanes].astype(LOW)


def feed_grad(at, normed, d_in, hidden, cot):
    rows = 8 * ROWS
    return pl.pallas_call(
        feed_grad_kernel,
        in_specs=[SMEM, VMEM, VMEM] + [ANY] * 16,
        out_specs=VMEM,
        out_shape=like((64, PIECE, FF_PART)),
        scratch_shapes=[
            pltpu.VMEM((8, ROWS, WIDTH), LOW),
            pltpu.VMEM((8, ROWS, WIDTH), LOW),
            pltpu.VMEM((WIDTH, FF_PART), WIDE),
            pltpu.VMEM((FF_PART, WIDTH), WIDE),
            pltpu.SemaphoreType.DMA((8,)),
            pltpu.SemaphoreType.DMA((8,)),
        ],
        compiler_params=pltpu.CompilerParams(vmem_limit_bytes=VMEM_LIMIT),
        cost_estimate=cost(0),
        name="feed_forward_grad",
    )(at, hidden, d_in, *cot, *normed)


def qkv_grad_kernel(at, normed, d_qkv, *refs):
    outs, total = refs[:4], refs[4]
    total[:, 3 * SPAN :] = jnp.zeros((WIDTH, FF_PART - 3 * SPAN), WIDE)
    total[:, : 3 * SPAN] = lax.dot_general(
        normed[...], d_qkv[...], DOWN, preferred_element_type=WIDE
    )
    for d, out in enumerate(outs):
        place = pl.multiple_of((at[X] ^ d) * PIECE_STEP, 8)
        for k in range(8):
            start = pl.multiple_of((k ^ at[ME]) * SHARD + place, 8)
            out[k] = total[pl.ds(start, PIECE), :].astype(LOW)


def added(refs, k):
    total = refs[0][k].astype(WIDE)
    for ref in refs[1:]:
        total = total + ref[k].astype(WIDE)
    return total.astype(LOW)


def feed_mid_kernel(at, total, half_got, keep, give_fc, give_proj):
    own = at[CORE] == at[YL]
    keep[:4] = total[:4]
    give_fc[...] = total[4:8]
    mine, other = total[pl.ds(8 + 4 * at[CORE], 4)], half_got[...]
    keep[4:] = jnp.where(own, mine, other)
    give_proj[...] = jnp.where(own, other, mine)


def add_halves_kernel(at, keep, first_half, second_half, out):
    count = first_half.shape[0]
    for k in range(keep.shape[0]):
        half = (first_half, k) if k < count else (second_half, k - count)
        out[k] = (keep[k].astype(WIDE) + half[0][half[1]].astype(WIDE)).astype(LOW)


def split_sum_kernel(at, one, two, *outs):
    place = 0
    for out in outs:
        for k in range(out.shape[0]):
            out[k] = added((one, two), place)
            place += 1


def qkv_x_kernel(at, *refs):
    parts, out_total, sums, (keep, give_one, give_two) = refs[:4], refs[4], refs[5], refs[6:]
    for k in range(3):
        keep[k] = added(parts, k)
        give_one[k] = added(parts, 4 + k)
    keep[3] = sums[0]
    give_one[3] = sums[0]
    keep[4] = added(parts, 3)
    give_two[0] = added(parts, 7)
    for k in range(2):
        keep[5 + k] = out_total[k]
        give_two[1 + k] = out_total[k]


def qkv_y_kernel(at, half, last, own, one, two, three, rest, sums):
    pair = (half, last)
    own[0] = added(pair, 0)
    total = added(pair, 3)
    sums[0] = total
    for out, place in ((one, 1), (two, 2), (three, 4)):
        out[0] = added(pair, place)
        out[1] = total
    for k in range(2):
        rest[k] = added(pair, 5 + k)


def qkv_z_kernel(at, own, sums, one, two, three, rest, out):
    out[0] = own[0]
    total = sums[0].astype(WIDE)
    for k, got in enumerate((one, two, three)):
        out[1 + k] = got[0]
        total = total + got[1].astype(WIDE)
    out[4:6] = rest[...]
    out[6] = total.astype(LOW)


def feed_z_kernel(at, own, one, two, three, rest, out):
    for k, got in enumerate((own, one, two, three)):
        out[k] = got[0]
    out[4:] = rest[...]


def place_feed_kernel(at, mine, other, fc, proj):
    for c in range(2):
        for q in range(4):
            count = PIECE_STEP if q < 3 else PIECE

            def block(k):
                return jnp.where(at[CORE] == c, mine[q, k], other[q, k]).astype(WIDE)

            for z in range(4):
                j = c * 4 + z
                fc[PIECE_STEP * q : PIECE_STEP * q + count, FF_PART * j : FF_PART * (j + 1)] = block(
                    z ^ at[Z]
                )[:count]
            for k in range(4):
                rows = PIECE_STEP if k < 3 else PIECE
                row = SHARD * q + PIECE_STEP * k
                proj[row : row + rows, FF_PART * c : FF_PART * (c + 1)] = block(4 + k)[:rows]


def place_qkv_kernel(at, *refs):
    mine, other, (qkv, out), refs = refs[:4], refs[4:8], refs[8:10], refs[10:]
    vectors, held, scratch = refs[:9], refs[9], refs[10:]
    for k in range(4):
        held[0, k] = mine[k][...]
        held[1, k] = other[k][...]
    own = jnp.where(at[CORE] == at[YL], 0, 1)
    for q in range(4):
        count = PIECE_STEP if q < 3 else PIECE
        rows = slice(PIECE_STEP * q, PIECE_STEP * q + count)
        for c in range(2):
            for z in range(4):
                block = held[c ^ at[CORE], q ^ at[X], z ^ at[Z]].astype(WIDE)
                for start, stop, target in qkv_columns(c * 4 + z):
                    qkv[rows, target : target + stop - start] = block[:count, start:stop]
        for half in range(2):
            block = held[own, q ^ at[X], 4 + half].astype(WIDE)
            out[rows, FF_PART * half : FF_PART * (half + 1)] = block[:count]
    total = held[0, 0, 6].astype(WIDE)
    for core in range(2):
        for k in range(4):
            if core + k:
                total = total + held[core, k, 6].astype(WIDE)
    place_vectors(at, total, *vectors, *scratch)


def place_vectors(at, total, *refs):
    outs, (small, joined) = refs[:9], refs[9:]
    small[...] = total
    for i in range(6):
        row = small[pl.ds(2 * i + at[ME] // 4, 1), :]
        for k in range(4):

            @pl.when(at[ME] % 4 == k)
            def _():
                outs[i][...] = row[:, SHARD * k : SHARD * (k + 1)].reshape(SHARD)

    outs[6][...] = small[pl.ds(16 + at[ME], 1), :].reshape(FF_PART)
    for n in range(2):
        for k in range(8):
            at_row = 24 + 8 * n + k
            joined[:, SPAN * k : SPAN * (k + 1)] = small[at_row : at_row + 1, :SPAN]
        for k in range(8):

            @pl.when(at[ME] == k)
            def _():
                outs[7 + n][...] = joined[:, SHARD * k : SHARD * (k + 1)].reshape(SHARD)


def qkv_columns(j):
    count = min(SPAN, WIDTH - SPAN * j)
    if count <= 0:
        return []
    return [(SPAN * p, SPAN * p + count, WIDTH * p + SPAN * j) for p in range(3)]


def gather_rows(block, *gates, late=()):
    beside = c_swap(block)
    sent = after(block, *gates)
    near = {d: z_swap(sent, d) for d in (1, 3, 2)}
    far = {d: c_swap(after(near[d], *late)) for d in (1, 3, 2)}
    return [block, near[1], near[2], near[3], beside, far[1], far[2], far[3]], list(near.values())


def team_parts(near, far, c_gates=(), z_gates=()):
    got = c_swap(after(far, *c_gates))
    pair = [add([v[ROWS * d : ROWS * (d + 1)] for v in (near, got)]) for d in (1, 2, 3)]
    sent = after(pair, *z_gates)
    came = [z_swap(sent[d - 1], d) for d in (1, 3, 2)]
    return [near, got] + came, sent, came


def z_blocks(own, sends, *gates):
    sends = after(sends, *gates)
    near = {d: z_swap(sends[d], d) for d in (1, 3, 2)}
    near[0] = own
    return near


def far_blocks(near, *gates):
    near = after(near, *gates)
    one, two = jnp.stack([near[0], near[1]]), jnp.stack([near[2], near[3]])
    return [one, two, y_swap(one, 1), y_swap(two, 3)]


def spread_x(value, swap):
    got = [swap(value, d) for d in (1, 3)]
    two = swap(after(value, got), 2)
    return [value, got[0], two, got[1]]


def add(values):
    total = values[0].astype(WIDE)
    for value in values[1:]:
        total = total + value.astype(WIDE)
    return total.astype(LOW)


def local(
    tokens,
    lengths,
    ln1_gain,
    ln1_bias,
    qkv_weight,
    q_bias,
    v_bias,
    out_weight,
    out_bias,
    ln2_gain,
    ln2_bias,
    fc_weight,
    fc_bias,
    proj_weight,
    proj_bias,
    cotangent,
):
    c, x, yl, z = (lax.axis_index(a) for a in ("c", "x", "yl", "z"))
    me, member = yl * 4 + z, c * 4 + z
    at = jnp.stack([me, member, c, x, yl, z]).astype(jnp.int32)

    vectors = [ln1_gain, ln1_bias, q_bias, v_bias, out_bias, ln2_gain, ln2_bias, proj_bias, fc_bias]
    own_tokens = turn(tokens)
    qkv_sends = whole_call_any(
        prepare_qkv_kernel,
        "prepare_qkv",
        [like((CARRY, 3 * SPAN))] * 4,
        [at, qkv_weight],
        vectors,
        scratch=[pltpu.VMEM(v.shape, LOW) for v in vectors] + [pltpu.SemaphoreType.DMA((9,))],
    )
    half = proj_weight.shape[0] // 2
    proj_sends = proj_weight[:half], proj_weight[half:]

    out_half, *fc_sends = whole_call(
        prepare_rest_kernel,
        "prepare_rest",
        [like((CARRY, FF_PART))] * 5,
        at,
        after(fc_weight, qkv_sends),
        out_weight,
    )
    all_tokens, tokens_came = gather_rows(own_tokens)
    qkv_near = z_blocks(qkv_sends[0], qkv_sends, own_tokens)
    other_lengths = c_swap(after(lengths, tokens_came[0]))
    places = at, jnp.where(c == yl, lengths, other_lengths)
    weight_qkv = far_blocks(qkv_near, out_half, fc_sends, places, proj_sends)
    own_cotangent = turn(after(cotangent, own_tokens))
    out_near = z_blocks(out_half, [out_half] * 4, qkv_near, all_tokens, own_cotangent)
    proj_sent = after(proj_sends, weight_qkv, out_near)
    proj_pieces = [
        proj_weight,
        y_swap_some(proj_sent[0], 1, True),
        y_swap_some(proj_sent[1], 3, True),
    ]

    normed_first, qkv, vectors_all, fc_bias_own = first(at, all_tokens, after(weight_qkv, out_near))
    all_cotangent, cotangent_came = gather_rows(own_cotangent, out_near, late=(qkv,))
    qkv = after(qkv, cotangent_came, proj_pieces)
    out_mine = far_blocks(out_near, qkv)
    fc_near = z_blocks(fc_sends[0], fc_sends, qkv)
    mixed_heads, logsum = attend(places, qkv)
    mixed_heads = after(mixed_heads, out_mine, fc_near)
    out_other = [c_swap(after(piece, mixed_heads)) for piece in out_mine]

    mixed_near = mixed_heads[: 4 * ROWS]
    mixed_got = after(c_swap(mixed_heads[4 * ROWS :]), out_other)
    mixed_sent = [
        jnp.concatenate([v[ROWS * d : ROWS * (d + 1)] for v in (mixed_near, mixed_got)], axis=1)
        for d in range(4)
    ]
    mixed_pieces = [mixed_sent[0]] + [z_swap(mixed_sent[d], d) for d in (1, 2, 3)]
    middle, normed_second, mixed = whole_call_any(
        middle_kernel,
        "out_and_second_norm",
        [like((ROWS, WIDTH), WIDE), like((ROWS, WIDTH)), like((ROWS, WIDTH))],
        [at, own_tokens, vectors_all] + mixed_pieces,
        out_mine + out_other,
        scratch=[
            pltpu.VMEM((ROWS, 8 * SPAN), LOW),
            pltpu.VMEM((ROWS, 8 * BLOCK), LOW),
            pltpu.VMEM((ROWS, WIDTH), WIDE),
        ]
        + OUT_WEIGHT_SCRATCH,
    )

    d_hidden = hidden_back(at, after(all_cotangent, normed_second), proj_pieces)
    all_second, second_came = gather_rows(normed_second, late=(d_hidden,))
    weight_fc = far_blocks(fc_near, normed_second)
    mixed_other = c_swap(after(mixed, second_came))
    hidden, d_hidden_in, d_second_near, d_second_far, fc_bias_sum = feed(
        at, all_second, d_hidden, weight_fc, fc_bias_own
    )
    d_second_parts, d_second_sent, d_second_came = team_parts(d_second_near, d_second_far)

    hidden_late = after(hidden, d_second_sent)
    feed_pieces = feed_grad(at, all_second, d_hidden_in, hidden_late, all_cotangent)
    feed_total = lax.psum_scatter(
        after(feed_pieces, d_second_came), "x", scatter_dimension=0, tiled=True
    )

    d_middle, d_branch, second_sums, *d_mixed = second_back(
        at,
        middle,
        own_cotangent,
        after(vectors_all, feed_pieces),
        d_second_parts[0],
        d_second_parts[1],
        d_second_parts[2:],
        out_mine,
        out_other,
    )
    d_got = [d_mixed[0]] + [z_swap(d_mixed[d], d) for d in (1, 2, 3)]
    out_sent = out_grad(at, mixed, mixed_other, d_branch, c_swap(d_branch))
    d_keep = jnp.concatenate([v[:, :SPAN] for v in d_got])
    d_give = jnp.concatenate([v[:, SPAN:] for v in d_got])
    d_mixed_heads = jnp.concatenate([d_keep, c_swap(after(d_give, out_sent))])
    out_late = after(out_sent, d_give)
    out_came = [z_swap(out_late[d], d) for d in (1, 3)]
    d_qkv = attend_back(places, qkv, logsum, d_mixed_heads)
    d_qkv = after(d_qkv, out_came)
    out_came.append(z_swap(after(out_late[2], out_came), 2))

    def blocks_call(body, name, counts, *args):
        outs = [like((count, PIECE, FF_PART)) for count in counts]
        return whole_call(body, name, outs, at, *args)

    qkv_pieces = whole_call(
        qkv_grad_kernel,
        "qkv_grad",
        [like((8, PIECE, FF_PART))] * 4,
        at,
        normed_first,
        d_qkv,
        scratch=[pltpu.VMEM((WIDTH, FF_PART), WIDE)],
        limit=VMEM_LIMIT,
    )
    qkv_got = [x_swap(qkv_pieces[d], d) for d in (1, 3)]
    d_first_near, d_first_far, qkv_sums = first_back(at, after(d_qkv, qkv_pieces), weight_qkv)
    qkv_got.append(x_swap(after(qkv_pieces[2], qkv_got), 2))
    d_first_parts, d_first_sent, d_first_came = team_parts(
        d_first_near, d_first_far, (qkv_got[:2], out_came)
    )
    (out_pieces,) = held_call(
        out_sum_kernel,
        "out_sum",
        [like((8, PIECE, FF_PART))],
        at,
        out_sent[0],
        *out_came,
        scratch=[pltpu.VMEM((CARRY, WIDTH), WIDE)],
    )
    out_total = lax.psum_scatter(out_pieces, "x", scatter_dimension=0, tiled=True)
    feed_total = after(feed_total, d_first_sent)
    half_got = c_swap(lax.dynamic_slice_in_dim(feed_total, 12 - 4 * c, 4, 0))
    feed_keep, give_fc, give_proj = blocks_call(
        feed_mid_kernel, "feed_mid", [8, 4, 4], feed_total, half_got
    )
    feed_y = [y_swap(give_fc, 1), y_swap(give_proj, 3)]
    (feed_half,) = blocks_call(
        add_halves_kernel, "feed_half", [8], after(feed_keep, d_first_came), *feed_y
    )
    feed_last = y_swap(feed_half, 2)
    grad_low, sums = input_back(
        at,
        own_tokens,
        d_middle,
        after(vectors_all, feed_half),
        second_sums,
        fc_bias_sum,
        qkv_sums,
        d_first_parts,
    )
    grad_turned = turn(grad_low)
    input_grad = jnp.transpose(grad_turned.astype(WIDE))

    qkv_keep, give_one, give_two = held_call(
        qkv_x_kernel,
        "qkv_x",
        [like((count, PIECE, FF_PART)) for count in (7, 4, 3)],
        at,
        qkv_pieces[0],
        *qkv_got,
        out_total,
        sums,
    )
    qkv_y = [y_swap(give_one, 1), y_swap(give_two, 3)]
    feed_own, feed_one, feed_two, feed_three, feed_rest = blocks_call(
        split_sum_kernel, "feed_y", [1, 1, 1, 1, 4], after(feed_half, give_one), feed_last
    )
    feed_z = [z_swap(part, d) for d, part in ((1, feed_one), (2, feed_two), (3, feed_three))]
    final_near, final_far = final_part(at, after(hidden, feed_own), proj_pieces)
    (qkv_half,) = blocks_call(add_halves_kernel, "qkv_half", [7], after(qkv_keep, final_far), *qkv_y)
    qkv_last = y_swap(qkv_half, 2)
    (feed_rows,) = blocks_call(
        feed_z_kernel, "feed_z", [8], after(feed_own, qkv_half), *feed_z, feed_rest
    )
    feed_rows = lax.all_gather(feed_rows, "x", axis=0)
    final_parts, final_sent, final_came = team_parts(final_near, after(final_far, qkv_half))
    qkv_own, qkv_one, qkv_two, qkv_three, qkv_rest, sums_total = blocks_call(
        qkv_y_kernel, "qkv_y", [1, 2, 2, 2, 2, 1], after(qkv_half, final_sent, grad_turned), qkv_last
    )
    qkv_z = [z_swap(part, d) for d, part in ((1, qkv_one), (2, qkv_two), (3, qkv_three))]
    (qkv_rows,) = blocks_call(
        qkv_z_kernel, "qkv_z", [7], after(qkv_own, final_came), sums_total, *qkv_z, qkv_rest
    )
    qkv_rows = spread_x(qkv_rows, x_swap)
    (output_low,) = held_call(
        output_kernel,
        "output_rows",
        [like((WIDTH, ROWS))],
        at,
        middle,
        after(vectors_all, qkv_rows[0]),
        *final_parts,
        rows=ROWS,
    )
    output = jnp.transpose(turn(output_low))
    grad_fc, grad_proj = whole_call(
        place_feed_kernel,
        "place_feed",
        [like((SHARD, 8 * FF_PART), WIDE), like((FF_PART, WIDTH), WIDE)],
        at,
        feed_rows,
        c_swap(after(feed_rows, qkv_rows[1], qkv_rows[3])),
        limit=VMEM_LIMIT,
    )
    qkv_other = [c_swap(after(part, output, grad_fc)) for part in qkv_rows]
    vector_shapes = [like((SHARD,), WIDE)] * 6 + [like((FF_PART,), WIDE)]
    vector_shapes += [like((SHARD,), WIDE)] * 2
    grad_qkv, grad_out, *vector_grads = whole_call(
        place_qkv_kernel,
        "place_qkv",
        [like((SHARD, 3 * WIDTH), WIDE), like((SHARD, WIDTH), WIDE)] + vector_shapes,
        at,
        *qkv_rows,
        *qkv_other,
        scratch=[
            pltpu.VMEM((2, 4, 7) + SUMS, LOW),
            pltpu.VMEM(SUMS, WIDE),
            pltpu.VMEM((1, 8 * SPAN), WIDE),
        ],
        limit=VMEM_LIMIT,
    )

    g_gain_one, g_bias_one, g_gain_two, g_bias_two, g_out_b, g_proj_b = vector_grads[:6]
    g_fc_b, g_query_b, g_value_b = vector_grads[6:]

    return (
        output,
        input_grad,
        g_gain_one,
        g_bias_one,
        grad_qkv,
        g_query_b,
        g_value_b,
        grad_out,
        g_out_b,
        g_gain_two,
        g_bias_two,
        grad_fc,
        g_fc_b,
        grad_proj,
        g_proj_b,
    )


def solution(mesh):
    fine = Mesh(mesh.devices.reshape(2, 4, 2, 2, 4), ("yh", "x", "c", "yl", "z"))
    group, owner = ("yh", "x", "c"), ("yl", "z")
    everyone = group + owner
    vector, matrix = P(owner), P(owner, None)
    rows = P(everyone, None)
    return jax.shard_map(
        local,
        mesh=fine,
        in_specs=(
            rows,
            P(group, None),
            vector,
            vector,
            matrix,
            vector,
            vector,
            matrix,
            vector,
            vector,
            vector,
            matrix,
            vector,
            matrix,
            vector,
            rows,
        ),
        out_specs=(
            rows,
            rows,
            vector,
            vector,
            matrix,
            vector,
            vector,
            matrix,
            vector,
            vector,
            vector,
            matrix,
            vector,
            matrix,
            vector,
        ),
        check_vma=False,
    )
```
